32 devices in a mesh: region: 2 (over x), ty: 16 (over z, y, core).
Axes of the slice: x: 2, y: 2, z: 4, core: 2. Of those that a mesh axis runs over, the one named last changes fastest.
Arguments:
- mask_init: float32 [32, 512, 512], P(('region', 'ty')), parts along dimension 0, may hold values from -1.6 to 1.6
- dual_init: float32 [32, 512, 512], P(('region', 'ty')), parts along dimension 0, may hold values from -1.5 to 1.5
- target: bfloat16 [32, 512, 512], P(('region', 'ty')), parts along dimension 0, may hold values from 0 to 1, as said below
- kernels: float32 [8, 2, 1024], replicated, may hold values from -9 to 9
- weights: float32 [8], replicated, may hold values from 0.1 to 1
Outputs:
- mask_final: float32 [32, 512, 512], P(('region', 'ty')), parts along dimension 0
- dual_final: float32 [32, 512, 512], P(('region', 'ty')), parts along dimension 0
The draws below stay inside these ranges and needn't reach their ends.
There are 2 independent parts, one for each index of `region`. The reference program is written for one: setup_inputs(seed, part) draws one part's arguments, and reference() takes and returns one part's arrays. A program takes and returns all parts, laid end to end along the dimension named above; an argument that names none is the same for every part. Nothing has to cross between parts.
Inputs may be any that keep to these rules, and one draw needn't show every extreme that they name: `target`: each entry is 0 or 1; wherever two tiles cover the same canvas position they hold the same value.
All inputs are finite; a program needn't handle non-finite values.
Results may differ from the reference program's by a relative error of at most 0.0045.
Values sent between devices are 32-bit elements; how exact they have to be, the bound alone decides.
No kernel may reach another device: no remote copies, remote signals or barrier semaphores. Data moves between devices by JAX's collectives and lax.ppermute only.
A program may use at most 128 MiB of HBM per device.

```python
import math
import jax
import jax.numpy as jnp
from jax import lax

N = 512
INTERSECTION = 128
F = 32
KERNELS = 8
GRID_COLS = 4
ITERS = 2
TILES = 16


def smooth_field(coarse):
    spacing = 2 * N // F
    pixels = jnp.arange(N, dtype=jnp.int32)
    cell_index = pixels // spacing
    fraction = (pixels % spacing).astype(jnp.float32) / spacing
    top_rows = coarse[:, cell_index, :]
    low_rows = coarse[:, cell_index + 1, :]
    rowwise = top_rows * (1.0 - fraction)[None, :, None] + low_rows * fraction[None, :, None]
    west_cols = rowwise[:, :, cell_index]
    east_cols = rowwise[:, :, cell_index + 1]
    return west_cols * (1.0 - fraction)[None, None, :] + east_cols * fraction[None, None, :]


def draw_mask_init(key, part):
    spacing = 2 * N // F
    points = N // spacing + 1
    coarse_key, rough_key = jax.random.split(jax.random.fold_in(key, 11))
    coarse = jnp.clip(0.22 * jax.random.normal(coarse_key, (TILES, points, points), jnp.float32), -0.75, 0.75)
    rough = jax.random.uniform(rough_key, (TILES, N, N), jnp.float32, -0.8, 0.8)
    return smooth_field(coarse) + rough


def draw_kernels(key, part):
    kernel_key = jax.random.fold_in(key, 23)
    return jnp.clip(3.0 * jax.random.normal(kernel_key, (KERNELS, 2, F * F), jnp.float32), -9.0, 9.0)


def draw_target(key, part):
    stride = N - INTERSECTION
    grid_height = TILES // GRID_COLS * stride + INTERSECTION
    grid_width = GRID_COLS * stride + INTERSECTION
    block_side = N // 8
    blocks_high = (grid_height + block_side - 1) // block_side
    blocks_wide = (grid_width + block_side - 1) // block_side
    kind_key, phase_key, bits_key = jax.random.split(jax.random.fold_in(key, 37), 3)
    block_kinds = jax.random.randint(kind_key, (blocks_high, blocks_wide), 0, 4)
    block_phase = jax.random.randint(phase_key, (blocks_high, blocks_wide), 0, 2)
    random_bits = jax.random.randint(bits_key, (grid_height, grid_width), 0, 2)
    canvas_rows = jnp.arange(grid_height, dtype=jnp.int32)
    canvas_cols = jnp.arange(grid_width, dtype=jnp.int32)
    kind_pixels = block_kinds[canvas_rows // block_side][:, canvas_cols // block_side]
    phase_pixels = block_phase[canvas_rows // block_side][:, canvas_cols // block_side]
    vertical = (canvas_cols[None, :] + phase_pixels) % 2
    horizontal = (canvas_rows[:, None] + phase_pixels) % 2
    canvas = jnp.where(kind_pixels == 0, random_bits, jnp.where(kind_pixels == 3, horizontal, vertical))
    tile_ids = jnp.arange(TILES, dtype=jnp.int32)
    row_start = tile_ids // GRID_COLS * stride
    col_start = tile_ids % GRID_COLS * stride
    pixels = jnp.arange(N, dtype=jnp.int32)
    rows_index = row_start[:, None, None] + pixels[None, :, None]
    cols_index = col_start[:, None, None] + pixels[None, None, :]
    return canvas[rows_index, cols_index].astype(jnp.bfloat16)


def shard_levels(stream_key, extent, pieces, least, top_value):
    factor_of = 1.0
    for axis_at, shards_of in pieces:
        heights = jax.random.uniform(jax.random.fold_in(jax.random.fold_in(stream_key, 6), axis_at), (shards_of,), jnp.float32, least / len(pieces), top_value / len(pieces))
        factor_of = factor_of * jnp.repeat(jnp.exp(heights), extent[axis_at] // shards_of).reshape((-1,) + (1,) * (len(extent) - 1 - axis_at))
    return factor_of


def gaussian(rng, extent, deviation, limit, cuts=(), held_as=jnp.bfloat16):
    array = jax.random.normal(rng, extent, jnp.float32) * deviation
    if len(cuts) > 0:
        array = shard_levels(rng, extent, cuts, -0.22, 0.18) * array
    return jnp.clip(array, min=-limit, max=limit).astype(held_as)


def setup_inputs(seed: int = 0, part: int = 0) -> dict:
    splits = jax.random.split(jax.random.key(seed), 6)
    part_keys = jax.random.split(jax.random.fold_in(splits[5], part), 6)
    return {
        "mask_init": draw_mask_init(jax.random.fold_in(jax.random.fold_in(splits[5], part), 71), part),
        "dual_init": gaussian(part_keys[1], (TILES, N, N), 0.3, 1.5, ((0, 16),), jnp.float32),
        "target": draw_target(jax.random.fold_in(jax.random.fold_in(splits[5], part), 71), part),
        "kernels": draw_kernels(jax.random.fold_in(splits[5], 71), part),
        "weights": jnp.clip(jnp.exp(jax.random.uniform(splits[4], (KERNELS,), jnp.float32, math.log(0.1), math.log(1.0))), 0.1, 1.0),
    }


SHARPNESS = 8.0
THRESHOLD = 0.3
STEP_SIZE = 0.25
PENALTY = 1.0
PRECISE = lax.Precision.HIGHEST


def tables():
    pixels = jnp.arange(N, dtype=jnp.int32)
    frequencies = jnp.arange(F, dtype=jnp.int32) - F // 2
    phases = (frequencies[:, None] * pixels[None, :]) % N
    angles = phases.astype(jnp.float32) * (2.0 * math.pi / N)
    return jnp.cos(angles), -jnp.sin(angles)


def exact_dot(left_side, right_side, contract):
    return lax.dot_general(left_side, right_side, (contract, ((), ())), precision=PRECISE, preferred_element_type=jnp.float32)


def plain_dot(left_side, right_side, contract):
    return lax.dot_general(left_side, right_side, (contract, ((), ())), preferred_element_type=jnp.float32)


def kernel_field(kernel, spectrum_real, spectrum_imag, cos_table, sin_table, rows_low):
    kernel_real = kernel[0].reshape(F, F)
    kernel_imag = kernel[1].reshape(F, F)
    gated_real = kernel_real * spectrum_real - kernel_imag * spectrum_imag
    gated_imag = kernel_real * spectrum_imag + kernel_imag * spectrum_real
    band_real = exact_dot(gated_real, cos_table, ((1,), (0,))) + exact_dot(gated_imag, sin_table, ((1,), (0,)))
    band_imag = exact_dot(gated_imag, cos_table, ((1,), (0,))) - exact_dot(gated_real, sin_table, ((1,), (0,)))
    upper = jnp.concatenate([band_real, band_imag], axis=1)
    lower = jnp.concatenate([band_imag, -band_real], axis=1)
    stacked = jnp.concatenate([upper, lower], axis=0).astype(jnp.bfloat16)
    field = plain_dot(rows_low, stacked, ((0,), (0,))) / (N * N)
    return field[:, :N], field[:, N:]


def mask_gradient(mask, target, kernels, weights):
    cos_table, sin_table = tables()
    rows_exact = jnp.concatenate([cos_table, sin_table], axis=0)
    rows_low = rows_exact.astype(jnp.bfloat16)
    cos_low = cos_table.astype(jnp.bfloat16)
    sin_low = sin_table.astype(jnp.bfloat16)
    partial_band = plain_dot(rows_low, mask.astype(jnp.bfloat16), ((1,), (1,)))
    part_real = partial_band[:F]
    part_imag = partial_band[F:]
    spectrum_real = exact_dot(cos_table, part_real, ((1,), (1,))) - exact_dot(sin_table, part_imag, ((1,), (1,)))
    spectrum_imag = exact_dot(cos_table, part_imag, ((1,), (1,))) + exact_dot(sin_table, part_real, ((1,), (1,)))
    weight_total = jnp.sum(weights)

    def forward(summed, item):
        kernel, weight = item
        field_real, field_imag = kernel_field(kernel, spectrum_real, spectrum_imag, cos_table, sin_table, rows_low)
        return summed + weight * (field_real * field_real + field_imag * field_imag), None

    summed, unused = lax.scan(forward, jnp.zeros((N, N), jnp.float32), (kernels, weights))
    intensity = summed / weight_total
    resist = jax.nn.sigmoid(SHARPNESS * (intensity - THRESHOLD))
    slope = 2.0 * (resist - target.astype(jnp.float32)) * SHARPNESS * resist * (1.0 - resist)
    back_table = jnp.concatenate([jnp.concatenate([cos_low, -sin_low], axis=1), jnp.concatenate([sin_low, cos_low], axis=1)], axis=0)

    def backward(carry, item):
        adjoint_real, adjoint_imag = carry
        kernel, weight = item
        field_real, field_imag = kernel_field(kernel, spectrum_real, spectrum_imag, cos_table, sin_table, rows_low)
        weighted = jnp.concatenate([slope * field_real, slope * field_imag], axis=1).astype(jnp.bfloat16)
        turned = plain_dot(back_table, weighted, ((1,), (1,)))
        turned_real = turned[:F]
        turned_imag = turned[F:]
        back_real = exact_dot(cos_table, turned_real, ((1,), (1,))) - exact_dot(sin_table, turned_imag, ((1,), (1,)))
        back_imag = exact_dot(cos_table, turned_imag, ((1,), (1,))) + exact_dot(sin_table, turned_real, ((1,), (1,)))
        kernel_real = kernel[0].reshape(F, F)
        kernel_imag = kernel[1].reshape(F, F)
        portion = weight / weight_total
        new_real = adjoint_real + portion * (kernel_real * back_real + kernel_imag * back_imag)
        new_imag = adjoint_imag + portion * (kernel_real * back_imag - kernel_imag * back_real)
        return (new_real, new_imag), None

    zero_block = jnp.zeros((F, F), jnp.float32)
    adjoints, unused = lax.scan(backward, (zero_block, zero_block), (kernels, weights))
    adjoint_real, adjoint_imag = adjoints
    tail_real = exact_dot(adjoint_real, cos_table, ((1,), (0,))) + exact_dot(adjoint_imag, sin_table, ((1,), (0,)))
    tail_imag = exact_dot(adjoint_imag, cos_table, ((1,), (0,))) - exact_dot(adjoint_real, sin_table, ((1,), (0,)))
    tails = jnp.concatenate([tail_real, tail_imag], axis=0)
    return exact_dot(rows_exact, tails, ((0,), (0,))) * (2.0 / (N * N))


def consensus(shared):
    stride = N - INTERSECTION
    grid_height = (TILES // GRID_COLS) * stride + INTERSECTION
    grid_width = GRID_COLS * stride + INTERSECTION
    canvas = jnp.zeros((grid_height, grid_width), jnp.float32)
    coverage = jnp.zeros((grid_height, grid_width), jnp.float32)
    ones_block = jnp.ones((N, N), jnp.float32)

    def corner_of(tile_index):
        tile_index = tile_index.astype(jnp.int32)
        top_pixel = ((tile_index // GRID_COLS) * stride).astype(jnp.int32)
        left_pixel = ((tile_index % GRID_COLS) * stride).astype(jnp.int32)
        return tile_index, top_pixel, left_pixel

    def place(tile_index, carry):
        canvas, coverage = carry
        tile_index, top_pixel, left_pixel = corner_of(tile_index)
        piece = lax.dynamic_index_in_dim(shared, tile_index, 0, keepdims=False)
        block = lax.dynamic_slice(canvas, (top_pixel, left_pixel), (N, N)) + piece
        canvas = lax.dynamic_update_slice(canvas, block, (top_pixel, left_pixel))
        counted = lax.dynamic_slice(coverage, (top_pixel, left_pixel), (N, N)) + ones_block
        coverage = lax.dynamic_update_slice(coverage, counted, (top_pixel, left_pixel))
        return canvas, coverage

    canvas, coverage = lax.fori_loop(0, TILES, place, (canvas, coverage))

    def take(tile_index):
        tile_index, top_pixel, left_pixel = corner_of(tile_index)
        summed = lax.dynamic_slice(canvas, (top_pixel, left_pixel), (N, N))
        counted = lax.dynamic_slice(coverage, (top_pixel, left_pixel), (N, N))
        return summed / counted

    return lax.map(take, jnp.arange(TILES, dtype=jnp.int32))


def reference(mask_init, dual_init, target, kernels, weights):
    mask = mask_init
    dual = dual_init
    for iteration in range(ITERS):
        agreed = consensus(mask + dual)
        dual = dual + mask - agreed
        gradient = lax.map(lambda item: mask_gradient(item[0], item[1], kernels, weights), (mask, target))
        mask = mask - STEP_SIZE * (gradient + PENALTY * (mask - agreed + dual))
    return mask, dual
```

```python
import functools
import math

import jax
import jax.numpy as jnp
import ml_dtypes
import numpy as np
from jax import lax
from jax.experimental import pallas as pl
from jax.experimental.pallas import tpu as pltpu
from jax.sharding import PartitionSpec as P

INTERSECTION = 128
GRID_COLS = 4
SHARPNESS = 8.0
THRESHOLD = 0.3
F32 = jnp.float32
BF16 = jnp.bfloat16
VMEM_LIMIT = 48 * 1024 * 1024


def halves(table):
    high = table.astype(ml_dtypes.bfloat16)
    low = (table - high.astype(np.float64)).astype(ml_dtypes.bfloat16)
    return high, low


def build_tables(size, band):
    coarse = 2 * band
    stride = size // coarse
    edge = size - INTERSECTION
    frequencies = np.arange(band) - band // 2
    angles = 2.0 * np.pi * ((frequencies[:, None] * np.arange(size)[None, :]) % size) / size
    cos, sin = np.cos(angles), -np.sin(angles)
    rows = np.concatenate([cos, sin], axis=0)
    quad = np.concatenate([cos.T, sin.T, -sin.T, cos.T], axis=1)
    dc, ds = cos[:, ::stride], sin[:, ::stride]
    wide = np.arange(-(band - 1), band)
    gaps = np.arange(size)[:, None] - stride * np.arange(coarse)[None, :]
    lift = np.cos(2.0 * np.pi * wide[:, None, None] * gaps[None] / size).sum(0) / coarse

    tables = {}
    quad_high, quad_low = halves(quad)
    tables["quad"] = np.concatenate([quad_high, quad_low], axis=1)
    rows_high, rows_low = halves(rows)
    tables["rows"] = np.concatenate([rows_high, rows_low], axis=0)
    spread = np.concatenate(
        [np.concatenate([dc, -ds, -ds, -dc], axis=1), np.concatenate([ds, dc, dc, -ds], axis=1)], axis=0
    )
    high, low = halves(np.concatenate([spread, spread], axis=0))
    tables["spread"] = np.concatenate([high, high, low], axis=0)
    high, low = halves(np.concatenate([dc.T, ds.T], axis=1))
    tables["field"] = np.concatenate([high, high, low], axis=1)
    high, low = halves(np.concatenate([lift.T, lift.T], axis=0))
    tables["lift_cols"] = np.concatenate([high, high, low], axis=0)
    high, low = halves(lift)
    tables["lift_rows"] = np.concatenate([high, high, low], axis=1)
    tables["drop_cols"] = np.concatenate([high, high, low, low], axis=1)
    tables["drop_rows"] = np.concatenate([high.T, low.T], axis=0)
    high, low = halves(np.concatenate([dc, ds], axis=0))
    tables["turn"] = np.concatenate([high, high, low], axis=1)
    back_real = np.concatenate([dc.T, -ds.T, -ds.T, -dc.T], axis=0)
    back_imag = np.concatenate([ds.T, dc.T, dc.T, -ds.T], axis=0)
    high, low = halves(np.concatenate([back_real, back_imag, back_imag, -back_real], axis=1))
    tables["back"] = np.concatenate([high, low], axis=1)
    flip = np.zeros((band, band))
    for place in range(1, band):
        flip[place, band - place] = 1.0
    eye, zero = np.eye(band), np.zeros((band, band))
    own = np.concatenate(
        [
            np.concatenate([eye, zero, zero, eye], axis=1),
            np.concatenate([zero, eye, -eye, zero], axis=1),
        ],
        axis=0,
    )
    turned = np.concatenate(
        [
            np.concatenate([flip, zero, zero, flip], axis=1),
            np.concatenate([zero, -flip, flip, zero], axis=1),
        ],
        axis=0,
    )
    tables["mirror_lanes"] = np.concatenate(
        [np.concatenate([own, own], axis=0), np.concatenate([turned, turned], axis=0)], axis=1
    ).astype(ml_dtypes.bfloat16)
    tables["mirror_rows"] = flip.astype(ml_dtypes.bfloat16)
    tail = np.concatenate([np.concatenate([cos, -sin], axis=1), np.concatenate([sin, cos], axis=1)], axis=0)
    high, low = halves(tail)
    tables["tail"] = np.concatenate([high, high, low, np.zeros_like(low)], axis=0)
    high, low = halves(rows.T)
    tables["final"] = np.concatenate([high, high, low], axis=1)
    near, far = rows[:, :INTERSECTION], rows[:, edge:]
    high, low = halves(np.concatenate([far.T, near.T], axis=0))
    tables["final_edge"] = np.concatenate([high, high, low], axis=1)
    return tables


def dot(left, right):
    return lax.dot_general(left, right, (((1,), (0,)), ((), ())), preferred_element_type=F32)


def split(value):
    high = value.astype(BF16)
    return high, (value - high.astype(F32)).astype(BF16)


def place(total):
    index = lax.axis_index("ty")
    row, col = index // GRID_COLS, index % GRID_COLS
    return row, col, total // GRID_COLS


def share_of(present):
    return jnp.where(present, 0.5, 1.0).astype(F32)


def column_scale(size, col):
    lanes = lax.broadcasted_iota(jnp.int32, (1, size), 1)
    left = jnp.where(lanes < INTERSECTION, share_of(col > 0), 1.0)
    return left * jnp.where(lanes >= size - INTERSECTION, share_of(col < GRID_COLS - 1), 1.0)


def row_scale(size, row, rows):
    steps = lax.broadcasted_iota(jnp.int32, (size, 1), 0)
    upper = jnp.where(steps < INTERSECTION, share_of(row > 0), 1.0)
    return upper * jnp.where(steps >= size - INTERSECTION, share_of(row < rows - 1), 1.0)


def quad_form(value):
    half = value.shape[0] // 2
    width = value.shape[1]
    lanes = lax.broadcasted_iota(jnp.int32, (half, width), 1)
    rolled = pltpu.roll(value[half:], width // 2, 1)
    return value[:half] + jnp.where(lanes < width // 2, rolled, -rolled)


def column_transform(value, table):
    width = table.shape[1] // 2
    high, low = split(value)
    both = dot(high, table)
    return both[:, :width] + both[:, width:] + dot(low, table[:, :width])


def row_transform(table, value):
    half = table.shape[0] // 2
    high, low = split(value)
    both = dot(table, high)
    return both[:half] + both[half:] + dot(table[:half], low)


def open_kernel(total, mask_ref, dual_ref, quad_ref, rows_ref, spectrum_ref, base_ref, own_ref, send1_ref, send2_ref, side1_ref, side2_ref, top_ref, bottom_ref):
    size = mask_ref.shape[0]
    width = quad_ref.shape[1] // 2
    edge = size - INTERSECTION
    row, col, rows = place(total)
    mask, dual = mask_ref[...], dual_ref[...]
    first = mask + dual
    second = mask + 0.25 * dual
    even = col % 2 == 0
    near = jnp.concatenate([first[:, :INTERSECTION], second[:, :INTERSECTION]], axis=1)
    far = jnp.concatenate([first[:, edge:], second[:, edge:]], axis=1)
    side1_ref[...] = jnp.where(even, far, near)
    side2_ref[...] = jnp.where(even, near, far)
    top_ref[...] = jnp.concatenate([first[:INTERSECTION], second[:INTERSECTION]], axis=0)
    bottom_ref[...] = jnp.concatenate([first[edge:], second[edge:]], axis=0)
    scaled = first * row_scale(size, row, rows) * column_scale(size, col)
    table = quad_ref[...]
    parts = [
        column_transform(mask, table),
        column_transform(0.5 * mask - 0.25 * dual, table),
        column_transform(scaled, table),
        column_transform(scaled[:, :INTERSECTION], table[edge:]),
        column_transform(scaled[:, edge:], table[:INTERSECTION]),
    ]
    lines = rows_ref[...]
    whole = row_transform(lines, jnp.concatenate(parts, axis=1))
    outer = jnp.concatenate(parts[2:], axis=1)
    upper = row_transform(lines[:, edge:], outer[:INTERSECTION])
    lower = row_transform(lines[:, :INTERSECTION], outer[edge:])

    def block(value, at):
        return quad_form(value[:, at * width : (at + 1) * width])

    spectrum_ref[...] = block(whole, 0)
    base_ref[...] = block(whole, 1)
    stacks = [
        jnp.concatenate([block(whole, 2 + at), block(upper, at), block(lower, at)], axis=0) for at in range(3)
    ]
    own_ref[...] = stacks[0]
    send1_ref[...] = jnp.where(even, stacks[2], stacks[1])
    send2_ref[...] = jnp.where(even, stacks[1], stacks[2])


def middle_kernel(total, own_ref, got1_ref, got2_ref, top_ref, bottom_ref, side1_ref, side2_ref, keep_ref, send1_ref, send2_ref, line1_ref, line2_ref):
    band = own_ref.shape[0] // 3
    size = top_ref.shape[1]
    edge = size - INTERSECTION
    row, col, rows = place(total)
    even_row, even_col = row % 2 == 0, col % 2 == 0
    summed = own_ref[...] + got1_ref[...] + got2_ref[...]
    keep_ref[...] = summed[:band]
    upper, lower = summed[band : 2 * band], summed[2 * band :]
    send1_ref[...] = jnp.where(even_row, lower, upper)
    send2_ref[...] = jnp.where(even_row, upper, lower)

    def widened(strip_ref, begin):
        ends1 = side1_ref[begin : begin + INTERSECTION, :]
        ends2 = side2_ref[begin : begin + INTERSECTION, :]
        left = jnp.where(even_col, ends2, ends1)
        right = jnp.where(even_col, ends1, ends2)
        left = jnp.concatenate([left[:, :INTERSECTION], left[:, INTERSECTION:]], axis=0)
        right = jnp.concatenate([right[:, :INTERSECTION], right[:, INTERSECTION:]], axis=0)
        strip = strip_ref[...]
        return jnp.concatenate(
            [strip[:, :INTERSECTION] + left, strip[:, INTERSECTION:edge], strip[:, edge:] + right], axis=1
        )

    top = widened(top_ref, 0)
    bottom = widened(bottom_ref, edge)
    line1_ref[...] = jnp.where(even_row, bottom, top)
    line2_ref[...] = jnp.where(even_row, top, bottom)


def adjoint_of(spectrum, gates_ref, target_ref, tables):
    band = spectrum.shape[0]
    width = 4 * band
    kernels = gates_ref.shape[0] // band
    size = target_ref.shape[0]
    gates = gates_ref[...]
    scaled = spectrum * (1.0 / (size * size))
    gated = gates * jnp.concatenate([scaled] * kernels, axis=0)
    high, low = split(gated)
    bands = dot(jnp.concatenate([high, low, high], axis=1), tables["spread"][...])
    stacked = jnp.concatenate(
        [
            jnp.concatenate([bands[band * k : band * (k + 1), :width] for k in range(kernels)], axis=1),
            jnp.concatenate([bands[band * k : band * (k + 1), width:] for k in range(kernels)], axis=1),
        ],
        axis=0,
    )
    high, low = split(stacked)
    fields = dot(tables["field"][...], jnp.concatenate([high, low, high], axis=0))
    squares = fields * fields
    power = squares[:, :width]
    for k in range(1, kernels):
        power = power + squares[:, k * width : (k + 1) * width]
    high, low = split(power)
    lifted = dot(jnp.concatenate([high, low, high], axis=1), tables["lift_cols"][...])
    high, low = split(lifted)
    intensity = dot(tables["lift_rows"][...], jnp.concatenate([high, low, high], axis=0))
    resist = 1.0 / (1.0 + jnp.exp(-SHARPNESS * (intensity - THRESHOLD)))
    slope = (2.0 * SHARPNESS) * (resist - target_ref[...].astype(F32)) * (resist * (1.0 - resist))
    both = dot(slope.astype(BF16), tables["drop_cols"][...])
    narrowed = both[:, :width] + both[:, width:]
    dropped = row_transform(tables["drop_rows"][...], narrowed)
    weighted = fields * jnp.concatenate([dropped] * kernels, axis=1)
    high, low = split(weighted)
    turned = dot(tables["turn"][...], jnp.concatenate([high, low, high], axis=0))
    across = jnp.concatenate(
        [
            jnp.concatenate([turned[:band, k * width : (k + 1) * width] for k in range(kernels)], axis=0),
            jnp.concatenate([turned[band:, k * width : (k + 1) * width] for k in range(kernels)], axis=0),
        ],
        axis=1,
    )
    back = column_transform(across, tables["back"][...])
    product = gates * back
    adjoint = product[:band]
    for k in range(1, kernels):
        adjoint = adjoint + product[k * band : (k + 1) * band]
    return adjoint + pltpu.roll(adjoint, width // 2, 1)


CORE_TABLES = ("spread", "field", "lift_cols", "lift_rows", "drop_cols", "drop_rows", "turn", "back")


def first_kernel(spectrum_ref, gates_ref, target_ref, *rest):
    tables = dict(zip(CORE_TABLES, rest))
    out_ref = rest[len(CORE_TABLES)]
    out_ref[...] = adjoint_of(spectrum_ref[...], gates_ref, target_ref, tables)


def second_kernel(base_ref, keep_ref, got1_ref, got2_ref, adjoint_ref, lanes_ref, flip_ref, gates_ref, target_ref, *rest):
    tables = dict(zip(CORE_TABLES, rest))
    out_ref = rest[len(CORE_TABLES)]
    adjoint = adjoint_ref[...]
    width = adjoint.shape[1]
    half = width // 2
    agreed = keep_ref[...] + got1_ref[...] + got2_ref[...]
    high, low = split(adjoint)
    lanes = lax.broadcasted_iota(jnp.int32, adjoint.shape, 1)
    pair = jnp.where(lanes < half, high, low)
    mirrored = dot(pair, lanes_ref[...])
    high, low = split(mirrored[:, width:])
    flip = flip_ref[...]
    gradient_band = mirrored[:, :width] + dot(flip, high) + dot(flip, low)
    spectrum = base_ref[...] + 0.5 * agreed - 0.25 * gradient_band
    out_ref[...] = adjoint_of(spectrum, gates_ref, target_ref, tables)


def last_kernel(total, mask_ref, dual_ref, side1_ref, side2_ref, line1_ref, line2_ref, own_ref, next1_ref, next2_ref, adjoint_ref, tail_ref, final_ref, edge_ref, mask_out_ref, dual_out_ref):
    size = mask_ref.shape[0]
    band = adjoint_ref.shape[0]
    width = adjoint_ref.shape[1]
    half = width // 2
    edge = size - INTERSECTION
    row, col, rows = place(total)
    even_row, even_col = row % 2 == 0, col % 2 == 0
    scale = 2.0 / (size * size)
    lanes = lax.broadcasted_iota(jnp.int32, (1, width), 1)
    tail_table = tail_ref[...]

    def spread(blocks, table):
        high, low = split(blocks * scale)
        pair = jnp.where(lanes < half, high, low)
        return dot(jnp.concatenate([pair, high], axis=1), table)

    def piece(begin, end):
        return jnp.concatenate([tail_table[:, begin:end], tail_table[:, size + begin : size + end]], axis=1)

    def stack(value, at):
        wide = value.shape[1] // 2
        lines = value[at * band : (at + 1) * band]
        return jnp.concatenate([lines[:, :wide], lines[:, wide:]], axis=0)

    above = jnp.where(even_row, next2_ref[...], next1_ref[...])
    below = jnp.where(even_row, next1_ref[...], next2_ref[...])
    mine = own_ref[...]

    def column(at):
        return jnp.concatenate([v[at * band : (at + 1) * band] for v in (mine, above, below)], axis=0)

    first1, first2 = column(1), column(2)
    left = jnp.where(even_col, first2, first1)
    right = jnp.where(even_col, first1, first2)
    centre = jnp.concatenate([column(0), adjoint_ref[...]], axis=0)
    tails = spread(centre, tail_table)
    left_tails = spread(left, piece(edge, size))
    right_tails = spread(right, piece(0, INTERSECTION))
    columns = column_scale(size, col)

    def summed_tail(at):
        middle = stack(tails, at)
        lhs = stack(left_tails, at)
        rhs = stack(right_tails, at)
        return columns * jnp.concatenate(
            [middle[:, :INTERSECTION] + lhs, middle[:, INTERSECTION:edge], middle[:, edge:] + rhs], axis=1
        )

    def deep(value):
        high, low = split(value)
        return jnp.concatenate([high, low, high], axis=0)

    all_tails = [summed_tail(at) for at in range(3)]
    own_tail, new_tail = stack(tails, 0), stack(tails, 3)
    wide_rhs = deep(jnp.concatenate([all_tails[0], own_tail, new_tail], axis=1))
    upper_rhs, lower_rhs = deep(all_tails[1]), deep(all_tails[2])
    up_share, low_share = share_of(row > 0), share_of(row < rows - 1)

    for begin in range(0, size, INTERSECTION):
        end = begin + INTERSECTION
        mask, dual = mask_ref[begin:end, :], dual_ref[begin:end, :]
        products = dot(final_ref[begin:end, :], wide_rhs)
        around = products[:, :size]
        gradient0 = products[:, size : 2 * size]
        gradient1 = products[:, 2 * size :]
        ends1, ends2 = side1_ref[begin:end, :], side2_ref[begin:end, :]
        left_ends = jnp.where(even_col, ends2, ends1)
        right_ends = jnp.where(even_col, ends1, ends2)

        def joined(value, at):
            cut = slice(at * INTERSECTION, (at + 1) * INTERSECTION)
            return jnp.concatenate(
                [value[:, :INTERSECTION] + left_ends[:, cut], value[:, INTERSECTION:edge], value[:, edge:] + right_ends[:, cut]],
                axis=1,
            )

        first = joined(mask + dual, 0)
        second = joined(mask + 0.25 * dual, 1)
        if begin == 0:
            line = jnp.where(even_row, line2_ref[...], line1_ref[...])
            around = up_share * (around + dot(edge_ref[:INTERSECTION, :], upper_rhs))
            first = up_share * (first + line[:INTERSECTION])
            second = up_share * (second + line[INTERSECTION:])
        if end == size:
            line = jnp.where(even_row, line1_ref[...], line2_ref[...])
            around = low_share * (around + dot(edge_ref[INTERSECTION:, :], lower_rhs))
            first = low_share * (first + line[:INTERSECTION])
            second = low_share * (second + line[INTERSECTION:])
        agreed0 = first * columns
        agreed1 = second * columns - 0.25 * around
        dual_out_ref[begin:end, :] = 1.5 * mask + 0.75 * dual - 0.5 * agreed0 - 0.25 * gradient0 - agreed1
        mask_out_ref[begin:end, :] = (
            0.5 * (agreed0 + agreed1) - 0.375 * dual - 0.125 * gradient0 - 0.25 * gradient1
        )


def call(kernel, outs, operands, flops, name):
    return pl.pallas_call(
        kernel,
        out_shape=[jax.ShapeDtypeStruct(shape, dtype) for shape, dtype in outs],
        in_specs=[pl.BlockSpec(memory_space=pltpu.VMEM)] * len(operands),
        out_specs=[pl.BlockSpec(memory_space=pltpu.VMEM)] * len(outs),
        compiler_params=pltpu.CompilerParams(vmem_limit_bytes=VMEM_LIMIT),
        cost_estimate=pl.CostEstimate(flops=flops, bytes_accessed=1 << 20, transcendentals=0),
        name=name,
    )(*operands)


def swaps(total):
    cols = GRID_COLS
    sets = [[], [], [], []]
    for index in range(total):
        row, col = index // cols, index % cols
        if col + 1 < cols:
            sets[col % 2] += [(index, index + 1), (index + 1, index)]
        if index + cols < total:
            sets[2 + row % 2] += [(index, index + cols), (index + cols, index)]
    return sets


def per_device(mask_init, dual_init, target, kernels, weights):
    mask, dual, goal = mask_init[0], dual_init[0], target[0]
    size = mask.shape[0]
    count = kernels.shape[0]
    band = math.isqrt(kernels.shape[2])
    width = 4 * band
    total = lax.axis_size("ty")
    row_pairs1, row_pairs2, col_pairs1, col_pairs2 = swaps(total)
    tables = {name: jnp.asarray(table) for name, table in build_tables(size, band).items()}
    core = [tables[name] for name in CORE_TABLES]

    def trade(value, pairs):
        return lax.ppermute(value, "ty", pairs)

    gain = jnp.sqrt(weights / jnp.sum(weights))
    parts = (kernels * gain[:, None, None]).reshape(count, 2, band, band)
    gates = jnp.concatenate([parts[:, 0], parts[:, 0], parts[:, 1], parts[:, 1]], axis=2)
    gates = gates.reshape(count * band, width)

    block, stack = ((band, width), F32), ((3 * band, width), F32)
    side, line = ((size, 2 * INTERSECTION), F32), ((2 * INTERSECTION, size), F32)
    spectrum, base, own, send1, send2, side1, side2, top, bottom = call(
        functools.partial(open_kernel, total),
        [block, block, stack, stack, stack, side, side, line, line],
        [mask, dual, tables["quad"], tables["rows"]],
        10**9,
        "open",
    )
    got1, got2 = trade(send1, row_pairs1), trade(send2, row_pairs2)
    sides1, sides2 = trade(side1, row_pairs1), trade(side2, row_pairs2)
    (adjoint0,) = call(first_kernel, [block], [spectrum, gates, goal] + core, 3 * 10**9, "first")
    near1, near2 = trade(adjoint0, row_pairs1), trade(adjoint0, row_pairs2)
    keep, send1, send2, line1, line2 = call(
        functools.partial(middle_kernel, total),
        [block, block, block, line, line],
        [own, got1, got2, top, bottom, sides1, sides2],
        10**7,
        "middle",
    )
    more1, more2 = trade(send1, col_pairs1), trade(send2, col_pairs2)
    lines1, lines2 = trade(line1, col_pairs1), trade(line2, col_pairs2)
    row_of = jnp.concatenate([adjoint0, near1, near2], axis=0)
    next1, next2 = trade(row_of, col_pairs1), trade(row_of, col_pairs2)
    (adjoint1,) = call(
        second_kernel,
        [block],
        [base, keep, more1, more2, adjoint0, tables["mirror_lanes"], tables["mirror_rows"], gates, goal] + core,
        3 * 10**9,
        "second",
    )
    whole = ((size, size), F32)
    mask, dual = call(
        functools.partial(last_kernel, total),
        [whole, whole],
        [mask, dual, sides1, sides2, lines1, lines2, row_of, next1, next2, adjoint1]
        + [tables["tail"], tables["final"], tables["final_edge"]],
        2 * 10**9,
        "last",
    )
    return (mask[None], dual[None])


def solution(mesh):
    tiles = P(("region", "ty"), None, None)
    return jax.shard_map(
        per_device,
        mesh=mesh,
        in_specs=(tiles, tiles, tiles, P(), P()),
        out_specs=(tiles, tiles),
        check_vma=False,
    )
```

```python
import functools
import math

import jax
import jax.numpy as jnp
import ml_dtypes
import numpy as np
from jax import lax
from jax.experimental import pallas as pl
from jax.experimental.pallas import tpu as pltpu
from jax.sharding import PartitionSpec as P

INTERSECTION = 128
GRID_COLS = 4
SHARPNESS = 8.0
THRESHOLD = 0.3
F32 = jnp.float32
BF16 = jnp.bfloat16
VMEM_LIMIT = 48 * 1024 * 1024


def halves(table):
    high = table.astype(ml_dtypes.bfloat16)
    low = (table - high.astype(np.float64)).astype(ml_dtypes.bfloat16)
    return high, low


def build_tables(size, band):
    coarse = 2 * band
    stride = size // coarse
    edge = size - INTERSECTION
    frequencies = np.arange(band) - band // 2
    angles = 2.0 * np.pi * ((frequencies[:, None] * np.arange(size)[None, :]) % size) / size
    cos, sin = np.cos(angles), -np.sin(angles)
    order = np.arange(band).reshape(-1, 128 // band).T.reshape(-1)
    rows = np.concatenate([cos[order], sin[order]], axis=0)
    quad = np.concatenate([cos.T, sin.T, -sin.T, cos.T], axis=1)
    dc, ds = cos[:, ::stride], sin[:, ::stride]
    dc_rows, ds_rows = dc[order], ds[order]
    wide = np.arange(-(band - 1), band)
    gaps = np.arange(size)[:, None] - stride * np.arange(coarse)[None, :]
    lift = np.cos(2.0 * np.pi * wide[:, None, None] * gaps[None] / size).sum(0) / coarse

    tables = {}
    tables["quad"] = halves(quad)[0]
    high, low = halves(rows)
    tables["rows"] = np.concatenate([high, low], axis=0)
    spread = np.concatenate(
        [np.concatenate([dc, -ds, -ds, -dc], axis=1), np.concatenate([ds, dc, dc, -ds], axis=1)], axis=0
    )
    high, low = halves(np.concatenate([spread, spread], axis=0))
    tables["spread"] = np.concatenate([high, high, low], axis=0)
    high, low = halves(np.concatenate([dc_rows.T, ds_rows.T], axis=1))
    tables["field"] = np.concatenate([high, high, low], axis=1)
    high, low = halves(np.concatenate([lift.T, lift.T], axis=0))
    tables["lift_cols"] = np.concatenate([high, low], axis=0)
    high, low = halves(lift * (0.5 * SHARPNESS))
    tables["lift_rows"] = np.concatenate([high, high, low], axis=1)
    high, low = halves(lift)
    tables["drop_cols"] = np.concatenate([high, high, low, low], axis=1)
    high, low = halves(lift.T * (0.25 * SHARPNESS))
    tables["drop_rows"] = np.concatenate([high, low], axis=0)
    high, low = halves(np.concatenate([dc_rows, ds_rows], axis=0))
    tables["turn"] = np.concatenate([high, high, low], axis=1)
    back_real = np.concatenate([dc.T, -ds.T, -ds.T, -dc.T], axis=0)
    back_imag = np.concatenate([ds.T, dc.T, dc.T, -ds.T], axis=0)
    high, low = halves(np.concatenate([back_real, back_imag, back_imag, -back_real], axis=1))
    tables["back"] = np.concatenate([high, low], axis=1)
    flip = np.zeros((band, band))
    for place in range(1, band):
        flip[place, band - place] = 1.0
    eye, zero = np.eye(band), np.zeros((band, band))
    own = np.concatenate(
        [
            np.concatenate([eye, zero, zero, eye], axis=1),
            np.concatenate([zero, eye, -eye, zero], axis=1),
        ],
        axis=0,
    )
    turned = np.concatenate(
        [
            np.concatenate([flip, zero, zero, flip], axis=1),
            np.concatenate([zero, -flip, flip, zero], axis=1),
        ],
        axis=0,
    )
    tables["mirror_lanes"] = np.concatenate(
        [np.concatenate([own, own], axis=0), np.concatenate([turned, turned], axis=0)], axis=1
    ).astype(ml_dtypes.bfloat16)
    tables["mirror_rows"] = flip[order][:, order].astype(ml_dtypes.bfloat16)
    tail = np.concatenate([np.concatenate([cos, -sin], axis=1), np.concatenate([sin, cos], axis=1)], axis=0)
    high, low = halves(tail)
    tables["tail"] = np.concatenate([high, high, low, np.zeros_like(low)], axis=0)
    high, low = halves(rows.T)
    tables["final"] = np.concatenate([high, high, low], axis=1)
    near, far = rows[:, :INTERSECTION], rows[:, edge:]
    high, low = halves(np.concatenate([far.T, near.T], axis=0))
    tables["final_edge"] = np.concatenate([high, high, low], axis=1)
    return tables


def dot(left, right):
    return lax.dot_general(left, right, (((1,), (0,)), ((), ())), preferred_element_type=F32)


def split(value):
    high = value.astype(BF16)
    return high, (value - high.astype(F32)).astype(BF16)


def place(total):
    index = lax.axis_index("ty")
    row, col = index // GRID_COLS, index % GRID_COLS
    return row, col, total // GRID_COLS


def share_of(present):
    return jnp.where(present, 0.5, 1.0).astype(F32)


def edge_scale(shape, dim, size, before, after):
    steps = lax.broadcasted_iota(jnp.int32, shape, dim)
    first = jnp.where(steps < INTERSECTION, share_of(before), 1.0)
    return first * jnp.where(steps >= size - INTERSECTION, share_of(after), 1.0)


def quad_form(value):
    half = value.shape[0] // 2
    width = value.shape[1]
    lanes = lax.broadcasted_iota(jnp.int32, (half, width), 1)
    rolled = pltpu.roll(value[half:], width // 2, 1)
    return value[:half] + jnp.where(lanes < width // 2, rolled, -rolled)


def row_transform(table, value):
    half = table.shape[0] // 2
    both = dot(table, value.astype(BF16))
    return both[:half] + both[half:]


def gates_of(kernels_ref, weights_ref, band):
    count, parts, length = kernels_ref.shape
    lanes = 128
    groups = lanes // band
    chunks = length // lanes
    total = weights_ref[0]
    for k in range(1, count):
        total = total + weights_ref[k]
    group = lax.broadcasted_iota(jnp.int32, (chunks, lanes), 1) // band
    blocks = []
    for k in range(count):
        gain = jnp.sqrt(jnp.full((chunks, lanes), weights_ref[k], F32) / total)
        real, imag = [
            gain
            * jnp.concatenate(
                [kernels_ref[k, part : part + 1, c * lanes : (c + 1) * lanes] for c in range(chunks)], axis=0
            )
            for part in range(2)
        ]
        reals = [pltpu.roll(real, band * g, 1) if g else real for g in range(groups)]
        imags = [pltpu.roll(imag, band * g, 1) if g else imag for g in range(groups)]
        for at in range(groups):
            line = imags[(3 - at) % groups]
            line = jnp.where(group == 2, imags[(2 - at) % groups], line)
            line = jnp.where(group == 1, reals[(1 - at) % groups], line)
            blocks.append(jnp.where(group == 0, reals[-at % groups], line))
    return jnp.concatenate(blocks, axis=0)


def adjoint_of(spectrum, gates, target_ref, tables):
    band = spectrum.shape[0]
    width = 4 * band
    kernels = gates.shape[0] // band
    size = target_ref.shape[0]
    scaled = spectrum * (1.0 / (size * size))
    high, low = split(gates * jnp.concatenate([scaled] * kernels, axis=0))
    bands = dot(jnp.concatenate([high, low, high], axis=1), tables["spread"][...])
    stacked = jnp.concatenate(
        [
            jnp.concatenate([bands[band * k : band * (k + 1), :width] for k in range(kernels)], axis=1),
            jnp.concatenate([bands[band * k : band * (k + 1), width:] for k in range(kernels)], axis=1),
        ],
        axis=0,
    )
    high, low = split(stacked)
    fields = dot(tables["field"][...], jnp.concatenate([high, low, high], axis=0))
    squares = fields * fields
    power = squares[:, :width]
    for k in range(1, kernels):
        power = power + squares[:, k * width : (k + 1) * width]
    high, low = split(power)
    lifted = dot(high, tables["lift_cols"][:width, :]) + dot(
        jnp.concatenate([low, high], axis=1), tables["lift_cols"][...]
    )
    high, low = split(lifted)
    half = dot(tables["lift_rows"][...], jnp.concatenate([high, low, high], axis=0))
    curve = jnp.tanh(half - 0.5 * SHARPNESS * THRESHOLD)
    slope = (1.0 + curve - 2.0 * target_ref[...].astype(F32)) * (1.0 - curve * curve)
    both = dot(slope.astype(BF16), tables["drop_cols"][...])
    dropped = row_transform(tables["drop_rows"][...], both[:, :width] + both[:, width:])
    weighted = fields * jnp.concatenate([dropped] * kernels, axis=1)
    high, low = split(weighted)
    turned = dot(tables["turn"][...], jnp.concatenate([high, low, high], axis=0))
    across = jnp.concatenate(
        [
            jnp.concatenate([turned[:band, k * width : (k + 1) * width] for k in range(kernels)], axis=0),
            jnp.concatenate([turned[band:, k * width : (k + 1) * width] for k in range(kernels)], axis=0),
        ],
        axis=1,
    )
    both = dot(across.astype(BF16), tables["back"][...])
    product = gates * (both[:, :width] + both[:, width:])
    adjoint = product[:band]
    for k in range(1, kernels):
        adjoint = adjoint + product[k * band : (k + 1) * band]
    return adjoint + pltpu.roll(adjoint, width // 2, 1)


CORE_TABLES = ("spread", "field", "lift_cols", "lift_rows", "drop_cols", "drop_rows", "turn", "back")
OPEN_TABLES = ("quad", "rows") + CORE_TABLES


def open_kernel(total, weights_ref, mask_hbm, dual_hbm, kernels_hbm, target_hbm, *rest):
    count = len(OPEN_TABLES)
    hbm = [mask_hbm, dual_hbm, *rest[:2], kernels_hbm, *rest[2:count], target_hbm]
    outs = rest[count : count + 11]
    base_ref, gates_ref, own_ref, corner1_ref, corner2_ref, middle1_ref, middle2_ref = outs[:7]
    line1_ref, line2_ref, top_ref, bottom_ref = outs[7:]
    vmem = rest[count + 11 : -1]
    semaphores = rest[-1]
    copies = [
        pltpu.make_async_copy(source, target, semaphores.at[at])
        for at, (source, target) in enumerate(zip(hbm, vmem))
    ]
    for copy in copies:
        copy.start()
    mask_ref, dual_ref, quad_ref, rows_ref, kernels_ref, *core_refs, target_ref = vmem
    size = mask_ref.shape[0]
    band = base_ref.shape[0]
    width = 4 * band
    edge = size - INTERSECTION
    row, col, rows = place(total)
    even_row, even_col = row % 2 == 0, col % 2 == 0
    for copy in copies[:4]:
        copy.wait()

    quad = quad_ref[...]
    scaled = quad * edge_scale((size, 1), 0, size, col > 0, col < GRID_COLS - 1).astype(BF16)
    pair = jnp.concatenate([quad, scaled], axis=1)
    mask_part = dot(mask_ref[...].astype(BF16), pair)
    dual_part = dot(dual_ref[...].astype(BF16), pair)

    def share(begin, end):
        return (0.5 * (mask_ref[:, begin:end] + dual_ref[:, begin:end])).astype(BF16)

    lines = rows_ref[...]
    line_scale = edge_scale((1, size), 1, size, row > 0, row < rows - 1).astype(BF16)
    whole = row_transform(lines, jnp.concatenate([mask_part[:, :width], dual_part[:, :width]], axis=1))
    outer = jnp.concatenate(
        [
            mask_part[:, width:] + dual_part[:, width:],
            dot(share(0, INTERSECTION), quad[edge:]),
            dot(share(edge, size), quad[:INTERSECTION]),
        ],
        axis=1,
    ).astype(BF16)
    around = row_transform(lines * line_scale, outer)
    upper = 0.5 * row_transform(lines[:, edge:], outer[:INTERSECTION])
    lower = 0.5 * row_transform(lines[:, :INTERSECTION], outer[edge:])

    def block(value, at):
        return quad_form(value[:, at * width : (at + 1) * width])

    spectrum, dual_spectrum = block(whole, 0), block(whole, 1)
    base_ref[...] = 0.5 * spectrum - 0.25 * dual_spectrum
    own_ref[: 3 * band, :] = jnp.concatenate([block(around, 0), block(upper, 0), block(lower, 0)], axis=0)

    def strips(lines_at, lanes_at):
        mask, dual = mask_ref[lines_at, lanes_at], dual_ref[lines_at, lanes_at]
        return mask + dual, mask + 0.25 * dual

    ends = (slice(0, INTERSECTION), slice(edge, size))
    inner = slice(INTERSECTION, edge)
    for out, lines_at in ((0, ends[0]), (INTERSECTION, ends[1])):
        near = jnp.concatenate(strips(lines_at, ends[0]), axis=1)
        far = jnp.concatenate(strips(lines_at, ends[1]), axis=1)
        corner1_ref[out : out + INTERSECTION, :] = jnp.where(even_col, far, near)
        corner2_ref[out : out + INTERSECTION, :] = jnp.where(even_col, near, far)
        edges_ref = top_ref if out == 0 else bottom_ref
        edges_ref[:INTERSECTION, :] = jnp.concatenate([near[:, :INTERSECTION], far[:, :INTERSECTION]], axis=1)
        edges_ref[INTERSECTION:, :] = jnp.concatenate([near[:, INTERSECTION:], far[:, INTERSECTION:]], axis=1)
    near = jnp.concatenate(strips(inner, ends[0]), axis=1)
    far = jnp.concatenate(strips(inner, ends[1]), axis=1)
    middle1_ref[...] = jnp.where(even_col, far, near)
    middle2_ref[...] = jnp.where(even_col, near, far)
    upper_strip = jnp.concatenate(strips(ends[0], inner), axis=0)
    lower_strip = jnp.concatenate(strips(ends[1], inner), axis=0)
    line1_ref[...] = jnp.where(even_row, lower_strip, upper_strip)
    line2_ref[...] = jnp.where(even_row, upper_strip, lower_strip)

    for copy in copies[4:]:
        copy.wait()
    gates = gates_of(kernels_ref, weights_ref, band)
    gates_ref[...] = gates
    adjoint = adjoint_of(spectrum, gates, target_ref, dict(zip(CORE_TABLES, core_refs)))
    own_ref[3 * band :, :] = adjoint
    left = [block(around, 1), block(upper, 1), block(lower, 1)]
    right = [block(around, 2), block(upper, 2), block(lower, 2)]
    for ref, first, second in ((corner1_ref, right, left), (corner2_ref, left, right)):
        chosen = [jnp.where(even_col, a, b) for a, b in zip(first, second)] + [adjoint]
        ref[2 * INTERSECTION :, :] = jnp.concatenate(
            [jnp.concatenate(chosen[:2], axis=0), jnp.concatenate(chosen[2:], axis=0)], axis=1
        )


def unpack(ref):
    tail = ref[2 * INTERSECTION :, :]
    band, width = tail.shape[0] // 2, tail.shape[1] // 2
    return tail[:band, :width], tail[band:, :width], tail[:band, width:], tail[band:, width:]


def pack(ref, blocks):
    ref[2 * INTERSECTION :, :] = jnp.concatenate(
        [jnp.concatenate(blocks[:2], axis=0), jnp.concatenate(blocks[2:], axis=0)], axis=1
    )


def middle_kernel(total, own_ref, got1_ref, got2_ref, top_ref, bottom_ref, keep_ref, send1_ref, send2_ref):
    band = keep_ref.shape[0]
    row, col, rows = place(total)
    even_row, even_col = row % 2 == 0, col % 2 == 0
    one, two = unpack(got1_ref), unpack(got2_ref)
    mine = [own_ref[at * band : (at + 1) * band, :] for at in range(4)]
    keep, upper, lower = [mine[at] + one[at] + two[at] for at in range(3)]
    keep_ref[...] = keep
    adjoints = [mine[3], one[3], two[3]]
    pack(send1_ref, [jnp.where(even_row, lower, upper)] + adjoints)
    pack(send2_ref, [jnp.where(even_row, upper, lower)] + adjoints)
    summed = []
    for begin, edges_ref in ((0, top_ref), (INTERSECTION, bottom_ref)):
        first, second = got1_ref[begin : begin + INTERSECTION, :], got2_ref[begin : begin + INTERSECTION, :]
        left, right = jnp.where(even_col, second, first), jnp.where(even_col, first, second)
        cut = INTERSECTION
        summed.append(
            edges_ref[...]
            + jnp.concatenate(
                [
                    jnp.concatenate([left[:, :cut], right[:, :cut]], axis=1),
                    jnp.concatenate([left[:, cut:], right[:, cut:]], axis=1),
                ],
                axis=0,
            )
        )
    send1_ref[: 2 * INTERSECTION, :] = jnp.where(even_row, summed[1], summed[0])
    send2_ref[: 2 * INTERSECTION, :] = jnp.where(even_row, summed[0], summed[1])


def second_kernel(base_ref, keep_ref, got1_ref, got2_ref, own_ref, lanes_ref, flip_ref, gates_ref, target_ref, *rest):
    tables = dict(zip(CORE_TABLES, rest))
    out_ref = rest[len(CORE_TABLES)]
    band = base_ref.shape[0]
    adjoint = own_ref[3 * band :, :]
    width = adjoint.shape[1]
    agreed = keep_ref[...] + unpack(got1_ref)[0] + unpack(got2_ref)[0]
    high, low = split(adjoint)
    lanes = lax.broadcasted_iota(jnp.int32, adjoint.shape, 1)
    mirrored = dot(jnp.where(lanes < width // 2, high, low), lanes_ref[...])
    high, low = split(mirrored[:, width:])
    flip = flip_ref[...]
    gradient_band = mirrored[:, :width] + dot(flip, high) + dot(flip, low)
    spectrum = base_ref[...] + 0.5 * agreed - 0.25 * gradient_band
    out_ref[...] = adjoint_of(spectrum, gates_ref[...], target_ref, tables)


def last_kernel(total, mask_ref, dual_ref, corner1_ref, corner2_ref, middle1_ref, middle2_ref, edge1_ref, edge2_ref, line1_ref, line2_ref, own_ref, adjoint_ref, tail_ref, final_ref, final_edge_ref, mask_hbm, dual_hbm, mask_out, dual_out, semaphores):
    size = mask_ref.shape[0]
    band, width = adjoint_ref.shape
    half = width // 2
    edge = size - INTERSECTION
    row, col, rows = place(total)
    even_row, even_col = row % 2 == 0, col % 2 == 0
    scale = 2.0 / (size * size)
    lanes = lax.broadcasted_iota(jnp.int32, (1, width), 1)
    tail_table = tail_ref[...]

    def spread(blocks, table):
        high, low = split(blocks * scale)
        pair = jnp.where(lanes < half, high, low)
        return dot(jnp.concatenate([pair, high], axis=1), table)

    def piece(begin, end):
        return jnp.concatenate([tail_table[:, begin:end], tail_table[:, size + begin : size + end]], axis=1)

    def stack(value, at):
        wide = value.shape[1] // 2
        lines = value[at * band : (at + 1) * band]
        return jnp.concatenate([lines[:, :wide], lines[:, wide:]], axis=0)

    one, two = unpack(edge1_ref), unpack(edge2_ref)
    mine = own_ref[3 * band :, :]
    own = [mine, unpack(corner1_ref)[3], unpack(corner2_ref)[3]]
    above = [jnp.where(even_row, two[at], one[at]) for at in (1, 2, 3)]
    below = [jnp.where(even_row, one[at], two[at]) for at in (1, 2, 3)]

    def column(at):
        return jnp.concatenate([own[at], above[at], below[at]], axis=0)

    first1, first2 = column(1), column(2)
    left = jnp.where(even_col, first2, first1)
    right = jnp.where(even_col, first1, first2)
    tails = spread(jnp.concatenate([column(0), adjoint_ref[...]], axis=0), tail_table)
    left_tails = spread(left, piece(edge, size))
    right_tails = spread(right, piece(0, INTERSECTION))
    columns = edge_scale((1, size), 1, size, col > 0, col < GRID_COLS - 1)

    def summed_tail(at):
        middle = stack(tails, at)
        lhs = stack(left_tails, at)
        rhs = stack(right_tails, at)
        return columns * jnp.concatenate(
            [middle[:, :INTERSECTION] + lhs, middle[:, INTERSECTION:edge], middle[:, edge:] + rhs], axis=1
        )

    def deep(value):
        high, low = split(value)
        return jnp.concatenate([high, low, high], axis=0)

    summed = [summed_tail(at) for at in range(3)]
    own_tail, new_tail = stack(tails, 0), stack(tails, 3)

    def pairs(share, tail, with_own):
        mask_part, dual_part = (-0.125 * share) * tail, (0.25 * share) * tail
        if with_own:
            mask_part = mask_part - 0.125 * own_tail - 0.25 * new_tail
            dual_part = dual_part - 0.25 * own_tail
        return deep(jnp.concatenate([mask_part, dual_part], axis=1))

    up_share, low_share = share_of(row > 0), share_of(row < rows - 1)
    inner_rhs = pairs(1.0, summed[0], True)
    copies = []
    for at, begin in enumerate(range(0, size, INTERSECTION)):
        end = begin + INTERSECTION
        mask, dual = mask_ref[begin:end, :], dual_ref[begin:end, :]
        table = final_ref[begin:end, :]
        if begin == 0:
            products = dot(table, pairs(up_share, summed[0], True)) + dot(
                final_edge_ref[:INTERSECTION, :], pairs(up_share, summed[1], False)
            )
        elif end == size:
            products = dot(table, pairs(low_share, summed[0], True)) + dot(
                final_edge_ref[INTERSECTION:, :], pairs(low_share, summed[2], False)
            )
        else:
            products = dot(table, inner_rhs)
        if begin == 0 or end == size:
            out = 0 if begin == 0 else INTERSECTION
            ends1, ends2 = corner1_ref[out : out + INTERSECTION, :], corner2_ref[out : out + INTERSECTION, :]
        else:
            out = begin - INTERSECTION
            ends1, ends2 = middle1_ref[out : out + INTERSECTION, :], middle2_ref[out : out + INTERSECTION, :]
        left_ends = jnp.where(even_col, ends2, ends1)
        right_ends = jnp.where(even_col, ends1, ends2)

        def joined(value, part):
            cut = slice(part * INTERSECTION, (part + 1) * INTERSECTION)
            return jnp.concatenate(
                [value[:, :INTERSECTION] + left_ends[:, cut], value[:, INTERSECTION:edge], value[:, edge:] + right_ends[:, cut]],
                axis=1,
            )

        first = joined(mask + dual, 0)
        second = joined(mask + 0.25 * dual, 1)
        share = columns
        if begin == 0 or end == size:
            upper = begin == 0
            side1, side2 = (edge2_ref, edge1_ref) if upper else (edge1_ref, edge2_ref)
            mid1, mid2 = (line2_ref, line1_ref) if upper else (line1_ref, line2_ref)
            share = columns * (up_share if upper else low_share)

            def across(part):
                cut = slice(part * INTERSECTION, (part + 1) * INTERSECTION)
                ends = jnp.where(even_row, side1[cut, :], side2[cut, :])
                inner = jnp.where(even_row, mid1[cut, :], mid2[cut, :])
                return jnp.concatenate([ends[:, :INTERSECTION], inner, ends[:, INTERSECTION:]], axis=1)

            first = first + across(0)
            second = second + across(1)
        agreed0 = first * share
        agreed1 = second * share
        dual_out[begin:end, :] = 1.5 * mask + 0.75 * dual - 0.5 * agreed0 - agreed1 + products[:, size:]
        mask_out[begin:end, :] = 0.5 * (agreed0 + agreed1) - 0.375 * dual + products[:, :size]
        for which, (source, target) in enumerate(((mask_out, mask_hbm), (dual_out, dual_hbm))):
            copy = pltpu.make_async_copy(
                source.at[begin:end, :], target.at[begin:end, :], semaphores.at[which, at]
            )
            copy.start()
            copies.append(copy)
    for copy in copies:
        copy.wait()


VMEM_SPEC = pl.BlockSpec(memory_space=pltpu.VMEM)
SMEM_SPEC = pl.BlockSpec(memory_space=pltpu.SMEM)
HBM_SPEC = pl.BlockSpec(memory_space=pltpu.HBM)


def call(kernel, outs, operands, flops, name, in_specs=None, out_spec=VMEM_SPEC, scratch=()):
    return pl.pallas_call(
        kernel,
        out_shape=[jax.ShapeDtypeStruct(shape, dtype) for shape, dtype in outs],
        in_specs=in_specs or [VMEM_SPEC] * len(operands),
        out_specs=[out_spec] * len(outs),
        scratch_shapes=list(scratch),
        compiler_params=pltpu.CompilerParams(vmem_limit_bytes=VMEM_LIMIT),
        cost_estimate=pl.CostEstimate(flops=flops, bytes_accessed=1 << 20, transcendentals=0),
        name=name,
    )(*operands)


def swaps(total):
    cols = GRID_COLS
    sets = [[], [], [], []]
    for index in range(total):
        row, col = index // cols, index % cols
        if col + 1 < cols:
            sets[col % 2] += [(index, index + 1), (index + 1, index)]
        if index + cols < total:
            sets[2 + row % 2] += [(index, index + cols), (index + cols, index)]
    return sets


def per_device(mask_init, dual_init, target, kernels, weights):
    mask, dual, goal = mask_init[0], dual_init[0], target[0]
    size = mask.shape[0]
    count = kernels.shape[0]
    band = math.isqrt(kernels.shape[2])
    width = 4 * band
    total = lax.axis_size("ty")
    row_pairs1, row_pairs2, col_pairs1, col_pairs2 = swaps(total)
    tables = {name: jnp.asarray(table) for name, table in build_tables(size, band).items()}
    core = [tables[name] for name in CORE_TABLES]

    def trade(value, pairs):
        return lax.ppermute(value, "ty", pairs)

    both = 2 * INTERSECTION
    inner = size - both
    block = ((band, width), F32)
    message = ((both + 2 * band, both), F32)
    operands = [weights, mask, dual, kernels, goal] + [tables[name] for name in OPEN_TABLES]
    staged = [mask, dual, tables["quad"], tables["rows"], kernels] + core + [goal]
    base, gates, own, corner1, corner2, middle1, middle2, line1, line2, top, bottom = call(
        functools.partial(open_kernel, total),
        [block, ((count * band, width), F32), ((4 * band, width), F32), message, message]
        + [((inner, both), F32)] * 2
        + [((both, inner), F32)] * 2
        + [((both, both), F32)] * 2,
        operands,
        4 * 10**9,
        "open",
        in_specs=[SMEM_SPEC] + [HBM_SPEC] * (len(operands) - 1),
        scratch=[pltpu.VMEM(value.shape, value.dtype) for value in staged] + [pltpu.SemaphoreType.DMA((len(staged),))],
    )
    corners2, corners1 = trade(corner2, row_pairs2), trade(corner1, row_pairs1)
    lines1, lines2 = trade(line1, col_pairs1), trade(line2, col_pairs2)
    keep, edge1, edge2 = call(
        functools.partial(middle_kernel, total),
        [block, message, message],
        [own, corners1, corners2, top, bottom],
        10**7,
        "middle",
    )
    edges1, edges2 = trade(edge1, col_pairs1), trade(edge2, col_pairs2)
    middles2, middles1 = trade(middle2, row_pairs2), trade(middle1, row_pairs1)
    (adjoint1,) = call(
        second_kernel,
        [block],
        [base, keep, edges1, edges2, own, tables["mirror_lanes"], tables["mirror_rows"], gates, goal] + core,
        3 * 10**9,
        "second",
    )
    whole = ((size, size), F32)
    mask, dual = call(
        functools.partial(last_kernel, total),
        [whole, whole],
        [mask, dual, corners1, corners2, middles1, middles2, edges1, edges2, lines1, lines2, own, adjoint1]
        + [tables["tail"], tables["final"], tables["final_edge"]],
        2 * 10**9,
        "last",
        out_spec=HBM_SPEC,
        scratch=[
            pltpu.VMEM((size, size), F32),
            pltpu.VMEM((size, size), F32),
            pltpu.SemaphoreType.DMA((2, size // INTERSECTION)),
        ],
    )
    return (mask[None], dual[None])


def solution(mesh):
    tiles = P(("region", "ty"), None, None)
    return jax.shard_map(
        per_device,
        mesh=mesh,
        in_specs=(tiles, tiles, tiles, P(), P()),
        out_specs=(tiles, tiles),
        check_vma=False,
    )
```

```python
import functools
import math

import jax
import jax.numpy as jnp
import ml_dtypes
import numpy as np
from jax import lax
from jax.experimental import pallas as pl
from jax.experimental.pallas import tpu as pltpu
from jax.sharding import PartitionSpec as P

INTERSECTION = 128
GRID_COLS = 4
SHARPNESS = 8.0
THRESHOLD = 0.3
F32 = jnp.float32
BF16 = jnp.bfloat16
VMEM_LIMIT = 32 * 1024 * 1024


def halves(table):
    high = table.astype(ml_dtypes.bfloat16)
    low = (table - high.astype(np.float64)).astype(ml_dtypes.bfloat16)
    return high, low


def build_tables(size, band):
    coarse = 2 * band
    stride = size // coarse
    edge = size - INTERSECTION
    frequencies = np.arange(band) - band // 2
    angles = 2.0 * np.pi * ((frequencies[:, None] * np.arange(size)[None, :]) % size) / size
    cos, sin = np.cos(angles), -np.sin(angles)
    order = np.arange(band).reshape(-1, 128 // band).T.reshape(-1)
    rows = np.concatenate([cos[order], sin[order]], axis=0)
    quad = np.concatenate([cos.T, sin.T, -sin.T, cos.T], axis=1)
    dc, ds = cos[:, ::stride], sin[:, ::stride]
    dc_rows, ds_rows = dc[order], ds[order]
    wide = np.arange(-(band - 1), band)
    gaps = np.arange(size)[:, None] - stride * np.arange(coarse)[None, :]
    lift = np.cos(2.0 * np.pi * wide[:, None, None] * gaps[None] / size).sum(0) / coarse

    tables = {}
    tables["quad"] = halves(quad)[0]
    high, low = halves(rows)
    tables["rows"] = np.concatenate([high, low], axis=0)
    spread = np.concatenate(
        [np.concatenate([dc, -ds, -ds, -dc], axis=1), np.concatenate([ds, dc, dc, -ds], axis=1)], axis=0
    )
    high, low = halves(np.concatenate([spread, spread], axis=0))
    tables["spread"] = np.concatenate([high, high, low], axis=0)
    high, low = halves(np.concatenate([dc_rows.T, ds_rows.T], axis=1))
    tables["field"] = np.concatenate([high, high, low], axis=1)
    high, low = halves(np.concatenate([lift.T, lift.T], axis=0))
    tables["lift_cols"] = np.concatenate([high, low], axis=0)
    high, low = halves(lift * (0.5 * SHARPNESS))
    tables["lift_rows"] = np.concatenate([high, high, low], axis=1)
    high, low = halves(lift)
    tables["drop_cols"] = np.concatenate([high, high, low, low], axis=1)
    high, low = halves(lift.T * (0.25 * SHARPNESS))
    tables["drop_rows"] = np.concatenate([high, low], axis=0)
    high, low = halves(np.concatenate([dc_rows, ds_rows], axis=0))
    tables["turn"] = np.concatenate([high, high, low], axis=1)
    back_real = np.concatenate([dc.T, -ds.T, -ds.T, -dc.T], axis=0)
    back_imag = np.concatenate([ds.T, dc.T, dc.T, -ds.T], axis=0)
    high, low = halves(np.concatenate([back_real, back_imag, back_imag, -back_real], axis=1))
    tables["back"] = np.concatenate([high, low], axis=1)
    flip = np.zeros((band, band))
    for place in range(1, band):
        flip[place, band - place] = 1.0
    eye, zero = np.eye(band), np.zeros((band, band))
    own = np.concatenate(
        [
            np.concatenate([eye, zero, zero, eye], axis=1),
            np.concatenate([zero, eye, -eye, zero], axis=1),
        ],
        axis=0,
    )
    turned = np.concatenate(
        [
            np.concatenate([flip, zero, zero, flip], axis=1),
            np.concatenate([zero, -flip, flip, zero], axis=1),
        ],
        axis=0,
    )
    tables["mirror_lanes"] = np.concatenate(
        [np.concatenate([own, own], axis=0), np.concatenate([turned, turned], axis=0)], axis=1
    ).astype(ml_dtypes.bfloat16)
    tables["mirror_rows"] = flip[order][:, order].astype(ml_dtypes.bfloat16)
    tail = np.concatenate([np.concatenate([cos, -sin], axis=1), np.concatenate([sin, cos], axis=1)], axis=0)
    high, low = halves(tail)
    tables["tail"] = np.concatenate([high, high, low, np.zeros_like(low)], axis=0)
    high, low = halves(rows.T)
    tables["final"] = np.concatenate([high, high, low], axis=1)
    near, far = rows[:, :INTERSECTION], rows[:, edge:]
    high, low = halves(np.concatenate([far.T, near.T], axis=0))
    tables["final_edge"] = np.concatenate([high, high, low], axis=1)
    return tables


def dot(left, right):
    return lax.dot_general(left, right, (((1,), (0,)), ((), ())), preferred_element_type=F32)


def split(value):
    high = value.astype(BF16)
    return high, (value - high.astype(F32)).astype(BF16)


def place(total):
    index = lax.axis_index("ty")
    row, col = index // GRID_COLS, index % GRID_COLS
    return row, col, total // GRID_COLS


def share_of(present):
    return jnp.where(present, 0.5, 1.0).astype(F32)


def edge_scale(shape, dim, size, before, after):
    steps = lax.broadcasted_iota(jnp.int32, shape, dim)
    first = jnp.where(steps < INTERSECTION, share_of(before), 1.0)
    return first * jnp.where(steps >= size - INTERSECTION, share_of(after), 1.0)


def quad_form(value):
    half = value.shape[0] // 2
    width = value.shape[1]
    lanes = lax.broadcasted_iota(jnp.int32, (half, width), 1)
    rolled = pltpu.roll(value[half:], width // 2, 1)
    return value[:half] + jnp.where(lanes < width // 2, rolled, -rolled)


def row_transform(table, value):
    half = table.shape[0] // 2
    both = dot(table, value.astype(BF16))
    return both[:half] + both[half:]


def gates_of(kernels_ref, weights_ref, band):
    count, parts, length = kernels_ref.shape
    lanes = 128
    groups = lanes // band
    chunks = length // lanes
    total = weights_ref[0]
    for k in range(1, count):
        total = total + weights_ref[k]
    group = lax.broadcasted_iota(jnp.int32, (chunks, lanes), 1) // band
    blocks = []
    for k in range(count):
        gain = jnp.sqrt(jnp.full((chunks, lanes), weights_ref[k], F32) / total)
        real, imag = [
            gain
            * jnp.concatenate(
                [kernels_ref[k, part : part + 1, c * lanes : (c + 1) * lanes] for c in range(chunks)], axis=0
            )
            for part in range(2)
        ]
        reals = [pltpu.roll(real, band * g, 1) if g else real for g in range(groups)]
        imags = [pltpu.roll(imag, band * g, 1) if g else imag for g in range(groups)]
        for at in range(groups):
            line = imags[(3 - at) % groups]
            line = jnp.where(group == 2, imags[(2 - at) % groups], line)
            line = jnp.where(group == 1, reals[(1 - at) % groups], line)
            blocks.append(jnp.where(group == 0, reals[-at % groups], line))
    return jnp.concatenate(blocks, axis=0)


def adjoint_of(spectrum, gates, target_ref, tables):
    band = spectrum.shape[0]
    width = 4 * band
    kernels = gates.shape[0] // band
    size = target_ref.shape[0]
    scaled = spectrum * (1.0 / (size * size))
    high, low = split(gates * jnp.concatenate([scaled] * kernels, axis=0))
    bands = dot(jnp.concatenate([high, low, high], axis=1), tables["spread"][...])
    stacked = jnp.concatenate(
        [
            jnp.concatenate([bands[band * k : band * (k + 1), :width] for k in range(kernels)], axis=1),
            jnp.concatenate([bands[band * k : band * (k + 1), width:] for k in range(kernels)], axis=1),
        ],
        axis=0,
    )
    high, low = split(stacked)
    fields = dot(tables["field"][...], jnp.concatenate([high, low, high], axis=0))
    squares = fields * fields
    power = squares[:, :width]
    for k in range(1, kernels):
        power = power + squares[:, k * width : (k + 1) * width]
    high, low = split(power)
    lifted = dot(high, tables["lift_cols"][:width, :]) + dot(
        jnp.concatenate([low, high], axis=1), tables["lift_cols"][...]
    )
    high, low = split(lifted)
    half = dot(tables["lift_rows"][...], jnp.concatenate([high, low, high], axis=0))
    curve = jnp.tanh(half - 0.5 * SHARPNESS * THRESHOLD)
    slope = (1.0 + curve - 2.0 * target_ref[...].astype(F32)) * (1.0 - curve * curve)
    both = dot(slope.astype(BF16), tables["drop_cols"][...])
    dropped = row_transform(tables["drop_rows"][...], both[:, :width] + both[:, width:])
    weighted = fields * jnp.concatenate([dropped] * kernels, axis=1)
    high, low = split(weighted)
    turned = dot(tables["turn"][...], jnp.concatenate([high, low, high], axis=0))
    across = jnp.concatenate(
        [
            jnp.concatenate([turned[:band, k * width : (k + 1) * width] for k in range(kernels)], axis=0),
            jnp.concatenate([turned[band:, k * width : (k + 1) * width] for k in range(kernels)], axis=0),
        ],
        axis=1,
    )
    both = dot(across.astype(BF16), tables["back"][...])
    product = gates * (both[:, :width] + both[:, width:])
    adjoint = product[:band]
    for k in range(1, kernels):
        adjoint = adjoint + product[k * band : (k + 1) * band]
    return adjoint + pltpu.roll(adjoint, width // 2, 1)


CORE_TABLES = ("spread", "field", "lift_cols", "lift_rows", "drop_cols", "drop_rows", "turn", "back")
OPEN_TABLES = ("quad", "rows") + CORE_TABLES


def open_kernel(total, weights_hbm, mask_hbm, dual_hbm, kernels_hbm, target_hbm, *rest):
    count = len(OPEN_TABLES)
    tables_hbm, rest = rest[:count], rest[count:]
    outs, rest = rest[:10], rest[10:]
    base_ref, gates_ref, own_ref, corner1, corner2, middle1, middle2, line1, line2, edges_ref = outs
    sources = [*tables_hbm[:2], kernels_hbm, weights_hbm, *tables_hbm[2:], target_hbm]
    mask_ref, dual_ref = rest[:2]
    staged, (line_semaphores, semaphores) = rest[2:-2], rest[-2:]
    size = mask_ref.shape[0]
    pieces = size // INTERSECTION
    edge = size - INTERSECTION

    def cut(at):
        return slice(at * INTERSECTION, (at + 1) * INTERSECTION)

    copies = [
        pltpu.make_async_copy(source, target, semaphores.at[at])
        for at, (source, target) in enumerate(zip(sources, staged))
    ]
    parts = [
        [
            pltpu.make_async_copy(source.at[cut(at), :], target.at[cut(at), :], line_semaphores.at[which, at])
            for which, (source, target) in enumerate(((mask_hbm, mask_ref), (dual_hbm, dual_ref)))
        ]
        for at in range(pieces)
    ]
    copies[0].start()
    for pair in parts:
        for copy in pair:
            copy.start()
    for copy in copies[1:]:
        copy.start()
    quad_ref, rows_ref, kernels_ref, weights_ref, *core_refs, target_ref = staged
    band = base_ref.shape[0]
    width = 4 * band
    row, col, rows = place(total)
    even_row, even_col = row % 2 == 0, col % 2 == 0

    copies[0].wait()
    quad = quad_ref[...]
    scaled = quad * edge_scale((size, 1), 0, size, col > 0, col < GRID_COLS - 1).astype(BF16)
    pair = jnp.concatenate([quad, scaled], axis=1)
    mask_parts, dual_parts, lefts, rights, strips = [], [], [], [], {}
    for at in range(pieces):
        for copy in parts[at]:
            copy.wait()
        mask, dual = mask_ref[cut(at), :], dual_ref[cut(at), :]
        mask_parts.append(dot(mask.astype(BF16), pair))
        dual_parts.append(dot(dual.astype(BF16), pair))
        first, second = mask + dual, mask + 0.25 * dual
        near = jnp.concatenate([first[:, :INTERSECTION], second[:, :INTERSECTION]], axis=1)
        far = jnp.concatenate([first[:, edge:], second[:, edge:]], axis=1)
        lefts.append(dot((0.5 * near[:, :INTERSECTION]).astype(BF16), quad[edge:]))
        rights.append(dot((0.5 * far[:, :INTERSECTION]).astype(BF16), quad[:INTERSECTION]))
        to1, to2 = jnp.where(even_col, far, near), jnp.where(even_col, near, far)
        if at == 0 or at == pieces - 1:
            out = cut(0 if at == 0 else 1)
            corner1[out, :], corner2[out, :] = to1, to2
            strips[at] = (first, second)
        else:
            out = cut(at - 1)
            middle1[out, :], middle2[out, :] = to1, to2
    for part, lines in enumerate((cut(0), cut(1))):
        upper, lower = strips[0][part], strips[pieces - 1][part]
        for at, strip in enumerate((upper, lower)):
            edges_ref[at, lines, :] = jnp.concatenate([strip[:, :INTERSECTION], strip[:, edge:]], axis=1)
        upper, lower = upper[:, INTERSECTION:edge], lower[:, INTERSECTION:edge]
        line1[lines, :] = jnp.where(even_row, lower, upper)
        line2[lines, :] = jnp.where(even_row, upper, lower)

    mask_part = jnp.concatenate(mask_parts, axis=0)
    dual_part = jnp.concatenate(dual_parts, axis=0)
    copies[1].wait()
    lines = rows_ref[...]
    line_scale = edge_scale((1, size), 1, size, row > 0, row < rows - 1).astype(BF16)
    whole = row_transform(lines, jnp.concatenate([mask_part[:, :width], dual_part[:, :width]], axis=1))
    outer = jnp.concatenate(
        [
            mask_part[:, width:] + dual_part[:, width:],
            jnp.concatenate(lefts, axis=0),
            jnp.concatenate(rights, axis=0),
        ],
        axis=1,
    ).astype(BF16)
    around = row_transform(lines * line_scale, outer)
    upper = 0.5 * row_transform(lines[:, edge:], outer[:INTERSECTION])
    lower = 0.5 * row_transform(lines[:, :INTERSECTION], outer[edge:])

    def block(value, at):
        return quad_form(value[:, at * width : (at + 1) * width])

    spectrum, dual_spectrum = block(whole, 0), block(whole, 1)
    base_ref[...] = 0.5 * spectrum - 0.25 * dual_spectrum

    for copy in copies[2:]:
        copy.wait()
    gates = gates_of(kernels_ref, weights_ref, band)
    gates_ref[...] = gates
    adjoint = adjoint_of(spectrum, gates, target_ref, dict(zip(CORE_TABLES, core_refs)))
    own_ref[...] = jnp.concatenate([block(around, 0), block(upper, 0), block(lower, 0), adjoint], axis=0)
    left = [block(around, 1), block(upper, 1), block(lower, 1)]
    right = [block(around, 2), block(upper, 2), block(lower, 2)]
    tail = slice(2 * INTERSECTION, 2 * INTERSECTION + 2 * band)
    for ref, first, second in ((corner1, right, left), (corner2, left, right)):
        ref[tail, :] = pack([jnp.where(even_col, a, b) for a, b in zip(first, second)] + [adjoint])


def unpack(ref, band):
    tail = ref[ref.shape[0] - 2 * band :, :]
    width = tail.shape[1] // 2
    return tail[:band, :width], tail[band:, :width], tail[:band, width:], tail[band:, width:]


def pack(blocks):
    return jnp.concatenate([jnp.concatenate(blocks[:2], axis=0), jnp.concatenate(blocks[2:], axis=0)], axis=1)


def middle_kernel(total, own_ref, got1_ref, got2_ref, edges_ref, line1_ref, line2_ref, keep_ref, send1_ref, send2_ref):
    band = keep_ref.shape[0]
    row, col, rows = place(total)
    even_row, even_col = row % 2 == 0, col % 2 == 0
    summed = []
    for at in range(2):
        lines = slice(at * INTERSECTION, (at + 1) * INTERSECTION)
        first, second = got1_ref[lines, :], got2_ref[lines, :]
        left, right = jnp.where(even_col, second, first), jnp.where(even_col, first, second)
        cut = INTERSECTION
        summed.append(
            edges_ref[at]
            + jnp.concatenate(
                [
                    jnp.concatenate([left[:, :cut], right[:, :cut]], axis=1),
                    jnp.concatenate([left[:, cut:], right[:, cut:]], axis=1),
                ],
                axis=0,
            )
        )
    both, inner = slice(0, 2 * INTERSECTION), slice(2 * INTERSECTION, 4 * INTERSECTION)
    tail = slice(4 * INTERSECTION, 4 * INTERSECTION + 2 * band)
    one, two = unpack(got1_ref, band), unpack(got2_ref, band)
    mine = [own_ref[at * band : (at + 1) * band, :] for at in range(4)]
    keep, upper, lower = [mine[at] + one[at] + two[at] for at in range(3)]
    keep_ref[...] = keep
    adjoints = [mine[3], one[3], two[3]]
    for ref, line_ref, on_even, on_odd in ((send1_ref, line1_ref, 1, 0), (send2_ref, line2_ref, 0, 1)):
        ref[both, :] = jnp.where(even_row, summed[on_even], summed[on_odd])
        ref[inner, :] = line_ref[...]
        ref[tail, :] = pack([jnp.where(even_row, (upper, lower)[on_even], (upper, lower)[on_odd])] + adjoints)


def prepare_kernel(base_ref, keep_ref, own_ref, lanes_ref, flip_ref, gates_ref, out_ref, gates_out):
    band = base_ref.shape[0]
    adjoint = own_ref[3 * band :, :]
    width = adjoint.shape[1]
    high, low = split(adjoint)
    lanes = lax.broadcasted_iota(jnp.int32, adjoint.shape, 1)
    mirrored = dot(jnp.where(lanes < width // 2, high, low), lanes_ref[...])
    high, low = split(mirrored[:, width:])
    flip = flip_ref[...]
    gradient_band = mirrored[:, :width] + dot(flip, high) + dot(flip, low)
    out_ref[...] = base_ref[...] + 0.5 * keep_ref[...] - 0.25 * gradient_band
    gates_out[...] = gates_ref[...]


def second_kernel(part_ref, got1_ref, got2_ref, gates_ref, target_ref, *rest):
    tables = dict(zip(CORE_TABLES, rest))
    out_ref = rest[len(CORE_TABLES)]
    band = part_ref.shape[0]
    spectrum = part_ref[...] + 0.5 * (unpack(got1_ref, band)[0] + unpack(got2_ref, band)[0])
    out_ref[...] = adjoint_of(spectrum, gates_ref[...], target_ref, tables)


def last_kernel(total, mask_ref, dual_ref, corner1_ref, corner2_ref, middle1_ref, middle2_ref, edge1_ref, edge2_ref, own_ref, adjoint_ref, tail_ref, final_ref, final_edge_ref, mask_hbm, dual_hbm, mask_out, dual_out, semaphores):
    size = mask_ref.shape[0]
    band, width = adjoint_ref.shape
    half = width // 2
    edge = size - INTERSECTION
    row, col, rows = place(total)
    even_row, even_col = row % 2 == 0, col % 2 == 0
    scale = 2.0 / (size * size)
    lanes = lax.broadcasted_iota(jnp.int32, (1, width), 1)
    tail_table = tail_ref[...]

    def spread(blocks, table):
        high, low = split(blocks * scale)
        pair = jnp.where(lanes < half, high, low)
        return dot(jnp.concatenate([pair, high], axis=1), table)

    def piece(begin, end):
        return jnp.concatenate([tail_table[:, begin:end], tail_table[:, size + begin : size + end]], axis=1)

    def stack(value, at):
        wide = value.shape[1] // 2
        lines = value[at * band : (at + 1) * band]
        return jnp.concatenate([lines[:, :wide], lines[:, wide:]], axis=0)

    one, two = unpack(edge1_ref, band), unpack(edge2_ref, band)
    mine = own_ref[3 * band :, :]
    own = [mine, unpack(corner1_ref, band)[3], unpack(corner2_ref, band)[3]]
    above = [jnp.where(even_row, two[at], one[at]) for at in (1, 2, 3)]
    below = [jnp.where(even_row, one[at], two[at]) for at in (1, 2, 3)]

    def column(at):
        return jnp.concatenate([own[at], above[at], below[at]], axis=0)

    first1, first2 = column(1), column(2)
    left = jnp.where(even_col, first2, first1)
    right = jnp.where(even_col, first1, first2)
    tails = spread(jnp.concatenate([column(0), adjoint_ref[...]], axis=0), tail_table)
    left_tails = spread(left, piece(edge, size))
    right_tails = spread(right, piece(0, INTERSECTION))
    columns = edge_scale((1, size), 1, size, col > 0, col < GRID_COLS - 1)

    def summed_tail(at):
        middle = stack(tails, at)
        lhs = stack(left_tails, at)
        rhs = stack(right_tails, at)
        return columns * jnp.concatenate(
            [middle[:, :INTERSECTION] + lhs, middle[:, INTERSECTION:edge], middle[:, edge:] + rhs], axis=1
        )

    def deep(value):
        high, low = split(value)
        return jnp.concatenate([high, low, high], axis=0)

    summed = [summed_tail(at) for at in range(3)]
    own_tail, new_tail = stack(tails, 0), stack(tails, 3)

    def pairs(share, tail, with_own):
        mask_part, dual_part = (-0.125 * share) * tail, (0.25 * share) * tail
        if with_own:
            mask_part = mask_part - 0.125 * own_tail - 0.25 * new_tail
            dual_part = dual_part - 0.25 * own_tail
        return deep(jnp.concatenate([mask_part, dual_part], axis=1))

    up_share, low_share = share_of(row > 0), share_of(row < rows - 1)
    inner_rhs = pairs(1.0, summed[0], True)
    copies = []
    for at, begin in enumerate(range(0, size, INTERSECTION)):
        end = begin + INTERSECTION
        mask, dual = mask_ref[begin:end, :], dual_ref[begin:end, :]
        table = final_ref[begin:end, :]
        if begin == 0:
            products = dot(table, pairs(up_share, summed[0], True)) + dot(
                final_edge_ref[:INTERSECTION, :], pairs(up_share, summed[1], False)
            )
        elif end == size:
            products = dot(table, pairs(low_share, summed[0], True)) + dot(
                final_edge_ref[INTERSECTION:, :], pairs(low_share, summed[2], False)
            )
        else:
            products = dot(table, inner_rhs)
        if begin == 0 or end == size:
            out = 0 if begin == 0 else INTERSECTION
            ends1, ends2 = corner1_ref[out : out + INTERSECTION, :], corner2_ref[out : out + INTERSECTION, :]
        else:
            out = begin - INTERSECTION
            ends1, ends2 = middle1_ref[out : out + INTERSECTION, :], middle2_ref[out : out + INTERSECTION, :]
        left_ends = jnp.where(even_col, ends2, ends1)
        right_ends = jnp.where(even_col, ends1, ends2)

        def joined(value, part):
            cut = slice(part * INTERSECTION, (part + 1) * INTERSECTION)
            return jnp.concatenate(
                [value[:, :INTERSECTION] + left_ends[:, cut], value[:, INTERSECTION:edge], value[:, edge:] + right_ends[:, cut]],
                axis=1,
            )

        first = joined(mask + dual, 0)
        second = joined(mask + 0.25 * dual, 1)
        share = columns
        if begin == 0 or end == size:
            upper = begin == 0
            side1, side2 = (edge2_ref, edge1_ref) if upper else (edge1_ref, edge2_ref)
            share = columns * (up_share if upper else low_share)

            def across(part):
                cut = slice(part * INTERSECTION, (part + 1) * INTERSECTION)
                ends = jnp.where(even_row, side1[cut, :], side2[cut, :])
                deep_cut = slice((part + 2) * INTERSECTION, (part + 3) * INTERSECTION)
                inner = jnp.where(even_row, side1[deep_cut, :], side2[deep_cut, :])
                return jnp.concatenate([ends[:, :INTERSECTION], inner, ends[:, INTERSECTION:]], axis=1)

            first = first + across(0)
            second = second + across(1)
        agreed0 = first * share
        agreed1 = second * share
        dual_out[begin:end, :] = 1.5 * mask + 0.75 * dual - 0.5 * agreed0 - agreed1 + products[:, size:]
        mask_out[begin:end, :] = 0.5 * (agreed0 + agreed1) - 0.375 * dual + products[:, :size]
        for which, (source, target) in enumerate(((mask_out, mask_hbm), (dual_out, dual_hbm))):
            copy = pltpu.make_async_copy(
                source.at[begin:end, :], target.at[begin:end, :], semaphores.at[which, at]
            )
            copy.start()
            copies.append(copy)
    for copy in copies:
        copy.wait()


VMEM_SPEC = pl.BlockSpec(memory_space=pltpu.VMEM)
HBM_SPEC = pl.BlockSpec(memory_space=pltpu.HBM)


def call(kernel, outs, operands, flops, name, in_specs=None, out_spec=VMEM_SPEC, scratch=(), limit=VMEM_LIMIT):
    return pl.pallas_call(
        kernel,
        out_shape=[jax.ShapeDtypeStruct(shape, dtype) for shape, dtype in outs],
        in_specs=in_specs or [VMEM_SPEC] * len(operands),
        out_specs=[out_spec] * len(outs),
        scratch_shapes=list(scratch),
        compiler_params=pltpu.CompilerParams(vmem_limit_bytes=limit),
        cost_estimate=pl.CostEstimate(flops=flops, bytes_accessed=1 << 20, transcendentals=0),
        name=name,
    )(*operands)


def swaps(total):
    cols = GRID_COLS
    sets = [[], [], [], []]
    for index in range(total):
        row, col = index // cols, index % cols
        if col + 1 < cols:
            sets[col % 2] += [(index, index + 1), (index + 1, index)]
        if index + cols < total:
            sets[2 + row % 2] += [(index, index + cols), (index + cols, index)]
    return sets


def per_device(mask_init, dual_init, target, kernels, weights):
    mask, dual, goal = mask_init[0], dual_init[0], target[0]
    size = mask.shape[0]
    count = kernels.shape[0]
    band = math.isqrt(kernels.shape[2])
    width = 4 * band
    total = lax.axis_size("ty")
    row_pairs1, row_pairs2, col_pairs1, col_pairs2 = swaps(total)
    tables = {name: jnp.asarray(table) for name, table in build_tables(size, band).items()}
    core = [tables[name] for name in CORE_TABLES]

    def trade(value, pairs):
        return lax.ppermute(value, "ty", pairs)

    both = 2 * INTERSECTION
    inner = size - both
    block, gate = ((band, width), F32), ((count * band, width), F32)
    stack, message = ((4 * band, width), F32), ((both + 2 * band, both), F32)
    side, line = ((inner, both), F32), ((both, inner), F32)
    operands = [weights, mask, dual, kernels, goal] + [tables[name] for name in OPEN_TABLES]
    operands = [pltpu.with_memory_space_constraint(value, pltpu.HBM) for value in operands]
    before, after = [mask, dual, tables["quad"], tables["rows"], kernels], core + [goal]
    base, gates, own, corner1, corner2, middle1, middle2, line1, line2, edges = call(
        functools.partial(open_kernel, total),
        [block, gate, stack, message, message, side, side, line, line, ((2, both, both), F32)],
        operands,
        4 * 10**9,
        "open",
        in_specs=[HBM_SPEC] * len(operands),
        scratch=[pltpu.VMEM(value.shape, value.dtype) for value in before]
        + [pltpu.SMEM(weights.shape, weights.dtype)]
        + [pltpu.VMEM(value.shape, value.dtype) for value in after]
        + [
            pltpu.SemaphoreType.DMA((2, size // INTERSECTION)),
            pltpu.SemaphoreType.DMA((len(before) + len(after) - 1,)),
        ],
    )
    corners2, corners1 = trade(corner2, row_pairs2), trade(corner1, row_pairs1)
    long_message = ((2 * both + 2 * band, both), F32)
    keep, edge1, edge2 = call(
        functools.partial(middle_kernel, total),
        [block, long_message, long_message],
        [own, corners1, corners2, edges, line1, line2],
        10**7,
        "middle",
    )
    edges1, edges2 = trade(edge1, col_pairs1), trade(edge2, col_pairs2)
    middles2, middles1 = trade(middle2, row_pairs2), trade(middle1, row_pairs1)
    part, gates = call(
        prepare_kernel,
        [block, gate],
        [base, keep, own, tables["mirror_lanes"], tables["mirror_rows"], gates],
        10**8,
        "prepare",
    )
    (adjoint1,) = call(
        second_kernel,
        [block],
        [part, edges1, edges2, gates, goal] + core,
        3 * 10**9,
        "second",
    )
    whole = ((size, size), F32)
    mask, dual = call(
        functools.partial(last_kernel, total),
        [whole, whole],
        [mask, dual, corners1, corners2, middles1, middles2, edges1, edges2, own, adjoint1]
        + [tables["tail"], tables["final"], tables["final_edge"]],
        2 * 10**9,
        "last",
        out_spec=HBM_SPEC,
        scratch=[
            pltpu.VMEM((size, size), F32),
            pltpu.VMEM((size, size), F32),
            pltpu.SemaphoreType.DMA((2, size // INTERSECTION)),
        ],
    )
    return (mask[None], dual[None])


def solution(mesh):
    tiles = P(("region", "ty"), None, None)
    return jax.shard_map(
        per_device,
        mesh=mesh,
        in_specs=(tiles, tiles, tiles, P(), P()),
        out_specs=(tiles, tiles),
        check_vma=False,
    )
```

```python
import functools
import math

import jax
import jax.numpy as jnp
import ml_dtypes
import numpy as np
from jax import lax
from jax.experimental import pallas as pl
from jax.experimental.pallas import tpu as pltpu
from jax.sharding import PartitionSpec as P

INTERSECTION = 128
GRID_COLS = 4
SETS = 2
SHARPNESS = 8.0
THRESHOLD = 0.3
F32 = jnp.float32
BF16 = jnp.bfloat16
VMEM_LIMIT = 32 * 1024 * 1024


def halves(table):
    high = table.astype(ml_dtypes.bfloat16)
    low = (table - high.astype(np.float64)).astype(ml_dtypes.bfloat16)
    return high, low


def build_tables(size, band):
    coarse = 2 * band
    stride = size // coarse
    edge = size - INTERSECTION
    frequencies = np.arange(band) - band // 2
    angles = 2.0 * np.pi * ((frequencies[:, None] * np.arange(size)[None, :]) % size) / size
    cos, sin = np.cos(angles), -np.sin(angles)
    order = np.arange(band).reshape(-1, 128 // band).T.reshape(-1)
    rows = np.concatenate([cos[order], sin[order]], axis=0)
    quad = np.concatenate([cos.T, sin.T, -sin.T, cos.T], axis=1)
    dc, ds = cos[:, ::stride], sin[:, ::stride]
    dc_rows, ds_rows = dc[order], ds[order]
    wide = np.arange(-(band - 1), band)
    gaps = np.arange(size)[:, None] - stride * np.arange(coarse)[None, :]
    lift = np.cos(2.0 * np.pi * wide[:, None, None] * gaps[None] / size).sum(0) / coarse

    tables = {}
    tables["quad"] = halves(quad)[0]
    high, low = halves(rows)
    tables["rows"] = np.concatenate([high, low], axis=0)
    spread = np.concatenate(
        [np.concatenate([dc, -ds, -ds, -dc], axis=1), np.concatenate([ds, dc, dc, -ds], axis=1)], axis=0
    )
    high, low = halves(np.concatenate([spread, spread], axis=0))
    tables["spread"] = np.concatenate([high, high, low], axis=0)
    high, low = halves(np.concatenate([dc_rows.T, ds_rows.T], axis=1))
    tables["field"] = np.concatenate([high, high, low], axis=1)
    high, low = halves(np.concatenate([lift.T, lift.T], axis=0))
    tables["lift_cols"] = np.concatenate([high, low], axis=0)
    high, low = halves(lift * (0.5 * SHARPNESS))
    tables["lift_rows"] = np.concatenate([high, high, low], axis=1)
    high, low = halves(lift)
    tables["drop_cols"] = np.concatenate([high, high, low, low], axis=1)
    high, low = halves(lift.T * (0.25 * SHARPNESS))
    tables["drop_rows"] = np.concatenate([high, low], axis=0)
    high, low = halves(np.concatenate([dc_rows, ds_rows], axis=0))
    tables["turn"] = np.concatenate([high, high, low], axis=1)
    back_real = np.concatenate([dc.T, -ds.T, -ds.T, -dc.T], axis=0)
    back_imag = np.concatenate([ds.T, dc.T, dc.T, -ds.T], axis=0)
    high, low = halves(np.concatenate([back_real, back_imag, back_imag, -back_real], axis=1))
    tables["back"] = np.concatenate([high, low], axis=1)
    flip = np.zeros((band, band))
    for place in range(1, band):
        flip[place, band - place] = 1.0
    eye, zero = np.eye(band), np.zeros((band, band))
    own = np.concatenate(
        [
            np.concatenate([eye, zero, zero, eye], axis=1),
            np.concatenate([zero, eye, -eye, zero], axis=1),
        ],
        axis=0,
    )
    turned = np.concatenate(
        [
            np.concatenate([flip, zero, zero, flip], axis=1),
            np.concatenate([zero, -flip, flip, zero], axis=1),
        ],
        axis=0,
    )
    tables["mirror_lanes"] = np.concatenate(
        [np.concatenate([own, own], axis=0), np.concatenate([turned, turned], axis=0)], axis=1
    ).astype(ml_dtypes.bfloat16)
    tables["mirror_rows"] = flip[order][:, order].astype(ml_dtypes.bfloat16)
    tail = np.concatenate([np.concatenate([cos, -sin], axis=1), np.concatenate([sin, cos], axis=1)], axis=0)
    high, low = halves(tail)
    tables["tail"] = np.concatenate([high, high, low, np.zeros_like(low)], axis=0)
    high, low = halves(rows.T)
    tables["final"] = np.concatenate([high, high, low], axis=1)
    near, far = rows[:, :INTERSECTION], rows[:, edge:]
    high, low = halves(np.concatenate([far.T, near.T], axis=0))
    tables["final_edge"] = np.concatenate([high, high, low], axis=1)
    return tables


def dot(left, right):
    return lax.dot_general(left, right, (((1,), (0,)), ((), ())), preferred_element_type=F32)


def split(value):
    high = value.astype(BF16)
    return high, (value - high.astype(F32)).astype(BF16)


def place(total):
    index = lax.axis_index("ty")
    row, col = index // GRID_COLS, index % GRID_COLS
    return row, col, total // GRID_COLS


def share_of(present):
    return jnp.where(present, 0.5, 1.0).astype(F32)


def edge_scale(shape, dim, size, before, after):
    steps = lax.broadcasted_iota(jnp.int32, shape, dim)
    first = jnp.where(steps < INTERSECTION, share_of(before), 1.0)
    return first * jnp.where(steps >= size - INTERSECTION, share_of(after), 1.0)


def quad_form(value):
    half = value.shape[0] // 2
    width = value.shape[1]
    lanes = lax.broadcasted_iota(jnp.int32, (half, width), 1)
    rolled = pltpu.roll(value[half:], width // 2, 1)
    return value[:half] + jnp.where(lanes < width // 2, rolled, -rolled)


def row_transform(table, value):
    half = table.shape[0] // 2
    both = dot(table, value.astype(BF16))
    return both[:half] + both[half:]


def gates_of(kernels_ref, weights_ref, band):
    count, parts, length = kernels_ref.shape
    lanes = 128
    groups = lanes // band
    chunks = length // lanes
    total = weights_ref[0]
    for k in range(1, count):
        total = total + weights_ref[k]
    group = lax.broadcasted_iota(jnp.int32, (chunks, lanes), 1) // band
    blocks = []
    for k in range(count):
        gain = jnp.sqrt(jnp.full((chunks, lanes), weights_ref[k], F32) / total)
        real, imag = [
            gain
            * jnp.concatenate(
                [kernels_ref[k, part : part + 1, c * lanes : (c + 1) * lanes] for c in range(chunks)], axis=0
            )
            for part in range(2)
        ]
        reals = [pltpu.roll(real, band * g, 1) if g else real for g in range(groups)]
        imags = [pltpu.roll(imag, band * g, 1) if g else imag for g in range(groups)]
        for at in range(groups):
            line = imags[(3 - at) % groups]
            line = jnp.where(group == 2, imags[(2 - at) % groups], line)
            line = jnp.where(group == 1, reals[(1 - at) % groups], line)
            blocks.append(jnp.where(group == 0, reals[-at % groups], line))
    return jnp.concatenate(blocks, axis=0)


def adjoint_of(spectrum, gates, target_ref, tables):
    band = spectrum.shape[0]
    width = 4 * band
    kernels = gates.shape[0] // band
    size = target_ref.shape[0]
    scaled = spectrum * (1.0 / (size * size))
    high, low = split(gates * jnp.concatenate([scaled] * kernels, axis=0))
    bands = dot(jnp.concatenate([high, low, high], axis=1), tables["spread"][...])
    stacked = jnp.concatenate(
        [
            jnp.concatenate([bands[band * k : band * (k + 1), :width] for k in range(kernels)], axis=1),
            jnp.concatenate([bands[band * k : band * (k + 1), width:] for k in range(kernels)], axis=1),
        ],
        axis=0,
    )
    high, low = split(stacked)
    fields = dot(tables["field"][...], jnp.concatenate([high, low, high], axis=0))
    squares = fields * fields
    power = squares[:, :width]
    for k in range(1, kernels):
        power = power + squares[:, k * width : (k + 1) * width]
    high, low = split(power)
    lifted = dot(high, tables["lift_cols"][:width, :]) + dot(
        jnp.concatenate([low, high], axis=1), tables["lift_cols"][...]
    )
    high, low = split(lifted)
    deep = jnp.concatenate([high, low, high], axis=0)
    narrowed = []
    step = size // 2
    for begin in range(0, size, step):
        lines = slice(begin, begin + step)
        curve = jnp.tanh(dot(tables["lift_rows"][lines, :], deep) - 0.5 * SHARPNESS * THRESHOLD)
        slope = (1.0 + curve - 2.0 * target_ref[lines, :].astype(F32)) * (1.0 - curve * curve)
        both = dot(slope.astype(BF16), tables["drop_cols"][...])
        narrowed.append((both[:, :width] + both[:, width:]).astype(BF16))
    dropped = row_transform(tables["drop_rows"][...], jnp.concatenate(narrowed, axis=0))
    weighted = fields * jnp.concatenate([dropped] * kernels, axis=1)
    high, low = split(weighted)
    turned = dot(tables["turn"][...], jnp.concatenate([high, low, high], axis=0))
    across = jnp.concatenate(
        [
            jnp.concatenate([turned[:band, k * width : (k + 1) * width] for k in range(kernels)], axis=0),
            jnp.concatenate([turned[band:, k * width : (k + 1) * width] for k in range(kernels)], axis=0),
        ],
        axis=1,
    )
    both = dot(across.astype(BF16), tables["back"][...])
    product = gates * (both[:, :width] + both[:, width:])
    adjoint = product[:band]
    for k in range(1, kernels):
        adjoint = adjoint + product[k * band : (k + 1) * band]
    return adjoint + pltpu.roll(adjoint, width // 2, 1)


CORE_TABLES = ("spread", "field", "lift_cols", "lift_rows", "drop_cols", "drop_rows", "turn", "back")
OPEN_TABLES = ("quad", "rows") + CORE_TABLES


def open_kernel(total, weights_hbm, mask_hbm, dual_hbm, kernels_hbm, target_hbm, *rest):
    count = len(OPEN_TABLES)
    tables_hbm, rest = rest[:count], rest[count:]
    outs, rest = rest[:8], rest[8:]
    base_ref, gates_ref, own_ref, corner1, corner2, middle2, lines_ref, edges_ref = outs
    sources = [*tables_hbm[:2], kernels_hbm, weights_hbm, *tables_hbm[2:], target_hbm]
    mask_ref, dual_ref = rest[:2]
    staged, (line_semaphores, semaphores) = rest[2:-2], rest[-2:]
    size = mask_ref.shape[0]
    pieces = size // INTERSECTION
    edge = size - INTERSECTION

    def cut(at):
        return slice(at * INTERSECTION, (at + 1) * INTERSECTION)

    copies = [
        pltpu.make_async_copy(source, target, semaphores.at[at])
        for at, (source, target) in enumerate(zip(sources, staged))
    ]
    parts = [
        [
            pltpu.make_async_copy(source.at[cut(at), :], target.at[cut(at), :], line_semaphores.at[which, at])
            for which, (source, target) in enumerate(((mask_hbm, mask_ref), (dual_hbm, dual_ref)))
        ]
        for at in range(pieces)
    ]
    for copy in (copies[2], copies[3], copies[0]):
        copy.start()
    for pair in parts:
        for copy in pair:
            copy.start()
    for copy in [copies[1]] + copies[4:]:
        copy.start()
    quad_ref, rows_ref, kernels_ref, weights_ref, *core_refs, target_ref = staged
    band = base_ref.shape[0]
    width = 4 * band
    row, col, rows = place(total)
    even_col = col % 2 == 0

    copies[2].wait()
    copies[3].wait()
    gates = gates_of(kernels_ref, weights_ref, band)
    gates_ref[...] = gates

    copies[0].wait()
    quad = quad_ref[...]
    scaled = quad * edge_scale((size, 1), 0, size, col > 0, col < GRID_COLS - 1).astype(BF16)
    pair = jnp.concatenate([quad, scaled], axis=1)
    mask_parts, dual_parts, lefts, rights = [], [], [], []
    for at in range(pieces):
        for copy in parts[at]:
            copy.wait()
        mask, dual = mask_ref[cut(at), :], dual_ref[cut(at), :]
        mask_parts.append(dot(mask.astype(BF16), pair))
        dual_parts.append(dot(dual.astype(BF16), pair))
        ends = [0.5 * (mask[:, lanes] + dual[:, lanes]) for lanes in (slice(0, INTERSECTION), slice(edge, size))]
        lefts.append(dot(ends[0].astype(BF16), quad[edge:]))
        rights.append(dot(ends[1].astype(BF16), quad[:INTERSECTION]))

    for copy in [copies[1]] + copies[4:]:
        copy.wait()
    lines = rows_ref[...]

    def block(value, at):
        return quad_form(value[:, at * width : (at + 1) * width])

    spectrum = block(row_transform(lines, jnp.concatenate([part[:, :width] for part in mask_parts], axis=0)), 0)
    dual_spectrum = block(row_transform(lines, jnp.concatenate([part[:, :width] for part in dual_parts], axis=0)), 0)
    base_ref[...] = 0.5 * spectrum - 0.25 * dual_spectrum
    line_scale = edge_scale((1, size), 1, size, row > 0, row < rows - 1).astype(BF16)
    outer = jnp.concatenate(
        [
            jnp.concatenate([a[:, width:] + b[:, width:] for a, b in zip(mask_parts, dual_parts)], axis=0),
            jnp.concatenate(lefts, axis=0),
            jnp.concatenate(rights, axis=0),
        ],
        axis=1,
    ).astype(BF16)
    around = row_transform(lines * line_scale, outer)
    upper = 0.5 * row_transform(lines[:, edge:], outer[:INTERSECTION])
    lower = 0.5 * row_transform(lines[:, :INTERSECTION], outer[edge:])

    adjoint = adjoint_of(spectrum, gates, target_ref, dict(zip(CORE_TABLES, core_refs)))
    strips = {}
    for at in range(pieces):
        mask, dual = mask_ref[cut(at), :], dual_ref[cut(at), :]
        first, second = mask + dual, mask + 0.25 * dual
        near = jnp.concatenate([first[:, :INTERSECTION], second[:, :INTERSECTION]], axis=1)
        far = jnp.concatenate([first[:, edge:], second[:, edge:]], axis=1)
        to1, to2 = jnp.where(even_col, far, near), jnp.where(even_col, near, far)
        if at == 0 or at == pieces - 1:
            out = cut(0 if at == 0 else 1)
            corner1[out, :], corner2[out, :] = to1, to2
            strips[at] = (first, second)
        else:
            begin = 2 * INTERSECTION + band + (at - 1) * INTERSECTION
            corner1[begin : begin + INTERSECTION, :] = to1
            middle2[cut(at - 1), :] = to2
    for part, lines_at in enumerate((cut(0), cut(1))):
        above, below = strips[0][part], strips[pieces - 1][part]
        for at, strip in enumerate((above, below)):
            edges_ref[at, lines_at, :] = jnp.concatenate([strip[:, :INTERSECTION], strip[:, edge:]], axis=1)
            lines_ref[at, lines_at, :] = strip[:, INTERSECTION:edge]

    own_ref[...] = jnp.concatenate([block(around, 0), block(upper, 0), block(lower, 0), adjoint], axis=0)
    left = [block(around, 1), block(upper, 1), block(lower, 1)]
    right = [block(around, 2), block(upper, 2), block(lower, 2)]
    tail = slice(2 * INTERSECTION, 2 * INTERSECTION + band)
    for ref, first, second in ((corner1, right, left), (corner2, left, right)):
        ref[tail, :] = pack([jnp.where(even_col, a, b) for a, b in zip(first, second)] + [adjoint])


def pack(blocks):
    lanes = lax.broadcasted_iota(jnp.int32, blocks[0].shape, 1)
    half = blocks[0].shape[1] // 2
    pairs = [jnp.where(lanes < half, a, pltpu.roll(b, half, 1)) for a, b in (blocks[:2], blocks[2:])]
    return jnp.concatenate(pairs, axis=1)


def unpack(tail):
    width = tail.shape[1] // 2
    first, second = tail[:, :width], tail[:, width:]
    return first, pltpu.roll(first, width // 2, 1), second, pltpu.roll(second, width // 2, 1)


def whole_adjoint(value):
    half = value.shape[1] // 2
    lanes = lax.broadcasted_iota(jnp.int32, value.shape, 1)
    return jnp.where(lanes < half, value, pltpu.roll(value, half, 1))


def whole_spectrum(value):
    band = value.shape[1] // 4
    lanes = lax.broadcasted_iota(jnp.int32, value.shape, 1)
    right = jnp.where(lanes < 3 * band, -pltpu.roll(value, band, 1), pltpu.roll(value, 3 * band, 1))
    return jnp.where(lanes < 2 * band, value, right)


def middle_kernel(total, own_ref, got1_ref, got2_ref, edges_ref, lines_ref, keep_ref, *sends):
    band = keep_ref.shape[0]
    row, col, rows = place(total)
    even_col = col % 2 == 0
    cut = INTERSECTION
    one, two = [unpack(ref[2 * cut : 2 * cut + band, :]) for ref in (got1_ref, got2_ref)]
    mine = [own_ref[at * band : (at + 1) * band, :] for at in range(4)]
    keep, upper, lower = [mine[at] + one[at] + two[at] for at in range(3)]
    keep_ref[...] = keep
    summed = []
    for at in range(2):
        lines = slice(at * cut, (at + 1) * cut)
        first, second = got1_ref[lines, :], got2_ref[lines, :]
        left, right = jnp.where(even_col, second, first), jnp.where(even_col, first, second)
        summed.append(
            edges_ref[at]
            + jnp.concatenate(
                [
                    jnp.concatenate([left[:, :cut], right[:, :cut]], axis=1),
                    jnp.concatenate([left[:, cut:], right[:, cut:]], axis=1),
                ],
                axis=0,
            )
        )
    tails = [pack([value, mine[3], one[3], two[3]]) for value in (upper, lower)]
    for at, ref in enumerate(sends):
        down = row % SETS == at
        ref[: 2 * cut, :] = jnp.where(down, summed[1], summed[0])
        ref[2 * cut : 4 * cut, :] = jnp.where(down, lines_ref[1], lines_ref[0])
        ref[4 * cut :, :] = jnp.where(down, tails[1], tails[0])


def from_rows(row, refs, lines):
    got = [ref[lines, :] for ref in refs]
    even = row % SETS == 0
    return jnp.where(even, got[1], got[0]), jnp.where(even, got[0], got[1])


def tails_of(blocks, table):
    size = table.shape[1] // 2
    width = blocks.shape[1]
    lanes = lax.broadcasted_iota(jnp.int32, (1, width), 1)
    high, low = split(blocks)
    pair = jnp.where(lanes < width // 2, high, low)
    return dot(jnp.concatenate([pair, high], axis=1), table)


def columns_of(table, begin, end):
    size = table.shape[1] // 2
    return jnp.concatenate([table[:, begin:end], table[:, size + begin : size + end]], axis=1)


def stack_of(value, at, band):
    wide = value.shape[1] // 2
    lines = value[at * band : (at + 1) * band]
    return jnp.concatenate([lines[:, :wide], lines[:, wide:]], axis=0)


def widen(value, left, right, edge):
    return jnp.concatenate(
        [value[:, :INTERSECTION] + left, value[:, INTERSECTION:edge], value[:, edge:] + right], axis=1
    )


def deep(value):
    high, low = split(value)
    return jnp.concatenate([high, low, high], axis=0)


def prepare_kernel(total, base_ref, keep_ref, own_ref, lanes_ref, flip_ref, gates_ref, mask_ref, dual_ref, corner1_ref, corner2_ref, tail_ref, final_ref, out_ref, gates_out, mask_out, dual_out):
    band = base_ref.shape[0]
    size = mask_ref.shape[0]
    edge = size - INTERSECTION
    adjoint = own_ref[3 * band :, :]
    width = adjoint.shape[1]
    high, low = split(adjoint)
    lanes = lax.broadcasted_iota(jnp.int32, adjoint.shape, 1)
    mirrored = dot(jnp.where(lanes < width // 2, high, low), lanes_ref[...])
    high, low = split(mirrored[:, width:])
    flip = flip_ref[...]
    gradient_band = mirrored[:, :width] + dot(flip, high) + dot(flip, low)
    out_ref[...] = base_ref[...] + 0.5 * keep_ref[...] - 0.25 * gradient_band
    gates_out[...] = gates_ref[...]

    row, col, rows = place(total)
    even_col = col % 2 == 0
    scale = 2.0 / (size * size)
    tail_table = tail_ref[...]
    first, second = [
        whole_adjoint(unpack(ref[2 * INTERSECTION : 2 * INTERSECTION + band, :])[3]) for ref in (corner1_ref, corner2_ref)
    ]
    left, right = jnp.where(even_col, second, first), jnp.where(even_col, first, second)
    own_tail = stack_of(tails_of(adjoint * scale, tail_table), 0, band)
    left_tail = stack_of(tails_of(left * scale, columns_of(tail_table, edge, size)), 0, band)
    right_tail = stack_of(tails_of(right * scale, columns_of(tail_table, 0, INTERSECTION)), 0, band)
    columns = edge_scale((1, size), 1, size, col > 0, col < GRID_COLS - 1)
    summed = columns * widen(own_tail, left_tail, right_tail, edge)
    for begin in range(0, size, INTERSECTION):
        end = begin + INTERSECTION
        share = jnp.asarray(1.0, F32)
        if begin == 0:
            share = share_of(row > 0)
        if end == size:
            share = share_of(row < rows - 1)
        if begin < 2 * INTERSECTION or end == size:
            rhs = deep(
                jnp.concatenate(
                    [(-0.125 * share) * summed - 0.125 * own_tail, (0.25 * share) * summed - 0.25 * own_tail], axis=1
                )
            )
        products = dot(final_ref[begin:end, :], rhs)
        mask, dual = mask_ref[begin:end, :], dual_ref[begin:end, :]
        agreed0, agreed1 = mask + dual, mask + 0.25 * dual
        if begin == 0 or end == size:
            out = slice(0, INTERSECTION) if begin == 0 else slice(INTERSECTION, 2 * INTERSECTION)
            ends1, ends2 = corner1_ref[out, :], corner2_ref[out, :]
            lefts, rights = jnp.where(even_col, ends2, ends1), jnp.where(even_col, ends1, ends2)
            agreed0 = widen(agreed0, lefts[:, :INTERSECTION], rights[:, :INTERSECTION], edge)
            agreed1 = widen(agreed1, lefts[:, INTERSECTION:], rights[:, INTERSECTION:], edge)
        weight = columns * share
        agreed0, agreed1 = agreed0 * weight, agreed1 * weight
        mask_out[begin:end, :] = 0.5 * (agreed0 + agreed1) - 0.375 * dual + products[:, :size]
        dual_out[begin:end, :] = 1.5 * mask + 0.75 * dual - 0.5 * agreed0 - agreed1 + products[:, size:]


def second_kernel(part_ref, got1_ref, got2_ref, gates_ref, target_ref, *rest):
    tables = dict(zip(CORE_TABLES, rest))
    out_ref = rest[len(CORE_TABLES)]
    got = [ref[4 * INTERSECTION :, : part_ref.shape[1]] for ref in (got1_ref, got2_ref)]
    spectrum = whole_spectrum(part_ref[...] + 0.5 * (got[0] + got[1]))
    out_ref[...] = adjoint_of(spectrum, gates_ref[...], target_ref, tables)


def last_kernel(total, mask_ref, dual_ref, corner1_ref, middle2_ref, edge1_ref, edge2_ref, adjoint_ref, tail_ref, final_ref, final_edge_ref, mask_hbm, dual_hbm, mask_out, dual_out, semaphores):
    size = mask_ref.shape[0]
    band, width = adjoint_ref.shape
    edge = size - INTERSECTION
    row, col, rows = place(total)
    even_col = col % 2 == 0
    scale = 2.0 / (size * size)
    tail_table = tail_ref[...]
    columns = edge_scale((1, size), 1, size, col > 0, col < GRID_COLS - 1)
    copies = []

    def store(begin, mask, dual):
        lines = slice(begin, begin + INTERSECTION)
        for which, (value, source, target) in enumerate(((mask, mask_out, mask_hbm), (dual, dual_out, dual_hbm))):
            source[lines, :] = value
            copy = pltpu.make_async_copy(
                source.at[lines, :], target.at[lines, :], semaphores.at[which, begin // INTERSECTION]
            )
            copy.start()
            copies.append(copy)

    new_rhs = deep(stack_of(tails_of(adjoint_ref[...] * (-0.25 * scale), tail_table), 0, band))
    left_share, right_share = share_of(col > 0), share_of(col < GRID_COLS - 1)
    for begin in range(INTERSECTION, edge, INTERSECTION):
        lines = slice(begin, begin + INTERSECTION)
        out = slice(begin - INTERSECTION, begin)
        along = begin + INTERSECTION + band
        ends1, ends2 = corner1_ref[along : along + INTERSECTION, :], middle2_ref[out, :]
        left = left_share * jnp.where(even_col, ends2, ends1)
        right = right_share * jnp.where(even_col, ends1, ends2)
        left0, left1, right0, right1 = [
            value[:, cut] for value in (left, right) for cut in (slice(0, INTERSECTION), slice(INTERSECTION, None))
        ]
        mask = mask_ref[lines, :] + dot(final_ref[lines, :], new_rhs)
        store(
            begin,
            widen(mask, 0.5 * (left0 + left1), 0.5 * (right0 + right1), edge),
            widen(dual_ref[lines, :], -0.5 * left0 - left1, -0.5 * right0 - right1, edge),
        )

    refs = (edge1_ref, edge2_ref)
    blocks = [unpack(value)[1:] for value in from_rows(row, refs, slice(4 * INTERSECTION, None))]
    columns_at = [whole_adjoint(jnp.concatenate([a, b], axis=0)) * scale for a, b in zip(*blocks)]
    left = jnp.where(even_col, columns_at[2], columns_at[1])
    right = jnp.where(even_col, columns_at[1], columns_at[2])
    tails = tails_of(columns_at[0], tail_table)
    left_tails = tails_of(left, columns_of(tail_table, edge, size))
    right_tails = tails_of(right, columns_of(tail_table, 0, INTERSECTION))
    inner = slice(INTERSECTION, edge)
    for at, begin in enumerate((0, edge)):
        lines = slice(begin, begin + INTERSECTION)
        share = share_of(row > 0) if at == 0 else share_of(row < rows - 1)
        summed = (columns * share) * widen(
            stack_of(tails, at, band), stack_of(left_tails, at, band), stack_of(right_tails, at, band), edge
        )
        rhs = deep(jnp.concatenate([-0.125 * summed, 0.25 * summed], axis=1))
        products = dot(final_edge_ref[at * INTERSECTION : (at + 1) * INTERSECTION, :], rhs)

        def across(part):
            cut = slice(part * INTERSECTION, (part + 1) * INTERSECTION)
            deep_cut = slice((part + 2) * INTERSECTION, (part + 3) * INTERSECTION)
            ends, middle = from_rows(row, refs, cut)[at], from_rows(row, refs, deep_cut)[at]
            return jnp.concatenate([ends[:, :INTERSECTION], middle, ends[:, INTERSECTION:]], axis=1)

        weight = columns * share
        first, second = across(0) * weight, across(1) * weight
        mask = mask_ref[lines, :] + dot(final_ref[lines, :], new_rhs) + products[:, :size]
        store(begin, mask + 0.5 * (first + second), dual_ref[lines, :] + products[:, size:] - 0.5 * first - second)
    for copy in copies:
        copy.wait()


VMEM_SPEC = pl.BlockSpec(memory_space=pltpu.VMEM)
HBM_SPEC = pl.BlockSpec(memory_space=pltpu.HBM)


def call(kernel, outs, operands, flops, name, in_specs=None, out_spec=VMEM_SPEC, scratch=(), limit=VMEM_LIMIT):
    return pl.pallas_call(
        kernel,
        out_shape=[jax.ShapeDtypeStruct(shape, dtype) for shape, dtype in outs],
        in_specs=in_specs or [VMEM_SPEC] * len(operands),
        out_specs=[out_spec] * len(outs),
        scratch_shapes=list(scratch),
        compiler_params=pltpu.CompilerParams(vmem_limit_bytes=limit),
        cost_estimate=pl.CostEstimate(flops=flops, bytes_accessed=1 << 20, transcendentals=0),
        name=name,
    )(*operands)


def swaps(total):
    cols = GRID_COLS
    along, across = [[], []], [[] for _ in range(SETS)]
    for index in range(total):
        row, col = index // cols, index % cols
        if col + 1 < cols:
            along[col % 2] += [(index, index + 1), (index + 1, index)]
        if index + cols < total:
            across[row % SETS] += [(index, index + cols), (index + cols, index)]
    return along, across


def per_device(mask_init, dual_init, target, kernels, weights):
    mask, dual, goal = mask_init[0], dual_init[0], target[0]
    size = mask.shape[0]
    count = kernels.shape[0]
    band = math.isqrt(kernels.shape[2])
    width = 4 * band
    total = lax.axis_size("ty")
    (row_pairs1, row_pairs2), col_pairs = swaps(total)
    tables = {name: jnp.asarray(table) for name, table in build_tables(size, band).items()}
    core = [tables[name] for name in CORE_TABLES]

    def trade(value, pairs):
        return lax.ppermute(value, "ty", pairs)

    both = 2 * INTERSECTION
    inner = size - both
    block, gate = ((band, width), F32), ((count * band, width), F32)
    stack, message = ((4 * band, width), F32), ((both + band, both), F32)
    side, lines = ((inner, both), F32), ((2, both, inner), F32)
    long_message = ((2 * both + band, both), F32)
    operands = [weights, mask, dual, kernels, goal] + [tables[name] for name in OPEN_TABLES]
    operands = [pltpu.with_memory_space_constraint(value, pltpu.HBM) for value in operands]
    before, after = [mask, dual, tables["quad"], tables["rows"], kernels], core + [goal]
    base, gates, own, corner1, corner2, middle2, line_ends, edges = call(
        functools.partial(open_kernel, total),
        [block, gate, stack, long_message, message, side, lines, ((2, both, both), F32)],
        operands,
        4 * 10**9,
        "open",
        in_specs=[HBM_SPEC] * len(operands),
        scratch=[pltpu.VMEM(value.shape, value.dtype) for value in before]
        + [pltpu.SMEM(weights.shape, weights.dtype)]
        + [pltpu.VMEM(value.shape, value.dtype) for value in after]
        + [
            pltpu.SemaphoreType.DMA((2, size // INTERSECTION)),
            pltpu.SemaphoreType.DMA((len(before) + len(after) - 1,)),
        ],
    )
    corners2, corners1 = trade(corner2, row_pairs2), trade(corner1, row_pairs1)
    keep, *sends = call(
        functools.partial(middle_kernel, total),
        [block] + [long_message] * SETS,
        [own, corners1, corners2, edges, line_ends],
        10**7,
        "middle",
    )
    gots = [trade(value, pairs) for value, pairs in zip(sends, col_pairs)]
    middles2 = trade(middle2, row_pairs2)
    whole = ((size, size), F32)
    part, gates, mask, dual = call(
        functools.partial(prepare_kernel, total),
        [block, gate, whole, whole],
        [base, keep, own, tables["mirror_lanes"], tables["mirror_rows"], gates, mask, dual, corners1, corners2]
        + [tables["tail"], tables["final"]],
        10**9,
        "prepare",
    )
    (adjoint1,) = call(
        second_kernel,
        [block],
        [part, *gots, gates, goal] + core,
        3 * 10**9,
        "second",
    )
    mask, dual = call(
        functools.partial(last_kernel, total),
        [whole, whole],
        [mask, dual, corners1, middles2, *gots, adjoint1]
        + [tables["tail"], tables["final"], tables["final_edge"]],
        2 * 10**9,
        "last",
        out_spec=HBM_SPEC,
        scratch=[
            pltpu.VMEM((size, size), F32),
            pltpu.VMEM((size, size), F32),
            pltpu.SemaphoreType.DMA((2, size // INTERSECTION)),
        ],
    )
    return (mask[None], dual[None])


def solution(mesh):
    tiles = P(("region", "ty"), None, None)
    return jax.shard_map(
        per_device,
        mesh=mesh,
        in_specs=(tiles, tiles, tiles, P(), P()),
        out_specs=(tiles, tiles),
        check_vma=False,
    )
```

```python
import functools
import math

import jax
import jax.numpy as jnp
import ml_dtypes
import numpy as np
from jax import lax
from jax.experimental import pallas as pl
from jax.experimental.pallas import tpu as pltpu
from jax.sharding import PartitionSpec as P

INTERSECTION = 128
GRID_COLS = 4
SETS = 2
SHARPNESS = 8.0
THRESHOLD = 0.3
F32 = jnp.float32
BF16 = jnp.bfloat16
VMEM_LIMIT = 32 * 1024 * 1024


def halves(table):
    high = table.astype(ml_dtypes.bfloat16)
    low = (table - high.astype(np.float64)).astype(ml_dtypes.bfloat16)
    return high, low


def build_tables(size, band):
    coarse = 2 * band
    stride = size // coarse
    edge = size - INTERSECTION
    frequencies = np.arange(band) - band // 2
    angles = 2.0 * np.pi * ((frequencies[:, None] * np.arange(size)[None, :]) % size) / size
    cos, sin = np.cos(angles), -np.sin(angles)
    order = np.arange(band).reshape(-1, 128 // band).T.reshape(-1)
    rows = np.concatenate([cos[order], sin[order]], axis=0)
    quad = np.concatenate([cos.T, sin.T, -sin.T, cos.T], axis=1)
    dc, ds = cos[:, ::stride], sin[:, ::stride]
    dc_rows, ds_rows = dc[order], ds[order]
    wide = np.arange(-(band - 1), band)
    gaps = np.arange(size)[:, None] - stride * np.arange(coarse)[None, :]
    lift = np.cos(2.0 * np.pi * wide[:, None, None] * gaps[None] / size).sum(0) / coarse

    tables = {}
    tables["quad"] = halves(quad)[0]
    high, low = halves(rows)
    tables["rows"] = np.concatenate([high, low], axis=0)
    spread = np.concatenate(
        [np.concatenate([dc, -ds, -ds, -dc], axis=1), np.concatenate([ds, dc, dc, -ds], axis=1)], axis=0
    )
    high, low = halves(np.concatenate([spread, spread], axis=0))
    tables["spread"] = np.concatenate([high, high, low], axis=0)
    high, low = halves(np.concatenate([dc_rows.T, ds_rows.T], axis=1))
    tables["field"] = np.concatenate([high, high, low], axis=1)
    high, low = halves(np.concatenate([lift.T, lift.T], axis=0))
    tables["lift_cols"] = np.concatenate([high, low], axis=0)
    high, low = halves(lift * (0.5 * SHARPNESS))
    tables["lift_rows"] = np.concatenate([high, high, low], axis=1)
    high, low = halves(lift)
    tables["drop_cols"] = np.concatenate([high, high, low, low], axis=1)
    high, low = halves(lift.T * (0.25 * SHARPNESS))
    tables["drop_rows"] = np.concatenate([high, low], axis=0)
    high, low = halves(np.concatenate([dc_rows, ds_rows], axis=0))
    tables["turn"] = np.concatenate([high, high, low], axis=1)
    back_real = np.concatenate([dc.T, -ds.T, -ds.T, -dc.T], axis=0)
    back_imag = np.concatenate([ds.T, dc.T, dc.T, -ds.T], axis=0)
    high, low = halves(np.concatenate([back_real, back_imag, back_imag, -back_real], axis=1))
    tables["back"] = np.concatenate([high, low], axis=1)
    flip = np.zeros((band, band))
    for place in range(1, band):
        flip[place, band - place] = 1.0
    eye, zero = np.eye(band), np.zeros((band, band))
    own = np.concatenate(
        [
            np.concatenate([eye, zero, zero, eye], axis=1),
            np.concatenate([zero, eye, -eye, zero], axis=1),
        ],
        axis=0,
    )
    turned = np.concatenate(
        [
            np.concatenate([flip, zero, zero, flip], axis=1),
            np.concatenate([zero, -flip, flip, zero], axis=1),
        ],
        axis=0,
    )
    tables["mirror_lanes"] = np.concatenate(
        [np.concatenate([own, own], axis=0), np.concatenate([turned, turned], axis=0)], axis=1
    ).astype(ml_dtypes.bfloat16)
    tables["mirror_rows"] = flip[order][:, order].astype(ml_dtypes.bfloat16)
    tail = np.concatenate([np.concatenate([cos, -sin], axis=1), np.concatenate([sin, cos], axis=1)], axis=0)
    high, low = halves(tail)
    tables["tail"] = np.concatenate([high, high, low, np.zeros_like(low)], axis=0)
    high, low = halves(rows.T)
    tables["final"] = np.concatenate([high, high, low], axis=1)
    near, far = rows[:, :INTERSECTION], rows[:, edge:]
    high, low = halves(np.concatenate([far.T, near.T], axis=0))
    tables["final_edge"] = np.concatenate([high, high, low], axis=1)
    return tables


def dot(left, right):
    return lax.dot_general(left, right, (((1,), (0,)), ((), ())), preferred_element_type=F32)


def split(value):
    high = value.astype(BF16)
    return high, (value - high.astype(F32)).astype(BF16)


def place(total):
    index = lax.axis_index("ty")
    row, col = index // GRID_COLS, index % GRID_COLS
    return row, col, total // GRID_COLS


def share_of(present):
    return jnp.where(present, 0.5, 1.0).astype(F32)


def edge_scale(shape, dim, size, before, after):
    steps = lax.broadcasted_iota(jnp.int32, shape, dim)
    first = jnp.where(steps < INTERSECTION, share_of(before), 1.0)
    return first * jnp.where(steps >= size - INTERSECTION, share_of(after), 1.0)


def quad_form(value):
    half = value.shape[0] // 2
    width = value.shape[1]
    lanes = lax.broadcasted_iota(jnp.int32, (half, width), 1)
    rolled = pltpu.roll(value[half:], width // 2, 1)
    return value[:half] + jnp.where(lanes < width // 2, rolled, -rolled)


def row_transform(table, value):
    half = table.shape[0] // 2
    both = dot(table, value.astype(BF16))
    return both[:half] + both[half:]


def gates_of(kernels_ref, weights_ref, band):
    count, parts, length = kernels_ref.shape
    lanes = 128
    groups = lanes // band
    chunks = length // lanes
    total = weights_ref[0]
    for k in range(1, count):
        total = total + weights_ref[k]
    group = lax.broadcasted_iota(jnp.int32, (chunks, lanes), 1) // band
    blocks = []
    for k in range(count):
        gain = jnp.sqrt(jnp.full((chunks, lanes), weights_ref[k], F32) / total)
        real, imag = [
            gain
            * jnp.concatenate(
                [kernels_ref[k, part : part + 1, c * lanes : (c + 1) * lanes] for c in range(chunks)], axis=0
            )
            for part in range(2)
        ]
        reals = [pltpu.roll(real, band * g, 1) if g else real for g in range(groups)]
        imags = [pltpu.roll(imag, band * g, 1) if g else imag for g in range(groups)]
        for at in range(groups):
            line = imags[(3 - at) % groups]
            line = jnp.where(group == 2, imags[(2 - at) % groups], line)
            line = jnp.where(group == 1, reals[(1 - at) % groups], line)
            blocks.append(jnp.where(group == 0, reals[-at % groups], line))
    return jnp.concatenate(blocks, axis=0)


def adjoint_of(spectrum, gates, target_ref, tables):
    band = spectrum.shape[0]
    width = 4 * band
    kernels = gates.shape[0] // band
    size = target_ref.shape[0]
    scaled = spectrum * (1.0 / (size * size))
    high, low = split(gates * jnp.concatenate([scaled] * kernels, axis=0))
    bands = dot(jnp.concatenate([high, low, high], axis=1), tables["spread"][...])
    stacked = jnp.concatenate(
        [
            jnp.concatenate([bands[band * k : band * (k + 1), :width] for k in range(kernels)], axis=1),
            jnp.concatenate([bands[band * k : band * (k + 1), width:] for k in range(kernels)], axis=1),
        ],
        axis=0,
    )
    high, low = split(stacked)
    fields = dot(tables["field"][...], jnp.concatenate([high, low, high], axis=0))
    squares = fields * fields
    power = squares[:, :width]
    for k in range(1, kernels):
        power = power + squares[:, k * width : (k + 1) * width]
    high, low = split(power)
    lifted = dot(high, tables["lift_cols"][:width, :]) + dot(
        jnp.concatenate([low, high], axis=1), tables["lift_cols"][...]
    )
    high, low = split(lifted)
    deep = jnp.concatenate([high, low, high], axis=0)
    narrowed = []
    step = size // 2
    for begin in range(0, size, step):
        lines = slice(begin, begin + step)
        curve = jnp.tanh(dot(tables["lift_rows"][lines, :], deep) - 0.5 * SHARPNESS * THRESHOLD)
        slope = (1.0 + curve - 2.0 * target_ref[lines, :].astype(F32)) * (1.0 - curve * curve)
        both = dot(slope.astype(BF16), tables["drop_cols"][...])
        narrowed.append((both[:, :width] + both[:, width:]).astype(BF16))
    dropped = row_transform(tables["drop_rows"][...], jnp.concatenate(narrowed, axis=0))
    weighted = fields * jnp.concatenate([dropped] * kernels, axis=1)
    high, low = split(weighted)
    turned = dot(tables["turn"][...], jnp.concatenate([high, low, high], axis=0))
    across = jnp.concatenate(
        [
            jnp.concatenate([turned[:band, k * width : (k + 1) * width] for k in range(kernels)], axis=0),
            jnp.concatenate([turned[band:, k * width : (k + 1) * width] for k in range(kernels)], axis=0),
        ],
        axis=1,
    )
    both = dot(across.astype(BF16), tables["back"][...])
    product = gates * (both[:, :width] + both[:, width:])
    adjoint = product[:band]
    for k in range(1, kernels):
        adjoint = adjoint + product[k * band : (k + 1) * band]
    return adjoint + pltpu.roll(adjoint, width // 2, 1)


CORE_TABLES = ("spread", "field", "lift_cols", "lift_rows", "drop_cols", "drop_rows", "turn", "back")
OPEN_TABLES = ("quad", "rows") + CORE_TABLES


def open_kernel(total, weights_hbm, mask_hbm, dual_hbm, kernels_hbm, target_hbm, *rest):
    count = len(OPEN_TABLES)
    tables_hbm, rest = rest[:count], rest[count:]
    outs, rest = rest[:8], rest[8:]
    base_ref, gates_ref, own_ref, corner1, corner2, middle2, lines_ref, edges_ref = outs
    sources = [*tables_hbm[:2], kernels_hbm, weights_hbm, *tables_hbm[2:], target_hbm]
    mask_ref, dual_ref = rest[:2]
    staged, (line_semaphores, semaphores) = rest[2:-2], rest[-2:]
    size = mask_ref.shape[0]
    pieces = size // INTERSECTION
    edge = size - INTERSECTION

    def cut(at):
        return slice(at * INTERSECTION, (at + 1) * INTERSECTION)

    copies = [
        pltpu.make_async_copy(source, target, semaphores.at[at])
        for at, (source, target) in enumerate(zip(sources, staged))
    ]
    parts = [
        [
            pltpu.make_async_copy(source.at[cut(at), :], target.at[cut(at), :], line_semaphores.at[which, at])
            for which, (source, target) in enumerate(((mask_hbm, mask_ref), (dual_hbm, dual_ref)))
        ]
        for at in range(pieces)
    ]
    for copy in (copies[2], copies[3], copies[0]):
        copy.start()
    for pair in parts:
        for copy in pair:
            copy.start()
    for copy in [copies[1]] + copies[4:]:
        copy.start()
    quad_ref, rows_ref, kernels_ref, weights_ref, *core_refs, target_ref = staged
    band = base_ref.shape[0]
    width = 4 * band
    row, col, rows = place(total)
    even_col = col % 2 == 0

    copies[2].wait()
    copies[3].wait()
    gates = gates_of(kernels_ref, weights_ref, band)
    gates_ref[...] = gates

    copies[0].wait()
    quad = quad_ref[...]
    scaled = quad * edge_scale((size, 1), 0, size, col > 0, col < GRID_COLS - 1).astype(BF16)
    pair = jnp.concatenate([quad, scaled], axis=1)
    mask_parts, dual_parts, lefts, rights = [], [], [], []
    for at in range(pieces):
        for copy in parts[at]:
            copy.wait()
        mask, dual = mask_ref[cut(at), :], dual_ref[cut(at), :]
        mask_parts.append(dot(mask.astype(BF16), pair))
        dual_parts.append(dot(dual.astype(BF16), pair))
        ends = [0.5 * (mask[:, lanes] + dual[:, lanes]) for lanes in (slice(0, INTERSECTION), slice(edge, size))]
        lefts.append(dot(ends[0].astype(BF16), quad[edge:]))
        rights.append(dot(ends[1].astype(BF16), quad[:INTERSECTION]))

    for copy in [copies[1]] + copies[4:]:
        copy.wait()
    lines = rows_ref[...]

    def block(value, at):
        return quad_form(value[:, at * width : (at + 1) * width])

    spectrum = block(row_transform(lines, jnp.concatenate([part[:, :width] for part in mask_parts], axis=0)), 0)
    dual_spectrum = block(row_transform(lines, jnp.concatenate([part[:, :width] for part in dual_parts], axis=0)), 0)
    base_ref[...] = 0.5 * spectrum - 0.25 * dual_spectrum
    line_scale = edge_scale((1, size), 1, size, row > 0, row < rows - 1).astype(BF16)
    outer = jnp.concatenate(
        [
            jnp.concatenate([a[:, width:] + b[:, width:] for a, b in zip(mask_parts, dual_parts)], axis=0),
            jnp.concatenate(lefts, axis=0),
            jnp.concatenate(rights, axis=0),
        ],
        axis=1,
    ).astype(BF16)
    around = row_transform(lines * line_scale, outer)
    upper = 0.5 * row_transform(lines[:, edge:], outer[:INTERSECTION])
    lower = 0.5 * row_transform(lines[:, :INTERSECTION], outer[edge:])

    adjoint = adjoint_of(spectrum, gates, target_ref, dict(zip(CORE_TABLES, core_refs)))
    strips = {}
    for at in range(pieces):
        mask, dual = mask_ref[cut(at), :], dual_ref[cut(at), :]
        first, second = mask + dual, mask + 0.25 * dual
        near = jnp.concatenate([first[:, :INTERSECTION], second[:, :INTERSECTION]], axis=1)
        far = jnp.concatenate([first[:, edge:], second[:, edge:]], axis=1)
        to1, to2 = jnp.where(even_col, far, near), jnp.where(even_col, near, far)
        if at == 0 or at == pieces - 1:
            out = cut(0 if at == 0 else 1)
            corner1[out, :], corner2[out, :] = to1, to2
            strips[at] = (first, second)
        else:
            begin = 2 * INTERSECTION + band + (at - 1) * INTERSECTION
            corner1[begin : begin + INTERSECTION, :] = to1
            middle2[cut(at - 1), :] = to2
    for part, lines_at in enumerate((cut(0), cut(1))):
        above, below = strips[0][part], strips[pieces - 1][part]
        for at, strip in enumerate((above, below)):
            edges_ref[at, lines_at, :] = jnp.concatenate([strip[:, :INTERSECTION], strip[:, edge:]], axis=1)
            lines_ref[at, lines_at, :] = strip[:, INTERSECTION:edge]

    own_ref[...] = jnp.concatenate([block(around, 0), block(upper, 0), block(lower, 0), adjoint], axis=0)
    left = [block(around, 1), block(upper, 1), block(lower, 1)]
    right = [block(around, 2), block(upper, 2), block(lower, 2)]
    tail = slice(2 * INTERSECTION, 2 * INTERSECTION + band)
    for ref, first, second in ((corner1, right, left), (corner2, left, right)):
        ref[tail, :] = pack([jnp.where(even_col, a, b) for a, b in zip(first, second)] + [adjoint])


def pack(blocks):
    lanes = lax.broadcasted_iota(jnp.int32, blocks[0].shape, 1)
    half = blocks[0].shape[1] // 2
    pairs = [jnp.where(lanes < half, a, pltpu.roll(b, half, 1)) for a, b in (blocks[:2], blocks[2:])]
    return jnp.concatenate(pairs, axis=1)


def unpack(tail):
    width = tail.shape[1] // 2
    first, second = tail[:, :width], tail[:, width:]
    return first, pltpu.roll(first, width // 2, 1), second, pltpu.roll(second, width // 2, 1)


def whole_adjoint(value):
    half = value.shape[1] // 2
    lanes = lax.broadcasted_iota(jnp.int32, value.shape, 1)
    return jnp.where(lanes < half, value, pltpu.roll(value, half, 1))


def whole_spectrum(value):
    band = value.shape[1] // 4
    lanes = lax.broadcasted_iota(jnp.int32, value.shape, 1)
    right = jnp.where(lanes < 3 * band, -pltpu.roll(value, band, 1), pltpu.roll(value, 3 * band, 1))
    return jnp.where(lanes < 2 * band, value, right)


def middle_kernel(total, own_ref, got1_ref, got2_ref, edges_ref, lines_ref, keep_ref, *sends):
    band = keep_ref.shape[0]
    row, col, rows = place(total)
    even_col = col % 2 == 0
    cut = INTERSECTION
    one, two = [unpack(ref[2 * cut : 2 * cut + band, :]) for ref in (got1_ref, got2_ref)]
    mine = [own_ref[at * band : (at + 1) * band, :] for at in range(4)]
    keep, upper, lower = [mine[at] + one[at] + two[at] for at in range(3)]
    keep_ref[...] = keep
    summed = []
    for at in range(2):
        lines = slice(at * cut, (at + 1) * cut)
        first, second = got1_ref[lines, :], got2_ref[lines, :]
        left, right = jnp.where(even_col, second, first), jnp.where(even_col, first, second)
        summed.append(
            edges_ref[at]
            + jnp.concatenate(
                [
                    jnp.concatenate([left[:, :cut], right[:, :cut]], axis=1),
                    jnp.concatenate([left[:, cut:], right[:, cut:]], axis=1),
                ],
                axis=0,
            )
        )
    tails = [pack([value, mine[3], one[3], two[3]]) for value in (upper, lower)]
    tails = [jnp.concatenate([value[:, :cut], value[:, cut:]], axis=0) for value in tails]
    for at in range(SETS):
        down = row % SETS == at
        message_ref, shared_ref = sends[at], sends[SETS + at]
        ends = jnp.where(down, summed[1], summed[0])
        left, right = ends[:, :cut], ends[:, cut:]
        inner = jnp.where(down, lines_ref[1], lines_ref[0])
        message_ref[: 2 * cut, :] = jnp.where(even_col, left, right)
        for block in range(inner.shape[1] // cut):
            message_ref[2 * (block + 1) * cut : 2 * (block + 2) * cut, :] = inner[:, block * cut : (block + 1) * cut]
        message_ref[message_ref.shape[0] - 2 * band :, :] = jnp.where(down, tails[1], tails[0])
        shared_ref[...] = jnp.where(even_col, right, left)


def from_rows(row, got):
    even = row % SETS == 0
    return jnp.where(even, got[1], got[0]), jnp.where(even, got[0], got[1])


def tails_of(blocks, table):
    size = table.shape[1] // 2
    width = blocks.shape[1]
    lanes = lax.broadcasted_iota(jnp.int32, (1, width), 1)
    high, low = split(blocks)
    pair = jnp.where(lanes < width // 2, high, low)
    return dot(jnp.concatenate([pair, high], axis=1), table)


def columns_of(table, begin, end):
    size = table.shape[1] // 2
    return jnp.concatenate([table[:, begin:end], table[:, size + begin : size + end]], axis=1)


def stack_of(value, at, band):
    wide = value.shape[1] // 2
    lines = value[at * band : (at + 1) * band]
    return jnp.concatenate([lines[:, :wide], lines[:, wide:]], axis=0)


def widen(value, left, right, edge):
    return jnp.concatenate(
        [value[:, :INTERSECTION] + left, value[:, INTERSECTION:edge], value[:, edge:] + right], axis=1
    )


def deep(value):
    high, low = split(value)
    return jnp.concatenate([high, low, high], axis=0)


def prepare_kernel(total, base_ref, keep_ref, own_ref, lanes_ref, flip_ref, gates_ref, mask_ref, dual_ref, corner1_ref, corner2_ref, shared1_ref, shared2_ref, tail_ref, final_ref, out_ref, gates_out, mask_out, dual_out, shared_out):
    band = base_ref.shape[0]
    size = mask_ref.shape[0]
    edge = size - INTERSECTION
    adjoint = own_ref[3 * band :, :]
    width = adjoint.shape[1]
    high, low = split(adjoint)
    lanes = lax.broadcasted_iota(jnp.int32, adjoint.shape, 1)
    mirrored = dot(jnp.where(lanes < width // 2, high, low), lanes_ref[...])
    high, low = split(mirrored[:, width:])
    flip = flip_ref[...]
    gradient_band = mirrored[:, :width] + dot(flip, high) + dot(flip, low)
    out_ref[...] = base_ref[...] + 0.5 * keep_ref[...] - 0.25 * gradient_band
    gates_out[...] = gates_ref[...]
    shared_out[...] = jnp.concatenate([shared1_ref[...], shared2_ref[...]], axis=0)

    row, col, rows = place(total)
    even_col = col % 2 == 0
    scale = 2.0 / (size * size)
    tail_table = tail_ref[...]
    first, second = [
        whole_adjoint(unpack(ref[2 * INTERSECTION : 2 * INTERSECTION + band, :])[3]) for ref in (corner1_ref, corner2_ref)
    ]
    left, right = jnp.where(even_col, second, first), jnp.where(even_col, first, second)
    own_tail = stack_of(tails_of(adjoint * scale, tail_table), 0, band)
    left_tail = stack_of(tails_of(left * scale, columns_of(tail_table, edge, size)), 0, band)
    right_tail = stack_of(tails_of(right * scale, columns_of(tail_table, 0, INTERSECTION)), 0, band)
    columns = edge_scale((1, size), 1, size, col > 0, col < GRID_COLS - 1)
    summed = columns * widen(own_tail, left_tail, right_tail, edge)
    for begin in range(0, size, INTERSECTION):
        end = begin + INTERSECTION
        share = jnp.asarray(1.0, F32)
        if begin == 0:
            share = share_of(row > 0)
        if end == size:
            share = share_of(row < rows - 1)
        if begin < 2 * INTERSECTION or end == size:
            rhs = deep(
                jnp.concatenate(
                    [(-0.125 * share) * summed - 0.125 * own_tail, (0.25 * share) * summed - 0.25 * own_tail], axis=1
                )
            )
        products = dot(final_ref[begin:end, :], rhs)
        mask, dual = mask_ref[begin:end, :], dual_ref[begin:end, :]
        agreed0, agreed1 = mask + dual, mask + 0.25 * dual
        if begin == 0 or end == size:
            out = slice(0, INTERSECTION) if begin == 0 else slice(INTERSECTION, 2 * INTERSECTION)
            ends1, ends2 = corner1_ref[out, :], corner2_ref[out, :]
            lefts, rights = jnp.where(even_col, ends2, ends1), jnp.where(even_col, ends1, ends2)
            agreed0 = widen(agreed0, lefts[:, :INTERSECTION], rights[:, :INTERSECTION], edge)
            agreed1 = widen(agreed1, lefts[:, INTERSECTION:], rights[:, INTERSECTION:], edge)
        weight = columns * share
        agreed0, agreed1 = agreed0 * weight, agreed1 * weight
        mask_out[begin:end, :] = 0.5 * (agreed0 + agreed1) - 0.375 * dual + products[:, :size]
        dual_out[begin:end, :] = 1.5 * mask + 0.75 * dual - 0.5 * agreed0 - agreed1 + products[:, size:]


def second_kernel(part_ref, got1_ref, got2_ref, gates_ref, target_ref, *rest):
    tables = dict(zip(CORE_TABLES, rest))
    out_ref = rest[len(CORE_TABLES)]
    band = part_ref.shape[0]
    got = [ref[ref.shape[0] - 2 * band : ref.shape[0] - band, :] for ref in (got1_ref, got2_ref)]
    spectrum = whole_spectrum(part_ref[...] + 0.5 * (got[0] + got[1]))
    out_ref[...] = adjoint_of(spectrum, gates_ref[...], target_ref, tables)


def last_kernel(total, mask_ref, dual_ref, corner1_ref, middle2_ref, edge1_ref, edge2_ref, shared1_ref, shared2_ref, handed_ref, adjoint_ref, tail_ref, final_ref, final_edge_ref, mask_hbm, dual_hbm, mask_out, dual_out, semaphores):
    size = mask_ref.shape[0]
    band, width = adjoint_ref.shape
    edge = size - INTERSECTION
    row, col, rows = place(total)
    even_col = col % 2 == 0
    scale = 2.0 / (size * size)
    tail_table = tail_ref[...]
    columns = edge_scale((1, size), 1, size, col > 0, col < GRID_COLS - 1)
    copies = []

    def store(begin, mask, dual):
        lines = slice(begin, begin + INTERSECTION)
        for which, (value, source, target) in enumerate(((mask, mask_out, mask_hbm), (dual, dual_out, dual_hbm))):
            source[lines, :] = value
            copy = pltpu.make_async_copy(
                source.at[lines, :], target.at[lines, :], semaphores.at[which, begin // INTERSECTION]
            )
            copy.start()
            copies.append(copy)

    new_rhs = deep(stack_of(tails_of(adjoint_ref[...] * (-0.25 * scale), tail_table), 0, band))
    left_share, right_share = share_of(col > 0), share_of(col < GRID_COLS - 1)
    for begin in range(INTERSECTION, edge, INTERSECTION):
        lines = slice(begin, begin + INTERSECTION)
        out = slice(begin - INTERSECTION, begin)
        along = begin + INTERSECTION + band
        ends1, ends2 = corner1_ref[along : along + INTERSECTION, :], middle2_ref[out, :]
        left = left_share * jnp.where(even_col, ends2, ends1)
        right = right_share * jnp.where(even_col, ends1, ends2)
        left0, left1, right0, right1 = [
            value[:, cut] for value in (left, right) for cut in (slice(0, INTERSECTION), slice(INTERSECTION, None))
        ]
        mask = mask_ref[lines, :] + dot(final_ref[lines, :], new_rhs)
        store(
            begin,
            widen(mask, 0.5 * (left0 + left1), 0.5 * (right0 + right1), edge),
            widen(dual_ref[lines, :], -0.5 * left0 - left1, -0.5 * right0 - right1, edge),
        )

    refs = (edge1_ref, edge2_ref)
    begin = edge1_ref.shape[0] - 2 * band
    ends = [
        jnp.concatenate([ref[begin : begin + band, :], ref[begin + band :, :]], axis=1) for ref in refs
    ]
    blocks = [unpack(value)[1:] for value in from_rows(row, ends)]
    columns_at = [whole_adjoint(jnp.concatenate([a, b], axis=0)) * scale for a, b in zip(*blocks)]
    left = jnp.where(even_col, columns_at[2], columns_at[1])
    right = jnp.where(even_col, columns_at[1], columns_at[2])
    tails = tails_of(columns_at[0], tail_table)
    left_tails = tails_of(left, columns_of(tail_table, edge, size))
    right_tails = tails_of(right, columns_of(tail_table, 0, INTERSECTION))
    inner = slice(INTERSECTION, edge)
    for at, begin in enumerate((0, edge)):
        lines = slice(begin, begin + INTERSECTION)
        share = share_of(row > 0) if at == 0 else share_of(row < rows - 1)
        summed = (columns * share) * widen(
            stack_of(tails, at, band), stack_of(left_tails, at, band), stack_of(right_tails, at, band), edge
        )
        rhs = deep(jnp.concatenate([-0.125 * summed, 0.25 * summed], axis=1))
        products = dot(final_edge_ref[at * INTERSECTION : (at + 1) * INTERSECTION, :], rhs)

        def across(part):
            def cut(block):
                begin = (2 * block + part) * INTERSECTION
                return slice(begin, begin + INTERSECTION)

            def got(block):
                return from_rows(row, [ref[cut(block), :] for ref in refs])[at]

            outer = (col == 0) | (col == GRID_COLS - 1)
            shared = [
                jnp.where(outer, ref[cut(0), :], handed_ref[cut(which), :])
                for which, ref in enumerate((shared1_ref, shared2_ref))
            ]
            shared, other = from_rows(row, shared)[at], got(0)
            inner = [got(1 + block) for block in range((size - 2 * INTERSECTION) // INTERSECTION)]
            left, right = jnp.where(even_col, other, shared), jnp.where(even_col, shared, other)
            return jnp.concatenate([left, *inner, right], axis=1)

        weight = columns * share
        first, second = across(0) * weight, across(1) * weight
        mask = mask_ref[lines, :] + dot(final_ref[lines, :], new_rhs) + products[:, :size]
        store(begin, mask + 0.5 * (first + second), dual_ref[lines, :] + products[:, size:] - 0.5 * first - second)
    for copy in copies:
        copy.wait()


VMEM_SPEC = pl.BlockSpec(memory_space=pltpu.VMEM)
HBM_SPEC = pl.BlockSpec(memory_space=pltpu.HBM)


def call(kernel, outs, operands, flops, name, in_specs=None, out_spec=VMEM_SPEC, scratch=(), limit=VMEM_LIMIT):
    return pl.pallas_call(
        kernel,
        out_shape=[jax.ShapeDtypeStruct(shape, dtype) for shape, dtype in outs],
        in_specs=in_specs or [VMEM_SPEC] * len(operands),
        out_specs=[out_spec] * len(outs),
        scratch_shapes=list(scratch),
        compiler_params=pltpu.CompilerParams(vmem_limit_bytes=limit),
        cost_estimate=pl.CostEstimate(flops=flops, bytes_accessed=1 << 20, transcendentals=0),
        name=name,
    )(*operands)


def swaps(total):
    cols = GRID_COLS
    along, across = [[], []], [[] for _ in range(SETS)]
    for index in range(total):
        row, col = index // cols, index % cols
        if col + 1 < cols:
            along[col % 2] += [(index, index + 1), (index + 1, index)]
        if index + cols < total:
            across[row % SETS] += [(index, index + cols), (index + cols, index)]
    return along, across


def per_device(mask_init, dual_init, target, kernels, weights):
    mask, dual, goal = mask_init[0], dual_init[0], target[0]
    size = mask.shape[0]
    count = kernels.shape[0]
    band = math.isqrt(kernels.shape[2])
    width = 4 * band
    total = lax.axis_size("ty")
    (row_pairs1, row_pairs2), col_pairs = swaps(total)
    tables = {name: jnp.asarray(table) for name, table in build_tables(size, band).items()}
    core = [tables[name] for name in CORE_TABLES]

    def trade(value, pairs):
        return lax.ppermute(value, "ty", pairs)

    both = 2 * INTERSECTION
    inner = size - both
    block, gate = ((band, width), F32), ((count * band, width), F32)
    stack, message = ((4 * band, width), F32), ((both + band, both), F32)
    side, lines = ((inner, both), F32), ((2, both, inner), F32)
    long_message = ((2 * both + band, both), F32)
    operands = [weights, mask, dual, kernels, goal] + [tables[name] for name in OPEN_TABLES]
    operands = [pltpu.with_memory_space_constraint(value, pltpu.HBM) for value in operands]
    before, after = [mask, dual, tables["quad"], tables["rows"], kernels], core + [goal]
    base, gates, own, corner1, corner2, middle2, line_ends, edges = call(
        functools.partial(open_kernel, total),
        [block, gate, stack, long_message, message, side, lines, ((2, both, both), F32)],
        operands,
        4 * 10**9,
        "open",
        in_specs=[HBM_SPEC] * len(operands),
        scratch=[pltpu.VMEM(value.shape, value.dtype) for value in before]
        + [pltpu.SMEM(weights.shape, weights.dtype)]
        + [pltpu.VMEM(value.shape, value.dtype) for value in after]
        + [
            pltpu.SemaphoreType.DMA((2, size // INTERSECTION)),
            pltpu.SemaphoreType.DMA((len(before) + len(after) - 1,)),
        ],
    )
    corners2, corners1 = trade(corner2, row_pairs2), trade(corner1, row_pairs1)
    keep, *sends = call(
        functools.partial(middle_kernel, total),
        [block] + [((both + 2 * inner + 2 * band, INTERSECTION), F32)] * SETS + [((both, INTERSECTION), F32)] * SETS,
        [own, corners1, corners2, edges, line_ends],
        10**7,
        "middle",
    )
    gots = [trade(value, pairs) for value, pairs in zip(sends, col_pairs)]
    outer_pairs = [[pair for pair in pairs if pair[0] % GRID_COLS in (0, GRID_COLS - 1)] for pairs in col_pairs]
    shared = [trade(value, pairs) for value, pairs in zip(sends[SETS:], outer_pairs)]
    middles2 = trade(middle2, row_pairs2)
    whole = ((size, size), F32)
    part, gates, mask, dual, shared_out = call(
        functools.partial(prepare_kernel, total),
        [block, gate, whole, whole, ((2 * both, INTERSECTION), F32)],
        [base, keep, own, tables["mirror_lanes"], tables["mirror_rows"], gates, mask, dual, corners1, corners2, *shared]
        + [tables["tail"], tables["final"]],
        10**9,
        "prepare",
    )
    handed = trade(shared_out, row_pairs1)
    (adjoint1,) = call(
        second_kernel,
        [block],
        [part, *gots, gates, goal] + core,
        3 * 10**9,
        "second",
    )
    mask, dual = call(
        functools.partial(last_kernel, total),
        [whole, whole],
        [mask, dual, corners1, middles2, *gots, *shared, handed, adjoint1]
        + [tables["tail"], tables["final"], tables["final_edge"]],
        2 * 10**9,
        "last",
        out_spec=HBM_SPEC,
        scratch=[
            pltpu.VMEM((size, size), F32),
            pltpu.VMEM((size, size), F32),
            pltpu.SemaphoreType.DMA((2, size // INTERSECTION)),
        ],
    )
    return (mask[None], dual[None])


def solution(mesh):
    tiles = P(("region", "ty"), None, None)
    return jax.shard_map(
        per_device,
        mesh=mesh,
        in_specs=(tiles, tiles, tiles, P(), P()),
        out_specs=(tiles, tiles),
        check_vma=False,
    )
```

```python
import functools
import math

import jax
import jax.numpy as jnp
import ml_dtypes
import numpy as np
from jax import lax
from jax.experimental import pallas as pl
from jax.experimental.pallas import tpu as pltpu
from jax.sharding import PartitionSpec as P

INTERSECTION = 128
GRID_COLS = 4
SETS = 2
SHARPNESS = 8.0
THRESHOLD = 0.3
F32 = jnp.float32
BF16 = jnp.bfloat16
VMEM_LIMIT = 32 * 1024 * 1024


def halves(table):
    high = table.astype(ml_dtypes.bfloat16)
    low = (table - high.astype(np.float64)).astype(ml_dtypes.bfloat16)
    return high, low


def build_tables(size, band):
    coarse = 2 * band
    stride = size // coarse
    edge = size - INTERSECTION
    frequencies = np.arange(band) - band // 2
    angles = 2.0 * np.pi * ((frequencies[:, None] * np.arange(size)[None, :]) % size) / size
    cos, sin = np.cos(angles), -np.sin(angles)
    order = np.arange(band).reshape(-1, 128 // band).T.reshape(-1)
    rows = np.concatenate([cos[order], sin[order]], axis=0)
    quad = np.concatenate([cos.T, sin.T, -sin.T, cos.T], axis=1)
    dc, ds = cos[:, ::stride], sin[:, ::stride]
    dc_rows, ds_rows = dc[order], ds[order]
    wide = np.arange(-(band - 1), band)
    gaps = np.arange(size)[:, None] - stride * np.arange(coarse)[None, :]
    lift = np.cos(2.0 * np.pi * wide[:, None, None] * gaps[None] / size).sum(0) / coarse

    tables = {}
    tables["quad"] = halves(quad)[0]
    high, low = halves(rows)
    tables["rows"] = np.concatenate([high, low], axis=0)
    spread = np.concatenate(
        [np.concatenate([dc, -ds, -ds, -dc], axis=1), np.concatenate([ds, dc, dc, -ds], axis=1)], axis=0
    )
    high, low = halves(np.concatenate([spread, spread], axis=0))
    tables["spread"] = np.concatenate([high, high, low], axis=0)
    high, low = halves(np.concatenate([dc_rows.T, ds_rows.T], axis=1))
    tables["field"] = np.concatenate([high, high, low], axis=1)
    high, low = halves(np.concatenate([lift.T, lift.T], axis=0))
    tables["lift_cols"] = np.concatenate([high, low], axis=0)
    high, low = halves(lift * (0.5 * SHARPNESS))
    tables["lift_rows"] = np.concatenate([high, high, low], axis=1)
    high, low = halves(lift)
    tables["drop_cols"] = np.concatenate([high, high, low, low], axis=1)
    high, low = halves(lift.T * (0.25 * SHARPNESS))
    tables["drop_rows"] = np.concatenate([high, low], axis=0)
    high, low = halves(np.concatenate([dc_rows, ds_rows], axis=0))
    tables["turn"] = np.concatenate([high, high, low], axis=1)
    back_real = np.concatenate([dc.T, -ds.T, -ds.T, -dc.T], axis=0)
    back_imag = np.concatenate([ds.T, dc.T, dc.T, -ds.T], axis=0)
    high, low = halves(np.concatenate([back_real, back_imag, back_imag, -back_real], axis=1))
    tables["back"] = np.concatenate([high, low], axis=1)
    flip = np.zeros((band, band))
    for place in range(1, band):
        flip[place, band - place] = 1.0
    eye, zero = np.eye(band), np.zeros((band, band))
    own = np.concatenate(
        [
            np.concatenate([eye, zero, zero, eye], axis=1),
            np.concatenate([zero, eye, -eye, zero], axis=1),
        ],
        axis=0,
    )
    turned = np.concatenate(
        [
            np.concatenate([flip, zero, zero, flip], axis=1),
            np.concatenate([zero, -flip, flip, zero], axis=1),
        ],
        axis=0,
    )
    tables["mirror_lanes"] = np.concatenate(
        [np.concatenate([own, own], axis=0), np.concatenate([turned, turned], axis=0)], axis=1
    ).astype(ml_dtypes.bfloat16)
    tables["mirror_rows"] = flip[order][:, order].astype(ml_dtypes.bfloat16)
    tail = np.concatenate([np.concatenate([cos, -sin], axis=1), np.concatenate([sin, cos], axis=1)], axis=0)
    high, low = halves(tail)
    tables["tail"] = np.concatenate([high, high, low, np.zeros_like(low)], axis=0)
    high, low = halves(rows.T)
    tables["final"] = np.concatenate([high, high, low], axis=1)
    near, far = rows[:, :INTERSECTION], rows[:, edge:]
    high, low = halves(np.concatenate([far.T, near.T], axis=0))
    tables["final_edge"] = np.concatenate([high, high, low], axis=1)
    return tables


def dot(left, right):
    return lax.dot_general(left, right, (((1,), (0,)), ((), ())), preferred_element_type=F32)


def split(value):
    high = value.astype(BF16)
    return high, (value - high.astype(F32)).astype(BF16)


def place(total):
    index = lax.axis_index("ty")
    row, col = index // GRID_COLS, index % GRID_COLS
    return row, col, total // GRID_COLS


def has_beside(col):
    return jnp.where(col % 2 == 0, col > 0, col < GRID_COLS - 1)


def kept(present, value):
    return jnp.where(present, value, jnp.zeros_like(value))


def share_of(present):
    return jnp.where(present, 0.5, 1.0).astype(F32)


def edge_scale(shape, dim, size, before, after):
    steps = lax.broadcasted_iota(jnp.int32, shape, dim)
    first = jnp.where(steps < INTERSECTION, share_of(before), 1.0)
    return first * jnp.where(steps >= size - INTERSECTION, share_of(after), 1.0)


def quad_form(value):
    half = value.shape[0] // 2
    width = value.shape[1]
    lanes = lax.broadcasted_iota(jnp.int32, (half, width), 1)
    rolled = pltpu.roll(value[half:], width // 2, 1)
    return value[:half] + jnp.where(lanes < width // 2, rolled, -rolled)


def row_transform(table, value):
    half = table.shape[0] // 2
    both = dot(table, value.astype(BF16))
    return both[:half] + both[half:]


def gates_of(kernels_ref, weights_ref, band):
    count, parts, length = kernels_ref.shape
    lanes = 128
    groups = lanes // band
    chunks = length // lanes
    total = weights_ref[0]
    for k in range(1, count):
        total = total + weights_ref[k]
    group = lax.broadcasted_iota(jnp.int32, (chunks, lanes), 1) // band
    blocks = []
    for k in range(count):
        gain = jnp.sqrt(jnp.full((chunks, lanes), weights_ref[k], F32) / total)
        real, imag = [
            gain
            * jnp.concatenate(
                [kernels_ref[k, part : part + 1, c * lanes : (c + 1) * lanes] for c in range(chunks)], axis=0
            )
            for part in range(2)
        ]
        reals = [pltpu.roll(real, band * g, 1) if g else real for g in range(groups)]
        imags = [pltpu.roll(imag, band * g, 1) if g else imag for g in range(groups)]
        for at in range(groups):
            line = imags[(3 - at) % groups]
            line = jnp.where(group == 2, imags[(2 - at) % groups], line)
            line = jnp.where(group == 1, reals[(1 - at) % groups], line)
            blocks.append(jnp.where(group == 0, reals[-at % groups], line))
    return jnp.concatenate(blocks, axis=0)


def adjoint_of(spectrum, gates, target_ref, tables):
    band = spectrum.shape[0]
    width = 4 * band
    kernels = gates.shape[0] // band
    size = target_ref.shape[0]
    scaled = spectrum * (1.0 / (size * size))
    high, low = split(gates * jnp.concatenate([scaled] * kernels, axis=0))
    bands = dot(jnp.concatenate([high, low, high], axis=1), tables["spread"][...])
    stacked = jnp.concatenate(
        [
            jnp.concatenate([bands[band * k : band * (k + 1), :width] for k in range(kernels)], axis=1),
            jnp.concatenate([bands[band * k : band * (k + 1), width:] for k in range(kernels)], axis=1),
        ],
        axis=0,
    )
    high, low = split(stacked)
    fields = dot(tables["field"][...], jnp.concatenate([high, low, high], axis=0))
    squares = fields * fields
    power = squares[:, :width]
    for k in range(1, kernels):
        power = power + squares[:, k * width : (k + 1) * width]
    high, low = split(power)
    lifted = dot(high, tables["lift_cols"][:width, :]) + dot(
        jnp.concatenate([low, high], axis=1), tables["lift_cols"][...]
    )
    high, low = split(lifted)
    deep = jnp.concatenate([high, low, high], axis=0)
    narrowed = []
    step = size // 2
    for begin in range(0, size, step):
        lines = slice(begin, begin + step)
        curve = jnp.tanh(dot(tables["lift_rows"][lines, :], deep) - 0.5 * SHARPNESS * THRESHOLD)
        slope = (1.0 + curve - 2.0 * target_ref[lines, :].astype(F32)) * (1.0 - curve * curve)
        both = dot(slope.astype(BF16), tables["drop_cols"][...])
        narrowed.append((both[:, :width] + both[:, width:]).astype(BF16))
    dropped = row_transform(tables["drop_rows"][...], jnp.concatenate(narrowed, axis=0))
    weighted = fields * jnp.concatenate([dropped] * kernels, axis=1)
    high, low = split(weighted)
    turned = dot(tables["turn"][...], jnp.concatenate([high, low, high], axis=0))
    across = jnp.concatenate(
        [
            jnp.concatenate([turned[:band, k * width : (k + 1) * width] for k in range(kernels)], axis=0),
            jnp.concatenate([turned[band:, k * width : (k + 1) * width] for k in range(kernels)], axis=0),
        ],
        axis=1,
    )
    both = dot(across.astype(BF16), tables["back"][...])
    product = gates * (both[:, :width] + both[:, width:])
    adjoint = product[:band]
    for k in range(1, kernels):
        adjoint = adjoint + product[k * band : (k + 1) * band]
    return adjoint + pltpu.roll(adjoint, width // 2, 1)


CORE_TABLES = ("spread", "field", "lift_cols", "lift_rows", "drop_cols", "drop_rows", "turn", "back")
OPEN_TABLES = ("quad", "rows") + CORE_TABLES


def open_kernel(total, weights_hbm, mask_hbm, dual_hbm, kernels_hbm, target_hbm, *rest):
    count = len(OPEN_TABLES)
    tables_hbm, rest = rest[:count], rest[count:]
    outs, rest = rest[:8], rest[8:]
    base_ref, gates_ref, own_ref, corner1, corner2, middle2, lines_ref, edges_ref = outs
    sources = [*tables_hbm[:2], kernels_hbm, weights_hbm, *tables_hbm[2:], target_hbm]
    mask_ref, dual_ref = rest[:2]
    staged, (line_semaphores, semaphores) = rest[2:-2], rest[-2:]
    size = mask_ref.shape[0]
    pieces = size // INTERSECTION
    edge = size - INTERSECTION

    def cut(at):
        return slice(at * INTERSECTION, (at + 1) * INTERSECTION)

    copies = [
        pltpu.make_async_copy(source, target, semaphores.at[at])
        for at, (source, target) in enumerate(zip(sources, staged))
    ]
    parts = [
        [
            pltpu.make_async_copy(source.at[cut(at), :], target.at[cut(at), :], line_semaphores.at[which, at])
            for which, (source, target) in enumerate(((mask_hbm, mask_ref), (dual_hbm, dual_ref)))
        ]
        for at in range(pieces)
    ]
    for copy in (copies[2], copies[3], copies[0]):
        copy.start()
    for pair in parts:
        for copy in pair:
            copy.start()
    for copy in [copies[1]] + copies[4:]:
        copy.start()
    quad_ref, rows_ref, kernels_ref, weights_ref, *core_refs, target_ref = staged
    band = base_ref.shape[0]
    width = 4 * band
    row, col, rows = place(total)
    even_col = col % 2 == 0

    copies[2].wait()
    copies[3].wait()
    gates = gates_of(kernels_ref, weights_ref, band)
    gates_ref[...] = gates

    copies[0].wait()
    quad = quad_ref[...]
    scaled = quad * edge_scale((size, 1), 0, size, col > 0, col < GRID_COLS - 1).astype(BF16)
    pair = jnp.concatenate([quad, scaled], axis=1)
    mask_parts, dual_parts, lefts, rights = [], [], [], []
    for at in range(pieces):
        for copy in parts[at]:
            copy.wait()
        mask, dual = mask_ref[cut(at), :], dual_ref[cut(at), :]
        mask_parts.append(dot(mask.astype(BF16), pair))
        dual_parts.append(dot(dual.astype(BF16), pair))
        ends = [0.5 * (mask[:, lanes] + dual[:, lanes]) for lanes in (slice(0, INTERSECTION), slice(edge, size))]
        lefts.append(dot(ends[0].astype(BF16), quad[edge:]))
        rights.append(dot(ends[1].astype(BF16), quad[:INTERSECTION]))

    for copy in [copies[1]] + copies[4:]:
        copy.wait()
    lines = rows_ref[...]

    def block(value, at):
        return quad_form(value[:, at * width : (at + 1) * width])

    spectrum = block(row_transform(lines, jnp.concatenate([part[:, :width] for part in mask_parts], axis=0)), 0)
    dual_spectrum = block(row_transform(lines, jnp.concatenate([part[:, :width] for part in dual_parts], axis=0)), 0)
    base_ref[...] = 0.5 * spectrum - 0.25 * dual_spectrum
    line_scale = edge_scale((1, size), 1, size, row > 0, row < rows - 1).astype(BF16)
    outer = jnp.concatenate(
        [
            jnp.concatenate([a[:, width:] + b[:, width:] for a, b in zip(mask_parts, dual_parts)], axis=0),
            jnp.concatenate(lefts, axis=0),
            jnp.concatenate(rights, axis=0),
        ],
        axis=1,
    ).astype(BF16)
    around = row_transform(lines * line_scale, outer)
    upper = 0.5 * row_transform(lines[:, edge:], outer[:INTERSECTION])
    lower = 0.5 * row_transform(lines[:, :INTERSECTION], outer[edge:])

    adjoint = adjoint_of(spectrum, gates, target_ref, dict(zip(CORE_TABLES, core_refs)))
    strips = {}
    for at in range(pieces):
        mask, dual = mask_ref[cut(at), :], dual_ref[cut(at), :]
        first, second = mask + dual, mask + 0.25 * dual
        near = jnp.concatenate([first[:, :INTERSECTION], second[:, :INTERSECTION]], axis=1)
        far = jnp.concatenate([first[:, edge:], second[:, edge:]], axis=1)
        to1, to2 = jnp.where(even_col, far, near), jnp.where(even_col, near, far)
        if at == 0 or at == pieces - 1:
            out = cut(0 if at == 0 else 1)
            corner1[out, :], corner2[out, :] = to1, to2
            strips[at] = (first, second)
        else:
            begin = 2 * INTERSECTION + band + (at - 1) * INTERSECTION
            corner1[begin : begin + INTERSECTION, :] = to1
            middle2[cut(at - 1), :] = to2
    middle2[size - 2 * INTERSECTION :, :] = jnp.zeros((middle2.shape[0] - size + 2 * INTERSECTION, middle2.shape[1]), F32)
    for part, lines_at in enumerate((cut(0), cut(1))):
        above, below = strips[0][part], strips[pieces - 1][part]
        for at, strip in enumerate((above, below)):
            edges_ref[at, lines_at, :] = jnp.concatenate([strip[:, :INTERSECTION], strip[:, edge:]], axis=1)
            lines_ref[at, lines_at, :] = strip[:, INTERSECTION:edge]

    own_ref[...] = jnp.concatenate([block(around, 0), block(upper, 0), block(lower, 0), adjoint], axis=0)
    left = [block(around, 1), block(upper, 1), block(lower, 1)]
    right = [block(around, 2), block(upper, 2), block(lower, 2)]
    tail = slice(2 * INTERSECTION, 2 * INTERSECTION + band)
    for ref, first, second in ((corner1, right, left), (corner2, left, right)):
        ref[tail, :] = pack([jnp.where(even_col, a, b) for a, b in zip(first, second)] + [adjoint])


def pack(blocks):
    lanes = lax.broadcasted_iota(jnp.int32, blocks[0].shape, 1)
    half = blocks[0].shape[1] // 2
    pairs = [jnp.where(lanes < half, a, pltpu.roll(b, half, 1)) for a, b in (blocks[:2], blocks[2:])]
    return jnp.concatenate(pairs, axis=1)


def unpack(tail):
    width = tail.shape[1] // 2
    first, second = tail[:, :width], tail[:, width:]
    return first, pltpu.roll(first, width // 2, 1), second, pltpu.roll(second, width // 2, 1)


def whole_adjoint(value):
    half = value.shape[1] // 2
    lanes = lax.broadcasted_iota(jnp.int32, value.shape, 1)
    return jnp.where(lanes < half, value, pltpu.roll(value, half, 1))


def whole_spectrum(value):
    band = value.shape[1] // 4
    lanes = lax.broadcasted_iota(jnp.int32, value.shape, 1)
    right = jnp.where(lanes < 3 * band, -pltpu.roll(value, band, 1), pltpu.roll(value, 3 * band, 1))
    return jnp.where(lanes < 2 * band, value, right)


def middle_kernel(total, own_ref, got1_ref, got2_ref, edges_ref, lines_ref, keep_ref, *sends):
    band = keep_ref.shape[0]
    row, col, rows = place(total)
    even_col = col % 2 == 0
    cut = INTERSECTION
    beside = has_beside(col)
    tail = slice(2 * cut, 2 * cut + band)
    one, two = unpack(got1_ref[tail, :]), unpack(kept(beside, got2_ref[tail, :]))
    mine = [own_ref[at * band : (at + 1) * band, :] for at in range(4)]
    keep, upper, lower = [mine[at] + one[at] + two[at] for at in range(3)]
    keep_ref[...] = keep
    summed = []
    for at in range(2):
        lines = slice(at * cut, (at + 1) * cut)
        first, second = got1_ref[lines, :], kept(beside, got2_ref[lines, :])
        left, right = jnp.where(even_col, second, first), jnp.where(even_col, first, second)
        summed.append(
            edges_ref[at]
            + jnp.concatenate(
                [
                    jnp.concatenate([left[:, :cut], right[:, :cut]], axis=1),
                    jnp.concatenate([left[:, cut:], right[:, cut:]], axis=1),
                ],
                axis=0,
            )
        )
    tails = [pack([value, mine[3], one[3], two[3]]) for value in (upper, lower)]
    tails = [jnp.concatenate([value[:, :cut], value[:, cut:]], axis=0) for value in tails]
    for at in range(SETS):
        down = row % SETS == at
        message_ref, shared_ref = sends[at], sends[SETS + at]
        ends = jnp.where(down, summed[1], summed[0])
        left, right = ends[:, :cut], ends[:, cut:]
        inner = jnp.where(down, lines_ref[1], lines_ref[0])
        message_ref[: 2 * cut, :] = jnp.where(even_col, left, right)
        for block in range(inner.shape[1] // cut):
            message_ref[2 * (block + 1) * cut : 2 * (block + 2) * cut, :] = inner[:, block * cut : (block + 1) * cut]
        message_ref[message_ref.shape[0] - 2 * band :, :] = jnp.where(down, tails[1], tails[0])
        shared_ref[...] = jnp.where(even_col, right, left)


def from_rows(row, rows, got):
    even = row % SETS == 0
    above, below = jnp.where(even, got[1], got[0]), jnp.where(even, got[0], got[1])
    return kept(row > 0, above), kept(row < rows - 1, below)


def tails_of(blocks, table):
    size = table.shape[1] // 2
    width = blocks.shape[1]
    lanes = lax.broadcasted_iota(jnp.int32, (1, width), 1)
    high, low = split(blocks)
    pair = jnp.where(lanes < width // 2, high, low)
    return dot(jnp.concatenate([pair, high], axis=1), table)


def columns_of(table, begin, end):
    size = table.shape[1] // 2
    return jnp.concatenate([table[:, begin:end], table[:, size + begin : size + end]], axis=1)


def stack_of(value, at, band):
    wide = value.shape[1] // 2
    lines = value[at * band : (at + 1) * band]
    return jnp.concatenate([lines[:, :wide], lines[:, wide:]], axis=0)


def widen(value, left, right, edge):
    return jnp.concatenate(
        [value[:, :INTERSECTION] + left, value[:, INTERSECTION:edge], value[:, edge:] + right], axis=1
    )


def deep(value):
    high, low = split(value)
    return jnp.concatenate([high, low, high], axis=0)


def prepare_kernel(total, base_ref, keep_ref, own_ref, lanes_ref, flip_ref, gates_ref, mask_ref, dual_ref, corner1_ref, corner2_ref, shared1_ref, shared2_ref, tail_ref, final_ref, early_hbm, out_ref, gates_out, mask_out, dual_out, shared_out):
    band = base_ref.shape[0]
    size = mask_ref.shape[0]
    edge = size - INTERSECTION
    adjoint = own_ref[3 * band :, :]
    width = adjoint.shape[1]
    high, low = split(adjoint)
    lanes = lax.broadcasted_iota(jnp.int32, adjoint.shape, 1)
    mirrored = dot(jnp.where(lanes < width // 2, high, low), lanes_ref[...])
    high, low = split(mirrored[:, width:])
    flip = flip_ref[...]
    gradient_band = mirrored[:, :width] + dot(flip, high) + dot(flip, low)
    out_ref[...] = base_ref[...] + 0.5 * keep_ref[...] - 0.25 * gradient_band
    gates_out[...] = gates_ref[...]
    shared_out[...] = jnp.concatenate([shared1_ref[...], shared2_ref[...]], axis=0)

    row, col, rows = place(total)
    even_col = col % 2 == 0
    scale = 2.0 / (size * size)
    tail_table = tail_ref[...]
    beside = has_beside(col)
    tail = slice(2 * INTERSECTION, 2 * INTERSECTION + band)
    first, second = [whole_adjoint(unpack(value)[3]) for value in (corner1_ref[tail, :], kept(beside, corner2_ref[tail, :]))]
    left, right = jnp.where(even_col, second, first), jnp.where(even_col, first, second)
    own_tail = stack_of(tails_of(adjoint * scale, tail_table), 0, band)
    left_tail = stack_of(tails_of(left * scale, columns_of(tail_table, edge, size)), 0, band)
    right_tail = stack_of(tails_of(right * scale, columns_of(tail_table, 0, INTERSECTION)), 0, band)
    columns = edge_scale((1, size), 1, size, col > 0, col < GRID_COLS - 1)
    summed = columns * widen(own_tail, left_tail, right_tail, edge)
    for begin in range(0, size, INTERSECTION):
        end = begin + INTERSECTION
        share = jnp.asarray(1.0, F32)
        if begin == 0:
            share = share_of(row > 0)
        if end == size:
            share = share_of(row < rows - 1)
        if begin < 2 * INTERSECTION or end == size:
            rhs = deep(
                jnp.concatenate(
                    [(-0.125 * share) * summed - 0.125 * own_tail, (0.25 * share) * summed - 0.25 * own_tail], axis=1
                )
            )
        products = dot(final_ref[begin:end, :], rhs)
        mask, dual = mask_ref[begin:end, :], dual_ref[begin:end, :]
        agreed0, agreed1 = mask + dual, mask + 0.25 * dual
        if begin == 0 or end == size:
            out = slice(0, INTERSECTION) if begin == 0 else slice(INTERSECTION, 2 * INTERSECTION)
            ends1, ends2 = corner1_ref[out, :], kept(beside, corner2_ref[out, :])
            lefts, rights = jnp.where(even_col, ends2, ends1), jnp.where(even_col, ends1, ends2)
            agreed0 = widen(agreed0, lefts[:, :INTERSECTION], rights[:, :INTERSECTION], edge)
            agreed1 = widen(agreed1, lefts[:, INTERSECTION:], rights[:, INTERSECTION:], edge)
        weight = columns * share
        agreed0, agreed1 = agreed0 * weight, agreed1 * weight
        mask_out[begin:end, :] = 0.5 * (agreed0 + agreed1) - 0.375 * dual + products[:, :size]
        dual_out[begin:end, :] = 1.5 * mask + 0.75 * dual - 0.5 * agreed0 - agreed1 + products[:, size:]


def second_kernel(total, part_ref, got1_ref, got2_ref, gates_ref, target_ref, *rest):
    tables = dict(zip(CORE_TABLES, rest))
    out_ref = rest[len(CORE_TABLES)]
    band = part_ref.shape[0]
    got = [ref[ref.shape[0] - 2 * band : ref.shape[0] - band, :] for ref in (got1_ref, got2_ref)]
    row, col, rows = place(total)
    above, below = from_rows(row, rows, got)
    spectrum = whole_spectrum(part_ref[...] + 0.5 * (above + below))
    out_ref[...] = adjoint_of(spectrum, gates_ref[...], target_ref, tables)


def last_kernel(total, mask_ref, dual_ref, corner1_ref, middle2_ref, edge1_ref, edge2_ref, shared1_ref, shared2_ref, handed_ref, adjoint_ref, tail_ref, final_ref, final_edge_ref, mask_hbm, dual_hbm, mask_out, dual_out, semaphores):
    size = mask_ref.shape[0]
    band, width = adjoint_ref.shape
    edge = size - INTERSECTION
    row, col, rows = place(total)
    even_col = col % 2 == 0
    scale = 2.0 / (size * size)
    tail_table = tail_ref[...]
    columns = edge_scale((1, size), 1, size, col > 0, col < GRID_COLS - 1)
    copies = []

    def store(begin, mask, dual):
        lines = slice(begin, begin + INTERSECTION)
        for which, (value, source, target) in enumerate(((mask, mask_out, mask_hbm), (dual, dual_out, dual_hbm))):
            source[lines, :] = value
            copy = pltpu.make_async_copy(
                source.at[lines, :], target.at[lines, :], semaphores.at[which, begin // INTERSECTION]
            )
            copy.start()
            copies.append(copy)

    new_rhs = deep(stack_of(tails_of(adjoint_ref[...] * (-0.25 * scale), tail_table), 0, band))
    left_share, right_share = share_of(col > 0), share_of(col < GRID_COLS - 1)
    for begin in range(INTERSECTION, edge, INTERSECTION):
        lines = slice(begin, begin + INTERSECTION)
        out = slice(begin - INTERSECTION, begin)
        along = begin + INTERSECTION + band
        ends1, ends2 = corner1_ref[along : along + INTERSECTION, :], kept(has_beside(col), middle2_ref[out, :])
        left = left_share * jnp.where(even_col, ends2, ends1)
        right = right_share * jnp.where(even_col, ends1, ends2)
        left0, left1, right0, right1 = [
            value[:, cut] for value in (left, right) for cut in (slice(0, INTERSECTION), slice(INTERSECTION, None))
        ]
        mask = mask_ref[lines, :] + dot(final_ref[lines, :], new_rhs)
        store(
            begin,
            widen(mask, 0.5 * (left0 + left1), 0.5 * (right0 + right1), edge),
            widen(dual_ref[lines, :], -0.5 * left0 - left1, -0.5 * right0 - right1, edge),
        )

    refs = (edge1_ref, edge2_ref)
    begin = edge1_ref.shape[0] - 2 * band
    ends = [
        jnp.concatenate([ref[begin : begin + band, :], ref[begin + band :, :]], axis=1) for ref in refs
    ]
    blocks = [unpack(value)[1:] for value in from_rows(row, rows, ends)]
    columns_at = [whole_adjoint(jnp.concatenate([a, b], axis=0)) * scale for a, b in zip(*blocks)]
    left = jnp.where(even_col, columns_at[2], columns_at[1])
    right = jnp.where(even_col, columns_at[1], columns_at[2])
    tails = tails_of(columns_at[0], tail_table)
    left_tails = tails_of(left, columns_of(tail_table, edge, size))
    right_tails = tails_of(right, columns_of(tail_table, 0, INTERSECTION))
    inner = slice(INTERSECTION, edge)
    for at, begin in enumerate((0, edge)):
        lines = slice(begin, begin + INTERSECTION)
        share = share_of(row > 0) if at == 0 else share_of(row < rows - 1)
        summed = (columns * share) * widen(
            stack_of(tails, at, band), stack_of(left_tails, at, band), stack_of(right_tails, at, band), edge
        )
        rhs = deep(jnp.concatenate([-0.125 * summed, 0.25 * summed], axis=1))
        products = dot(final_edge_ref[at * INTERSECTION : (at + 1) * INTERSECTION, :], rhs)

        def across(part):
            def cut(block):
                begin = (2 * block + part) * INTERSECTION
                return slice(begin, begin + INTERSECTION)

            def got(block):
                return from_rows(row, rows, [ref[cut(block), :] for ref in refs])[at]

            outer = (col == 0) | (col == GRID_COLS - 1)
            shared = [
                jnp.where(outer, ref[cut(0), :], handed_ref[cut(which), :])
                for which, ref in enumerate((shared1_ref, shared2_ref))
            ]
            shared, other = from_rows(row, rows, shared)[at], got(0)
            inner = [got(1 + block) for block in range((size - 2 * INTERSECTION) // INTERSECTION)]
            left, right = jnp.where(even_col, other, shared), jnp.where(even_col, shared, other)
            return jnp.concatenate([left, *inner, right], axis=1)

        weight = columns * share
        first, second = across(0) * weight, across(1) * weight
        mask = mask_ref[lines, :] + dot(final_ref[lines, :], new_rhs) + products[:, :size]
        store(begin, mask + 0.5 * (first + second), dual_ref[lines, :] + products[:, size:] - 0.5 * first - second)
    for copy in copies:
        copy.wait()


VMEM_SPEC = pl.BlockSpec(memory_space=pltpu.VMEM)
HBM_SPEC = pl.BlockSpec(memory_space=pltpu.HBM)


def call(kernel, outs, operands, flops, name, in_specs=None, out_spec=VMEM_SPEC, scratch=(), limit=VMEM_LIMIT):
    return pl.pallas_call(
        kernel,
        out_shape=[jax.ShapeDtypeStruct(shape, dtype) for shape, dtype in outs],
        in_specs=in_specs or [VMEM_SPEC] * len(operands),
        out_specs=[out_spec] * len(outs),
        scratch_shapes=list(scratch),
        compiler_params=pltpu.CompilerParams(vmem_limit_bytes=limit),
        cost_estimate=pl.CostEstimate(flops=flops, bytes_accessed=1 << 20, transcendentals=0),
        name=name,
    )(*operands)


def swaps(total):
    cols = GRID_COLS
    along, across = [[], []], [[] for _ in range(SETS)]
    for index in range(total):
        row, col = index // cols, index % cols
        if col + 1 < cols:
            along[col % 2] += [(index, index + 1), (index + 1, index)]
        if index + cols < total:
            across[row % SETS] += [(index, index + cols), (index + cols, index)]
    return along, across


def per_device(mask_init, dual_init, target, kernels, weights):
    mask, dual, goal = mask_init[0], dual_init[0], target[0]
    size = mask.shape[0]
    count = kernels.shape[0]
    band = math.isqrt(kernels.shape[2])
    width = 4 * band
    total = lax.axis_size("ty")
    (row_pairs1, row_pairs2), col_pairs = swaps(total)
    tables = {name: jnp.asarray(table) for name, table in build_tables(size, band).items()}
    core = [tables[name] for name in CORE_TABLES]

    regions = lax.axis_size("region")

    def trade(value, pairs, twinned=False):
        if not twinned:
            return lax.ppermute(value, "ty", pairs)
        busy = {first for first, second in pairs}
        twins = [(first, first ^ 1) for first in range(regions) if first ^ 1 < regions]
        whole = [(at * total + first, at * total + second) for at in range(regions) for first, second in pairs]
        whole += [(a * total + tile, b * total + tile) for tile in range(total) if tile not in busy for a, b in twins]
        return lax.ppermute(value, ("region", "ty"), whole)

    both = 2 * INTERSECTION
    inner = size - both
    block, gate = ((band, width), F32), ((count * band, width), F32)
    stack, message = ((4 * band, width), F32), ((both + band, both), F32)
    side, lines = ((384, both), F32), ((2, both, inner), F32)
    long_message = ((2 * both + band, both), F32)
    operands = [weights, mask, dual, kernels, goal] + [tables[name] for name in OPEN_TABLES]
    operands = [pltpu.with_memory_space_constraint(value, pltpu.HBM) for value in operands]
    before, after = [mask, dual, tables["quad"], tables["rows"], kernels], core + [goal]
    base, gates, own, corner1, corner2, middle2, line_ends, edges = call(
        functools.partial(open_kernel, total),
        [block, gate, stack, long_message, message, side, lines, ((2, both, both), F32)],
        operands,
        4 * 10**9,
        "open",
        in_specs=[HBM_SPEC] * len(operands),
        scratch=[pltpu.VMEM(value.shape, value.dtype) for value in before]
        + [pltpu.SMEM(weights.shape, weights.dtype)]
        + [pltpu.VMEM(value.shape, value.dtype) for value in after]
        + [
            pltpu.SemaphoreType.DMA((2, size // INTERSECTION)),
            pltpu.SemaphoreType.DMA((len(before) + len(after) - 1,)),
        ],
    )
    corners2, corners1 = trade(corner2, row_pairs2), trade(corner1, row_pairs1)
    keep, *sends = call(
        functools.partial(middle_kernel, total),
        [block] + [((both + 2 * inner + 2 * band, INTERSECTION), F32)] * SETS + [((both, INTERSECTION), F32)] * SETS,
        [own, corners1, corners2, edges, line_ends],
        10**7,
        "middle",
    )
    gots = [trade(value, pairs, True) for value, pairs in zip(sends, col_pairs)]
    outer_pairs = [[pair for pair in pairs if pair[0] % GRID_COLS in (0, GRID_COLS - 1)] for pairs in col_pairs]
    shared = [trade(value, pairs) for value, pairs in zip(sends[SETS:], outer_pairs)]
    middles2 = trade(middle2, row_pairs2)
    whole = ((size, size), F32)
    part, gates, mask, dual, shared_out = call(
        functools.partial(prepare_kernel, total),
        [block, gate, whole, whole, ((2 * both, INTERSECTION), F32)],
        [base, keep, own, tables["mirror_lanes"], tables["mirror_rows"], gates, mask, dual, corners1, corners2, *shared]
        + [tables["tail"], tables["final"], middles2],
        10**9,
        "prepare",
        in_specs=[VMEM_SPEC] * 14 + [HBM_SPEC],
    )
    handed = trade(shared_out, row_pairs1)
    (adjoint1,) = call(
        functools.partial(second_kernel, total),
        [block],
        [part, *gots, gates, goal] + core,
        3 * 10**9,
        "second",
    )
    mask, dual = call(
        functools.partial(last_kernel, total),
        [whole, whole],
        [mask, dual, corners1, middles2, *gots, *shared, handed, adjoint1]
        + [tables["tail"], tables["final"], tables["final_edge"]],
        2 * 10**9,
        "last",
        out_spec=HBM_SPEC,
        scratch=[
            pltpu.VMEM((size, size), F32),
            pltpu.VMEM((size, size), F32),
            pltpu.SemaphoreType.DMA((2, size // INTERSECTION)),
        ],
    )
    return (mask[None], dual[None])


def solution(mesh):
    tiles = P(("region", "ty"), None, None)
    return jax.shard_map(
        per_device,
        mesh=mesh,
        in_specs=(tiles, tiles, tiles, P(), P()),
        out_specs=(tiles, tiles),
        check_vma=False,
    )
```

```python
import functools
import math

import jax
import jax.numpy as jnp
import ml_dtypes
import numpy as np
from jax import lax
from jax.experimental import pallas as pl
from jax.experimental.pallas import tpu as pltpu
from jax.sharding import PartitionSpec as P

INTERSECTION = 128
GRID_COLS = 4
SETS = 2
SHARPNESS = 8.0
THRESHOLD = 0.3
F32 = jnp.float32
BF16 = jnp.bfloat16
VMEM_LIMIT = 32 * 1024 * 1024


def halves(table):
    high = table.astype(ml_dtypes.bfloat16)
    low = (table - high.astype(np.float64)).astype(ml_dtypes.bfloat16)
    return high, low


def build_tables(size, band):
    coarse = 2 * band
    stride = size // coarse
    edge = size - INTERSECTION
    frequencies = np.arange(band) - band // 2
    angles = 2.0 * np.pi * ((frequencies[:, None] * np.arange(size)[None, :]) % size) / size
    cos, sin = np.cos(angles), -np.sin(angles)
    order = np.arange(band).reshape(-1, 128 // band).T.reshape(-1)
    rows = np.concatenate([cos[order], sin[order]], axis=0)
    quad = np.concatenate([cos.T, sin.T, -sin.T, cos.T], axis=1)
    dc, ds = cos[:, ::stride], sin[:, ::stride]
    dc_rows, ds_rows = dc[order], ds[order]
    wide = np.arange(-(band - 1), band)
    gaps = np.arange(size)[:, None] - stride * np.arange(coarse)[None, :]
    lift = np.cos(2.0 * np.pi * wide[:, None, None] * gaps[None] / size).sum(0) / coarse

    tables = {}
    tables["quad"] = halves(quad)[0]
    high, low = halves(rows)
    tables["rows"] = np.concatenate([high, low], axis=0)
    spread = np.concatenate(
        [np.concatenate([dc, -ds, -ds, -dc], axis=1), np.concatenate([ds, dc, dc, -ds], axis=1)], axis=0
    )
    high, low = halves(np.concatenate([spread, spread], axis=0))
    tables["spread"] = np.concatenate([high, high, low], axis=0)
    high, low = halves(np.concatenate([dc_rows.T, ds_rows.T], axis=1))
    tables["field"] = np.concatenate([high, high, low], axis=1)
    high, low = halves(np.concatenate([lift.T, lift.T], axis=0))
    tables["lift_cols"] = np.concatenate([high, low], axis=0)
    high, low = halves(lift * (0.5 * SHARPNESS))
    tables["lift_rows"] = np.concatenate([high, high, low], axis=1)
    high, low = halves(lift)
    tables["drop_cols"] = np.concatenate([high, high, low, low], axis=1)
    high, low = halves(lift.T * (0.25 * SHARPNESS))
    tables["drop_rows"] = np.concatenate([high, low], axis=0)
    high, low = halves(np.concatenate([dc_rows, ds_rows], axis=0))
    tables["turn"] = np.concatenate([high, high, low], axis=1)
    back_real = np.concatenate([dc.T, -ds.T, -ds.T, -dc.T], axis=0)
    back_imag = np.concatenate([ds.T, dc.T, dc.T, -ds.T], axis=0)
    high, low = halves(np.concatenate([back_real, back_imag, back_imag, -back_real], axis=1))
    tables["back"] = np.concatenate([high, low], axis=1)
    flip = np.zeros((band, band))
    for place in range(1, band):
        flip[place, band - place] = 1.0
    eye, zero = np.eye(band), np.zeros((band, band))
    own = np.concatenate(
        [
            np.concatenate([eye, zero, zero, eye], axis=1),
            np.concatenate([zero, eye, -eye, zero], axis=1),
        ],
        axis=0,
    )
    turned = np.concatenate(
        [
            np.concatenate([flip, zero, zero, flip], axis=1),
            np.concatenate([zero, -flip, flip, zero], axis=1),
        ],
        axis=0,
    )
    tables["mirror_lanes"] = np.concatenate(
        [np.concatenate([own, own], axis=0), np.concatenate([turned, turned], axis=0)], axis=1
    ).astype(ml_dtypes.bfloat16)
    tables["mirror_rows"] = flip[order][:, order].astype(ml_dtypes.bfloat16)
    tail = np.concatenate([np.concatenate([cos, -sin], axis=1), np.concatenate([sin, cos], axis=1)], axis=0)
    high, low = halves(tail)
    tables["tail"] = np.concatenate([high, high, low, np.zeros_like(low)], axis=0)
    high, low = halves(rows.T)
    tables["final"] = np.concatenate([high, high, low], axis=1)
    near, far = rows[:, :INTERSECTION], rows[:, edge:]
    high, low = halves(np.concatenate([far.T, near.T], axis=0))
    tables["final_edge"] = np.concatenate([high, high, low], axis=1)
    return tables


def dot(left, right):
    return lax.dot_general(left, right, (((1,), (0,)), ((), ())), preferred_element_type=F32)


def split(value):
    high = value.astype(BF16)
    return high, (value - high.astype(F32)).astype(BF16)


def place(total):
    index = lax.axis_index("ty")
    row, col = index // GRID_COLS, index % GRID_COLS
    return row, col, total // GRID_COLS


def has_beside(col):
    return jnp.where(col % 2 == 0, col > 0, col < GRID_COLS - 1)


def kept(present, value):
    return jnp.where(present, value, jnp.zeros_like(value))


def share_of(present):
    return jnp.where(present, 0.5, 1.0).astype(F32)


def edge_scale(shape, dim, size, before, after):
    steps = lax.broadcasted_iota(jnp.int32, shape, dim)
    first = jnp.where(steps < INTERSECTION, share_of(before), 1.0)
    return first * jnp.where(steps >= size - INTERSECTION, share_of(after), 1.0)


def quad_form(value):
    half = value.shape[0] // 2
    width = value.shape[1]
    lanes = lax.broadcasted_iota(jnp.int32, (half, width), 1)
    rolled = pltpu.roll(value[half:], width // 2, 1)
    return value[:half] + jnp.where(lanes < width // 2, rolled, -rolled)


def row_transform(table, value):
    half = table.shape[0] // 2
    both = dot(table, value.astype(BF16))
    return both[:half] + both[half:]


def gates_of(kernels_ref, weights_ref, band):
    count, parts, length = kernels_ref.shape
    lanes = 128
    groups = lanes // band
    chunks = length // lanes
    total = weights_ref[0]
    for k in range(1, count):
        total = total + weights_ref[k]
    group = lax.broadcasted_iota(jnp.int32, (chunks, lanes), 1) // band
    blocks = []
    for k in range(count):
        gain = jnp.sqrt(jnp.full((chunks, lanes), weights_ref[k], F32) / total)
        real, imag = [
            gain
            * jnp.concatenate(
                [kernels_ref[k, part : part + 1, c * lanes : (c + 1) * lanes] for c in range(chunks)], axis=0
            )
            for part in range(2)
        ]
        reals = [pltpu.roll(real, band * g, 1) if g else real for g in range(groups)]
        imags = [pltpu.roll(imag, band * g, 1) if g else imag for g in range(groups)]
        for at in range(groups):
            line = imags[(3 - at) % groups]
            line = jnp.where(group == 2, imags[(2 - at) % groups], line)
            line = jnp.where(group == 1, reals[(1 - at) % groups], line)
            blocks.append(jnp.where(group == 0, reals[-at % groups], line))
    return jnp.concatenate(blocks, axis=0)


def adjoint_of(spectrum, gates, target_ref, tables):
    band = spectrum.shape[0]
    width = 4 * band
    kernels = gates.shape[0] // band
    size = target_ref.shape[0]
    scaled = spectrum * (1.0 / (size * size))
    high, low = split(gates * jnp.concatenate([scaled] * kernels, axis=0))
    bands = dot(jnp.concatenate([high, low, high], axis=1), tables["spread"][...])
    stacked = jnp.concatenate(
        [
            jnp.concatenate([bands[band * k : band * (k + 1), :width] for k in range(kernels)], axis=1),
            jnp.concatenate([bands[band * k : band * (k + 1), width:] for k in range(kernels)], axis=1),
        ],
        axis=0,
    )
    high, low = split(stacked)
    fields = dot(tables["field"][...], jnp.concatenate([high, low, high], axis=0))
    squares = fields * fields
    power = squares[:, :width]
    for k in range(1, kernels):
        power = power + squares[:, k * width : (k + 1) * width]
    high, low = split(power)
    lifted = dot(high, tables["lift_cols"][:width, :]) + dot(
        jnp.concatenate([low, high], axis=1), tables["lift_cols"][...]
    )
    high, low = split(lifted)
    deep = jnp.concatenate([high, low, high], axis=0)
    narrowed = []
    step = size // 2
    for begin in range(0, size, step):
        lines = slice(begin, begin + step)
        curve = jnp.tanh(dot(tables["lift_rows"][lines, :], deep) - 0.5 * SHARPNESS * THRESHOLD)
        slope = (1.0 + curve - 2.0 * target_ref[lines, :].astype(F32)) * (1.0 - curve * curve)
        both = dot(slope.astype(BF16), tables["drop_cols"][...])
        narrowed.append((both[:, :width] + both[:, width:]).astype(BF16))
    dropped = row_transform(tables["drop_rows"][...], jnp.concatenate(narrowed, axis=0))
    weighted = fields * jnp.concatenate([dropped] * kernels, axis=1)
    high, low = split(weighted)
    turned = dot(tables["turn"][...], jnp.concatenate([high, low, high], axis=0))
    across = jnp.concatenate(
        [
            jnp.concatenate([turned[:band, k * width : (k + 1) * width] for k in range(kernels)], axis=0),
            jnp.concatenate([turned[band:, k * width : (k + 1) * width] for k in range(kernels)], axis=0),
        ],
        axis=1,
    )
    both = dot(across.astype(BF16), tables["back"][...])
    product = gates * (both[:, :width] + both[:, width:])
    adjoint = product[:band]
    for k in range(1, kernels):
        adjoint = adjoint + product[k * band : (k + 1) * band]
    return adjoint + pltpu.roll(adjoint, width // 2, 1)


CORE_TABLES = ("spread", "field", "lift_cols", "lift_rows", "drop_cols", "drop_rows", "turn", "back")
OPEN_TABLES = ("quad", "rows") + CORE_TABLES


def open_kernel(total, weights_hbm, mask_hbm, dual_hbm, kernels_hbm, target_hbm, *rest):
    count = len(OPEN_TABLES)
    tables_hbm, rest = rest[:count], rest[count:]
    outs, rest = rest[:8], rest[8:]
    base_ref, gates_ref, own_ref, corner1, corner2, middle2, lines_ref, edges_ref = outs
    sources = [*tables_hbm[:2], kernels_hbm, weights_hbm, *tables_hbm[2:], target_hbm]
    mask_ref, dual_ref = rest[:2]
    staged, (line_semaphores, semaphores) = rest[2:-2], rest[-2:]
    size = mask_ref.shape[0]
    pieces = size // INTERSECTION
    edge = size - INTERSECTION

    def cut(at):
        return slice(at * INTERSECTION, (at + 1) * INTERSECTION)

    copies = [
        pltpu.make_async_copy(source, target, semaphores.at[at])
        for at, (source, target) in enumerate(zip(sources, staged))
    ]
    parts = [
        [
            pltpu.make_async_copy(source.at[cut(at), :], target.at[cut(at), :], line_semaphores.at[which, at])
            for which, (source, target) in enumerate(((mask_hbm, mask_ref), (dual_hbm, dual_ref)))
        ]
        for at in range(pieces)
    ]
    for copy in (copies[2], copies[3], copies[0]):
        copy.start()
    for pair in parts:
        for copy in pair:
            copy.start()
    for copy in [copies[1]] + copies[4:]:
        copy.start()
    quad_ref, rows_ref, kernels_ref, weights_ref, *core_refs, target_ref = staged
    band = base_ref.shape[0]
    width = 4 * band
    row, col, rows = place(total)
    even_col = col % 2 == 0

    copies[2].wait()
    copies[3].wait()
    gates = gates_of(kernels_ref, weights_ref, band)
    gates_ref[...] = gates

    copies[0].wait()
    quad = quad_ref[...]
    scaled = quad * edge_scale((size, 1), 0, size, col > 0, col < GRID_COLS - 1).astype(BF16)
    pair = jnp.concatenate([quad, scaled], axis=1)
    mask_parts, dual_parts, lefts, rights = [], [], [], []
    for at in range(pieces):
        for copy in parts[at]:
            copy.wait()
        mask, dual = mask_ref[cut(at), :], dual_ref[cut(at), :]
        mask_parts.append(dot(mask.astype(BF16), pair))
        dual_parts.append(dot(dual.astype(BF16), pair))
        ends = [0.5 * (mask[:, lanes] + dual[:, lanes]) for lanes in (slice(0, INTERSECTION), slice(edge, size))]
        lefts.append(dot(ends[0].astype(BF16), quad[edge:]))
        rights.append(dot(ends[1].astype(BF16), quad[:INTERSECTION]))

    for copy in [copies[1]] + copies[4:]:
        copy.wait()
    lines = rows_ref[...]

    def block(value, at):
        return quad_form(value[:, at * width : (at + 1) * width])

    spectrum = block(row_transform(lines, jnp.concatenate([part[:, :width] for part in mask_parts], axis=0)), 0)
    dual_spectrum = block(row_transform(lines, jnp.concatenate([part[:, :width] for part in dual_parts], axis=0)), 0)
    base_ref[...] = 0.5 * spectrum - 0.25 * dual_spectrum
    line_scale = edge_scale((1, size), 1, size, row > 0, row < rows - 1).astype(BF16)
    outer = jnp.concatenate(
        [
            jnp.concatenate([a[:, width:] + b[:, width:] for a, b in zip(mask_parts, dual_parts)], axis=0),
            jnp.concatenate(lefts, axis=0),
            jnp.concatenate(rights, axis=0),
        ],
        axis=1,
    ).astype(BF16)
    around = row_transform(lines * line_scale, outer)
    upper = 0.5 * row_transform(lines[:, edge:], outer[:INTERSECTION])
    lower = 0.5 * row_transform(lines[:, :INTERSECTION], outer[edge:])

    adjoint = adjoint_of(spectrum, gates, target_ref, dict(zip(CORE_TABLES, core_refs)))
    strips = {}
    for at in range(pieces):
        mask, dual = mask_ref[cut(at), :], dual_ref[cut(at), :]
        first, second = mask + dual, mask + 0.25 * dual
        near = jnp.concatenate([first[:, :INTERSECTION], second[:, :INTERSECTION]], axis=1)
        far = jnp.concatenate([first[:, edge:], second[:, edge:]], axis=1)
        to1, to2 = jnp.where(even_col, far, near), jnp.where(even_col, near, far)
        if at == 0 or at == pieces - 1:
            out = cut(0 if at == 0 else 1)
            corner1[out, :], corner2[out, :] = to1, to2
            strips[at] = (first, second)
        else:
            begin = 2 * INTERSECTION + band + (at - 1) * INTERSECTION
            corner1[begin : begin + INTERSECTION, :] = to1
            middle2[cut(at - 1), :] = to2
    middle2[size - 2 * INTERSECTION :, :] = jnp.zeros((middle2.shape[0] - size + 2 * INTERSECTION, middle2.shape[1]), F32)
    for part, lines_at in enumerate((cut(0), cut(1))):
        above, below = strips[0][part], strips[pieces - 1][part]
        for at, strip in enumerate((above, below)):
            edges_ref[at, lines_at, :] = jnp.concatenate([strip[:, :INTERSECTION], strip[:, edge:]], axis=1)
            lines_ref[at, lines_at, :] = strip[:, INTERSECTION:edge]

    own_ref[...] = jnp.concatenate([block(around, 0), block(upper, 0), block(lower, 0), adjoint], axis=0)
    left = [block(around, 1), block(upper, 1), block(lower, 1)]
    right = [block(around, 2), block(upper, 2), block(lower, 2)]
    tail = slice(2 * INTERSECTION, 2 * INTERSECTION + band)
    for ref, first, second in ((corner1, right, left), (corner2, left, right)):
        ref[tail, :] = pack([jnp.where(even_col, a, b) for a, b in zip(first, second)] + [adjoint])


def pack(blocks):
    lanes = lax.broadcasted_iota(jnp.int32, blocks[0].shape, 1)
    half = blocks[0].shape[1] // 2
    pairs = [jnp.where(lanes < half, a, pltpu.roll(b, half, 1)) for a, b in (blocks[:2], blocks[2:])]
    return jnp.concatenate(pairs, axis=1)


def unpack(tail):
    width = tail.shape[1] // 2
    first, second = tail[:, :width], tail[:, width:]
    return first, pltpu.roll(first, width // 2, 1), second, pltpu.roll(second, width // 2, 1)


def whole_adjoint(value):
    half = value.shape[1] // 2
    lanes = lax.broadcasted_iota(jnp.int32, value.shape, 1)
    return jnp.where(lanes < half, value, pltpu.roll(value, half, 1))


def whole_spectrum(value):
    band = value.shape[1] // 4
    lanes = lax.broadcasted_iota(jnp.int32, value.shape, 1)
    right = jnp.where(lanes < 3 * band, -pltpu.roll(value, band, 1), pltpu.roll(value, 3 * band, 1))
    return jnp.where(lanes < 2 * band, value, right)


def middle_kernel(total, own_ref, got1_ref, got2_ref, edges_ref, lines_ref, keep_ref, *sends):
    band = keep_ref.shape[0]
    row, col, rows = place(total)
    even_col = col % 2 == 0
    cut = INTERSECTION
    beside = has_beside(col)
    tail = slice(2 * cut, 2 * cut + band)
    one, two = unpack(got1_ref[tail, :]), unpack(kept(beside, got2_ref[tail, :]))
    mine = [own_ref[at * band : (at + 1) * band, :] for at in range(4)]
    keep, upper, lower = [mine[at] + one[at] + two[at] for at in range(3)]
    keep_ref[...] = keep
    summed = []
    for at in range(2):
        lines = slice(at * cut, (at + 1) * cut)
        first, second = got1_ref[lines, :], kept(beside, got2_ref[lines, :])
        left, right = jnp.where(even_col, second, first), jnp.where(even_col, first, second)
        summed.append(
            edges_ref[at]
            + jnp.concatenate(
                [
                    jnp.concatenate([left[:, :cut], right[:, :cut]], axis=1),
                    jnp.concatenate([left[:, cut:], right[:, cut:]], axis=1),
                ],
                axis=0,
            )
        )
    tails = [pack([value, mine[3], one[3], two[3]]) for value in (upper, lower)]
    tails = [jnp.concatenate([value[:, :cut], value[:, cut:]], axis=0) for value in tails]
    for at in range(SETS):
        down = row % SETS == at
        message_ref, shared_ref = sends[at], sends[SETS + at]
        ends = jnp.where(down, summed[1], summed[0])
        left, right = ends[:, :cut], ends[:, cut:]
        inner = jnp.where(down, lines_ref[1], lines_ref[0])
        message_ref[: 2 * cut, :] = jnp.where(even_col, left, right)
        for block in range(inner.shape[1] // cut):
            message_ref[2 * (block + 1) * cut : 2 * (block + 2) * cut, :] = inner[:, block * cut : (block + 1) * cut]
        message_ref[message_ref.shape[0] - 2 * band :, :] = jnp.where(down, tails[1], tails[0])
        shared_ref[...] = jnp.where(even_col, right, left)


def from_rows(row, rows, got):
    even = row % SETS == 0
    above, below = jnp.where(even, got[1], got[0]), jnp.where(even, got[0], got[1])
    return kept(row > 0, above), kept(row < rows - 1, below)


def tails_of(blocks, table):
    size = table.shape[1] // 2
    width = blocks.shape[1]
    lanes = lax.broadcasted_iota(jnp.int32, (1, width), 1)
    high, low = split(blocks)
    pair = jnp.where(lanes < width // 2, high, low)
    return dot(jnp.concatenate([pair, high], axis=1), table)


def columns_of(table, begin, end):
    size = table.shape[1] // 2
    return jnp.concatenate([table[:, begin:end], table[:, size + begin : size + end]], axis=1)


def stack_of(value, at, band):
    wide = value.shape[1] // 2
    lines = value[at * band : (at + 1) * band]
    return jnp.concatenate([lines[:, :wide], lines[:, wide:]], axis=0)


def widen(value, left, right, edge):
    return jnp.concatenate(
        [value[:, :INTERSECTION] + left, value[:, INTERSECTION:edge], value[:, edge:] + right], axis=1
    )


def deep(value):
    high, low = split(value)
    return jnp.concatenate([high, low, high], axis=0)


def prepare_kernel(total, base_ref, keep_ref, own_ref, lanes_ref, flip_ref, gates_ref, mask_ref, dual_ref, corner1_ref, corner2_ref, shared1_ref, shared2_ref, tail_ref, final_ref, early_hbm, out_ref, gates_out, mask_out, dual_out, shared_out):
    band = base_ref.shape[0]
    size = mask_ref.shape[0]
    edge = size - INTERSECTION
    adjoint = own_ref[3 * band :, :]
    width = adjoint.shape[1]
    high, low = split(adjoint)
    lanes = lax.broadcasted_iota(jnp.int32, adjoint.shape, 1)
    mirrored = dot(jnp.where(lanes < width // 2, high, low), lanes_ref[...])
    high, low = split(mirrored[:, width:])
    flip = flip_ref[...]
    gradient_band = mirrored[:, :width] + dot(flip, high) + dot(flip, low)
    out_ref[...] = base_ref[...] + 0.5 * keep_ref[...] - 0.25 * gradient_band
    gates_out[...] = gates_ref[...]
    shared_out[...] = jnp.concatenate([shared1_ref[...], shared2_ref[...]], axis=0)

    row, col, rows = place(total)
    even_col = col % 2 == 0
    scale = 2.0 / (size * size)
    tail_table = tail_ref[...]
    beside = has_beside(col)
    tail = slice(2 * INTERSECTION, 2 * INTERSECTION + band)
    first, second = [whole_adjoint(unpack(value)[3]) for value in (corner1_ref[tail, :], kept(beside, corner2_ref[tail, :]))]
    left, right = jnp.where(even_col, second, first), jnp.where(even_col, first, second)
    own_tail = stack_of(tails_of(adjoint * scale, tail_table), 0, band)
    left_tail = stack_of(tails_of(left * scale, columns_of(tail_table, edge, size)), 0, band)
    right_tail = stack_of(tails_of(right * scale, columns_of(tail_table, 0, INTERSECTION)), 0, band)
    columns = edge_scale((1, size), 1, size, col > 0, col < GRID_COLS - 1)
    summed = columns * widen(own_tail, left_tail, right_tail, edge)
    for begin in range(0, size, INTERSECTION):
        end = begin + INTERSECTION
        share = jnp.asarray(1.0, F32)
        if begin == 0:
            share = share_of(row > 0)
        if end == size:
            share = share_of(row < rows - 1)
        if begin < 2 * INTERSECTION or end == size:
            rhs = deep(
                jnp.concatenate(
                    [(-0.125 * share) * summed - 0.125 * own_tail, (0.25 * share) * summed - 0.25 * own_tail], axis=1
                )
            )
        products = dot(final_ref[begin:end, :], rhs)
        mask, dual = mask_ref[begin:end, :], dual_ref[begin:end, :]
        agreed0, agreed1 = mask + dual, mask + 0.25 * dual
        if begin == 0 or end == size:
            out = slice(0, INTERSECTION) if begin == 0 else slice(INTERSECTION, 2 * INTERSECTION)
            ends1, ends2 = corner1_ref[out, :], kept(beside, corner2_ref[out, :])
            lefts, rights = jnp.where(even_col, ends2, ends1), jnp.where(even_col, ends1, ends2)
            agreed0 = widen(agreed0, lefts[:, :INTERSECTION], rights[:, :INTERSECTION], edge)
            agreed1 = widen(agreed1, lefts[:, INTERSECTION:], rights[:, INTERSECTION:], edge)
        weight = columns * share
        agreed0, agreed1 = agreed0 * weight, agreed1 * weight
        mask_out[begin:end, :] = 0.5 * (agreed0 + agreed1) - 0.375 * dual + products[:, :size]
        dual_out[begin:end, :] = 1.5 * mask + 0.75 * dual - 0.5 * agreed0 - agreed1 + products[:, size:]


def second_kernel(total, part_ref, got1_ref, got2_ref, gates_ref, target_ref, *rest):
    tables = dict(zip(CORE_TABLES, rest))
    out_ref = rest[len(CORE_TABLES)]
    band = part_ref.shape[0]
    got = [ref[ref.shape[0] - 2 * band : ref.shape[0] - band, :] for ref in (got1_ref, got2_ref)]
    row, col, rows = place(total)
    above, below = from_rows(row, rows, got)
    spectrum = whole_spectrum(part_ref[...] + 0.5 * (above + below))
    out_ref[...] = adjoint_of(spectrum, gates_ref[...], target_ref, tables)


def last_kernel(total, mask_ref, dual_ref, corner1_ref, middle2_ref, edge1_ref, edge2_ref, shared1_ref, shared2_ref, handed_ref, adjoint_ref, tail_ref, final_ref, final_edge_ref, mask_hbm, dual_hbm, mask_out, dual_out, semaphores):
    size = mask_ref.shape[0]
    band, width = adjoint_ref.shape
    edge = size - INTERSECTION
    row, col, rows = place(total)
    even_col = col % 2 == 0
    scale = 2.0 / (size * size)
    tail_table = tail_ref[...]
    columns = edge_scale((1, size), 1, size, col > 0, col < GRID_COLS - 1)
    copies = []

    def store(begin, mask, dual):
        lines = slice(begin, begin + INTERSECTION)
        for which, (value, source, target) in enumerate(((mask, mask_out, mask_hbm), (dual, dual_out, dual_hbm))):
            source[lines, :] = value
            copy = pltpu.make_async_copy(
                source.at[lines, :], target.at[lines, :], semaphores.at[which, begin // INTERSECTION]
            )
            copy.start()
            copies.append(copy)

    new_rhs = deep(stack_of(tails_of(adjoint_ref[...] * (-0.25 * scale), tail_table), 0, band))
    left_share, right_share = share_of(col > 0), share_of(col < GRID_COLS - 1)
    for begin in range(INTERSECTION, edge, INTERSECTION):
        lines = slice(begin, begin + INTERSECTION)
        out = slice(begin - INTERSECTION, begin)
        along = begin + INTERSECTION + band
        ends1, ends2 = corner1_ref[along : along + INTERSECTION, :], kept(has_beside(col), middle2_ref[out, :])
        left = left_share * jnp.where(even_col, ends2, ends1)
        right = right_share * jnp.where(even_col, ends1, ends2)
        left0, left1, right0, right1 = [
            value[:, cut] for value in (left, right) for cut in (slice(0, INTERSECTION), slice(INTERSECTION, None))
        ]
        mask = mask_ref[lines, :] + dot(final_ref[lines, :], new_rhs)
        store(
            begin,
            widen(mask, 0.5 * (left0 + left1), 0.5 * (right0 + right1), edge),
            widen(dual_ref[lines, :], -0.5 * left0 - left1, -0.5 * right0 - right1, edge),
        )

    refs = (edge1_ref, edge2_ref)
    begin = edge1_ref.shape[0] - 2 * band
    ends = [
        jnp.concatenate([ref[begin : begin + band, :], ref[begin + band :, :]], axis=1) for ref in refs
    ]
    blocks = [unpack(value)[1:] for value in from_rows(row, rows, ends)]
    columns_at = [whole_adjoint(jnp.concatenate([a, b], axis=0)) * scale for a, b in zip(*blocks)]
    left = jnp.where(even_col, columns_at[2], columns_at[1])
    right = jnp.where(even_col, columns_at[1], columns_at[2])
    tails = tails_of(columns_at[0], tail_table)
    left_tails = tails_of(left, columns_of(tail_table, edge, size))
    right_tails = tails_of(right, columns_of(tail_table, 0, INTERSECTION))
    inner = slice(INTERSECTION, edge)
    for at, begin in enumerate((0, edge)):
        lines = slice(begin, begin + INTERSECTION)
        share = share_of(row > 0) if at == 0 else share_of(row < rows - 1)
        summed = (columns * share) * widen(
            stack_of(tails, at, band), stack_of(left_tails, at, band), stack_of(right_tails, at, band), edge
        )
        rhs = deep(jnp.concatenate([-0.125 * summed, 0.25 * summed], axis=1))
        products = dot(final_edge_ref[at * INTERSECTION : (at + 1) * INTERSECTION, :], rhs)

        def across(part):
            def cut(block):
                begin = (2 * block + part) * INTERSECTION
                return slice(begin, begin + INTERSECTION)

            def got(block):
                return from_rows(row, rows, [ref[cut(block), :] for ref in refs])[at]

            outer = (col == 0) | (col == GRID_COLS - 1)
            shared = [
                jnp.where(outer, ref[cut(0), :], handed_ref[cut(which), :])
                for which, ref in enumerate((shared1_ref, shared2_ref))
            ]
            shared, other = from_rows(row, rows, shared)[at], got(0)
            inner = [got(1 + block) for block in range((size - 2 * INTERSECTION) // INTERSECTION)]
            left, right = jnp.where(even_col, other, shared), jnp.where(even_col, shared, other)
            return jnp.concatenate([left, *inner, right], axis=1)

        weight = columns * share
        first, second = across(0) * weight, across(1) * weight
        mask = mask_ref[lines, :] + dot(final_ref[lines, :], new_rhs) + products[:, :size]
        store(begin, mask + 0.5 * (first + second), dual_ref[lines, :] + products[:, size:] - 0.5 * first - second)
    for copy in copies:
        copy.wait()


VMEM_SPEC = pl.BlockSpec(memory_space=pltpu.VMEM)
HBM_SPEC = pl.BlockSpec(memory_space=pltpu.HBM)


def call(kernel, outs, operands, flops, name, in_specs=None, out_spec=VMEM_SPEC, scratch=(), limit=VMEM_LIMIT):
    return pl.pallas_call(
        kernel,
        out_shape=[jax.ShapeDtypeStruct(shape, dtype) for shape, dtype in outs],
        in_specs=in_specs or [VMEM_SPEC] * len(operands),
        out_specs=[out_spec] * len(outs),
        scratch_shapes=list(scratch),
        compiler_params=pltpu.CompilerParams(vmem_limit_bytes=limit),
        cost_estimate=pl.CostEstimate(flops=flops, bytes_accessed=1 << 20, transcendentals=0),
        name=name,
    )(*operands)


def swaps(total):
    cols = GRID_COLS
    along, across = [[], []], [[] for _ in range(SETS)]
    for index in range(total):
        row, col = index // cols, index % cols
        if col + 1 < cols:
            along[col % 2] += [(index, index + 1), (index + 1, index)]
        if index + cols < total:
            across[row % SETS] += [(index, index + cols), (index + cols, index)]
    return along, across


def per_device(mask_init, dual_init, target, kernels, weights):
    mask, dual, goal = mask_init[0], dual_init[0], target[0]
    size = mask.shape[0]
    count = kernels.shape[0]
    band = math.isqrt(kernels.shape[2])
    width = 4 * band
    total = lax.axis_size("ty")
    (row_pairs1, row_pairs2), col_pairs = swaps(total)
    tables = {name: jnp.asarray(table) for name, table in build_tables(size, band).items()}
    core = [tables[name] for name in CORE_TABLES]

    regions = lax.axis_size("region")

    def trade(value, pairs, twinned=False):
        if not twinned:
            return lax.ppermute(value, "ty", pairs)
        busy = {first for first, second in pairs}
        twins = [(first, first ^ 1) for first in range(regions) if first ^ 1 < regions]
        whole = [(at * total + first, at * total + second) for at in range(regions) for first, second in pairs]
        whole += [(a * total + tile, b * total + tile) for tile in range(total) if tile not in busy for a, b in twins]
        return lax.ppermute(value, ("region", "ty"), whole)

    both = 2 * INTERSECTION
    inner = size - both
    block, gate = ((band, width), F32), ((count * band, width), F32)
    stack, message = ((4 * band, width), F32), ((both + band, both), F32)
    side, lines = ((inner + INTERSECTION, both), F32), ((2, both, inner), F32)
    long_message = ((2 * both + band, both), F32)
    operands = [weights, mask, dual, kernels, goal] + [tables[name] for name in OPEN_TABLES]
    operands = [pltpu.with_memory_space_constraint(value, pltpu.HBM) for value in operands]
    before, after = [mask, dual, tables["quad"], tables["rows"], kernels], core + [goal]
    base, gates, own, corner1, corner2, middle2, line_ends, edges = call(
        functools.partial(open_kernel, total),
        [block, gate, stack, long_message, message, side, lines, ((2, both, both), F32)],
        operands,
        4 * 10**9,
        "open",
        in_specs=[HBM_SPEC] * len(operands),
        scratch=[pltpu.VMEM(value.shape, value.dtype) for value in before]
        + [pltpu.SMEM(weights.shape, weights.dtype)]
        + [pltpu.VMEM(value.shape, value.dtype) for value in after]
        + [
            pltpu.SemaphoreType.DMA((2, size // INTERSECTION)),
            pltpu.SemaphoreType.DMA((len(before) + len(after) - 1,)),
        ],
    )
    corners2, corners1 = trade(corner2, row_pairs2), trade(corner1, row_pairs1)
    keep, *sends = call(
        functools.partial(middle_kernel, total),
        [block] + [((both + 2 * inner + 2 * band, INTERSECTION), F32)] * SETS + [((both, INTERSECTION), F32)] * SETS,
        [own, corners1, corners2, edges, line_ends],
        10**7,
        "middle",
    )
    gots = [trade(value, pairs, True) for value, pairs in zip(sends, col_pairs)]
    outer_pairs = [[pair for pair in pairs if pair[0] % GRID_COLS in (0, GRID_COLS - 1)] for pairs in col_pairs]
    shared = [trade(value, pairs) for value, pairs in zip(sends[SETS:], outer_pairs)]
    middles2 = trade(middle2, row_pairs2)
    whole = ((size, size), F32)
    part, gates, mask, dual, shared_out = call(
        functools.partial(prepare_kernel, total),
        [block, gate, whole, whole, ((2 * both, INTERSECTION), F32)],
        [base, keep, own, tables["mirror_lanes"], tables["mirror_rows"], gates, mask, dual, corners1, corners2, *shared]
        + [tables["tail"], tables["final"], middles2],
        10**9,
        "prepare",
        in_specs=[VMEM_SPEC] * 14 + [HBM_SPEC],
    )
    handed = trade(shared_out, row_pairs1)
    (adjoint1,) = call(
        functools.partial(second_kernel, total),
        [block],
        [part, *gots, gates, goal] + core,
        3 * 10**9,
        "second",
    )
    mask, dual = call(
        functools.partial(last_kernel, total),
        [whole, whole],
        [mask, dual, corners1, middles2, *gots, *shared, handed, adjoint1]
        + [tables["tail"], tables["final"], tables["final_edge"]],
        2 * 10**9,
        "last",
        out_spec=HBM_SPEC,
        scratch=[
            pltpu.VMEM((size, size), F32),
            pltpu.VMEM((size, size), F32),
            pltpu.SemaphoreType.DMA((2, size // INTERSECTION)),
        ],
    )
    return (mask[None], dual[None])


def solution(mesh):
    tiles = P(("region", "ty"), None, None)
    return jax.shard_map(
        per_device,
        mesh=mesh,
        in_specs=(tiles, tiles, tiles, P(), P()),
        out_specs=(tiles, tiles),
        check_vma=False,
    )
```

```python
import functools
import math

import jax
import jax.numpy as jnp
import ml_dtypes
import numpy as np
from jax import lax
from jax.experimental import pallas as pl
from jax.experimental.pallas import tpu as pltpu
from jax.sharding import PartitionSpec as P

INTERSECTION = 128
GRID_COLS = 4
SETS = 2
SHARPNESS = 8.0
THRESHOLD = 0.3
F32 = jnp.float32
BF16 = jnp.bfloat16
VMEM_LIMIT = 32 * 1024 * 1024


def halves(table):
    high = table.astype(ml_dtypes.bfloat16)
    low = (table - high.astype(np.float64)).astype(ml_dtypes.bfloat16)
    return high, low


def build_tables(size, band):
    coarse = 2 * band
    stride = size // coarse
    edge = size - INTERSECTION
    frequencies = np.arange(band) - band // 2
    angles = 2.0 * np.pi * ((frequencies[:, None] * np.arange(size)[None, :]) % size) / size
    cos, sin = np.cos(angles), -np.sin(angles)
    order = np.arange(band).reshape(-1, 128 // band).T.reshape(-1)
    rows = np.concatenate([cos[order], sin[order]], axis=0)
    quad = np.concatenate([cos.T, sin.T, -sin.T, cos.T], axis=1)
    dc, ds = cos[:, ::stride], sin[:, ::stride]
    dc_rows, ds_rows = dc[order], ds[order]
    wide = np.arange(-(band - 1), band)
    gaps = np.arange(size)[:, None] - stride * np.arange(coarse)[None, :]
    lift = np.cos(2.0 * np.pi * wide[:, None, None] * gaps[None] / size).sum(0) / coarse

    tables = {}
    tables["quad"] = halves(quad)[0]
    high, low = halves(rows)
    tables["rows"] = np.concatenate([high, low], axis=0)
    spread = np.concatenate(
        [np.concatenate([dc, -ds, -ds, -dc], axis=1), np.concatenate([ds, dc, dc, -ds], axis=1)], axis=0
    )
    high, low = halves(np.concatenate([spread, spread], axis=0))
    tables["spread"] = np.concatenate([high, high, low], axis=0)
    high, low = halves(np.concatenate([dc_rows.T, ds_rows.T], axis=1))
    tables["field"] = np.concatenate([high, high, low], axis=1)
    high, low = halves(np.concatenate([lift.T, lift.T], axis=0))
    tables["lift_cols"] = np.concatenate([high, low], axis=0)
    high, low = halves(lift * (0.5 * SHARPNESS))
    tables["lift_rows"] = np.concatenate([high, high, low], axis=1)
    high, low = halves(lift)
    tables["drop_cols"] = np.concatenate([high, high, low, low], axis=1)
    high, low = halves(lift.T * (0.25 * SHARPNESS))
    tables["drop_rows"] = np.concatenate([high, low], axis=0)
    high, low = halves(np.concatenate([dc_rows, ds_rows], axis=0))
    tables["turn"] = np.concatenate([high, high, low], axis=1)
    back_real = np.concatenate([dc.T, -ds.T, -ds.T, -dc.T], axis=0)
    back_imag = np.concatenate([ds.T, dc.T, dc.T, -ds.T], axis=0)
    high, low = halves(np.concatenate([back_real, back_imag, back_imag, -back_real], axis=1))
    tables["back"] = np.concatenate([high, low], axis=1)
    flip = np.zeros((band, band))
    for place in range(1, band):
        flip[place, band - place] = 1.0
    eye, zero = np.eye(band), np.zeros((band, band))
    own = np.concatenate(
        [
            np.concatenate([eye, zero, zero, eye], axis=1),
            np.concatenate([zero, eye, -eye, zero], axis=1),
        ],
        axis=0,
    )
    turned = np.concatenate(
        [
            np.concatenate([flip, zero, zero, flip], axis=1),
            np.concatenate([zero, -flip, flip, zero], axis=1),
        ],
        axis=0,
    )
    tables["mirror_lanes"] = np.concatenate(
        [np.concatenate([own, own], axis=0), np.concatenate([turned, turned], axis=0)], axis=1
    ).astype(ml_dtypes.bfloat16)
    tables["mirror_rows"] = flip[order][:, order].astype(ml_dtypes.bfloat16)
    tail = np.concatenate([np.concatenate([cos, -sin], axis=1), np.concatenate([sin, cos], axis=1)], axis=0)
    high, low = halves(tail)
    tables["tail"] = np.concatenate([high, high, low, np.zeros_like(low)], axis=0)
    high, low = halves(rows.T)
    tables["final"] = np.concatenate([high, high, low], axis=1)
    near, far = rows[:, :INTERSECTION], rows[:, edge:]
    high, low = halves(np.concatenate([far.T, near.T], axis=0))
    tables["final_edge"] = np.concatenate([high, high, low], axis=1)
    return tables


def dot(left, right):
    return lax.dot_general(left, right, (((1,), (0,)), ((), ())), preferred_element_type=F32)


def split(value):
    high = value.astype(BF16)
    return high, (value - high.astype(F32)).astype(BF16)


def place(total):
    index = lax.axis_index("ty")
    row, col = index // GRID_COLS, index % GRID_COLS
    return row, col, total // GRID_COLS


def has_beside(col):
    return jnp.where(col % 2 == 0, col > 0, col < GRID_COLS - 1)


def kept(present, value):
    return jnp.where(present, value, jnp.zeros_like(value))


def share_of(present):
    return jnp.where(present, 0.5, 1.0).astype(F32)


def edge_scale(shape, dim, size, before, after):
    steps = lax.broadcasted_iota(jnp.int32, shape, dim)
    first = jnp.where(steps < INTERSECTION, share_of(before), 1.0)
    return first * jnp.where(steps >= size - INTERSECTION, share_of(after), 1.0)


def quad_form(value):
    half = value.shape[0] // 2
    width = value.shape[1]
    lanes = lax.broadcasted_iota(jnp.int32, (half, width), 1)
    rolled = pltpu.roll(value[half:], width // 2, 1)
    return value[:half] + jnp.where(lanes < width // 2, rolled, -rolled)


def row_transform(table, value):
    half = table.shape[0] // 2
    both = dot(table, value.astype(BF16))
    return both[:half] + both[half:]


def gates_of(kernels_ref, weights_ref, band):
    count, parts, length = kernels_ref.shape
    lanes = 128
    groups = lanes // band
    chunks = length // lanes
    total = weights_ref[0]
    for k in range(1, count):
        total = total + weights_ref[k]
    group = lax.broadcasted_iota(jnp.int32, (chunks, lanes), 1) // band
    blocks = []
    for k in range(count):
        gain = jnp.sqrt(jnp.full((chunks, lanes), weights_ref[k], F32) / total)
        real, imag = [
            gain
            * jnp.concatenate(
                [kernels_ref[k, part : part + 1, c * lanes : (c + 1) * lanes] for c in range(chunks)], axis=0
            )
            for part in range(2)
        ]
        reals = [pltpu.roll(real, band * g, 1) if g else real for g in range(groups)]
        imags = [pltpu.roll(imag, band * g, 1) if g else imag for g in range(groups)]
        for at in range(groups):
            line = imags[(3 - at) % groups]
            line = jnp.where(group == 2, imags[(2 - at) % groups], line)
            line = jnp.where(group == 1, reals[(1 - at) % groups], line)
            blocks.append(jnp.where(group == 0, reals[-at % groups], line))
    return jnp.concatenate(blocks, axis=0)


def adjoint_of(spectrum, gates, target_ref, tables, rest_here=lambda: None):
    band = spectrum.shape[0]
    width = 4 * band
    kernels = gates.shape[0] // band
    size = target_ref.shape[0]
    scaled = spectrum * (1.0 / (size * size))
    high, low = split(gates * jnp.concatenate([scaled] * kernels, axis=0))
    bands = dot(jnp.concatenate([high, low, high], axis=1), tables["spread"][...])
    stacked = jnp.concatenate(
        [
            jnp.concatenate([bands[band * k : band * (k + 1), :width] for k in range(kernels)], axis=1),
            jnp.concatenate([bands[band * k : band * (k + 1), width:] for k in range(kernels)], axis=1),
        ],
        axis=0,
    )
    high, low = split(stacked)
    fields = dot(tables["field"][...], jnp.concatenate([high, low, high], axis=0))
    squares = fields * fields
    power = squares[:, :width]
    for k in range(1, kernels):
        power = power + squares[:, k * width : (k + 1) * width]
    high, low = split(power)
    lifted = dot(high, tables["lift_cols"][:width, :]) + dot(
        jnp.concatenate([low, high], axis=1), tables["lift_cols"][...]
    )
    high, low = split(lifted)
    deep = jnp.concatenate([high, low, high], axis=0)
    rest_here()
    narrowed = []
    step = size // 2
    for begin in range(0, size, step):
        lines = slice(begin, begin + step)
        curve = jnp.tanh(dot(tables["lift_rows"][lines, :], deep) - 0.5 * SHARPNESS * THRESHOLD)
        slope = (1.0 + curve - 2.0 * target_ref[lines, :].astype(F32)) * (1.0 - curve * curve)
        both = dot(slope.astype(BF16), tables["drop_cols"][...])
        narrowed.append((both[:, :width] + both[:, width:]).astype(BF16))
    dropped = row_transform(tables["drop_rows"][...], jnp.concatenate(narrowed, axis=0))
    weighted = fields * jnp.concatenate([dropped] * kernels, axis=1)
    high, low = split(weighted)
    turned = dot(tables["turn"][...], jnp.concatenate([high, low, high], axis=0))
    across = jnp.concatenate(
        [
            jnp.concatenate([turned[:band, k * width : (k + 1) * width] for k in range(kernels)], axis=0),
            jnp.concatenate([turned[band:, k * width : (k + 1) * width] for k in range(kernels)], axis=0),
        ],
        axis=1,
    )
    both = dot(across.astype(BF16), tables["back"][...])
    product = gates * (both[:, :width] + both[:, width:])
    adjoint = product[:band]
    for k in range(1, kernels):
        adjoint = adjoint + product[k * band : (k + 1) * band]
    return adjoint + pltpu.roll(adjoint, width // 2, 1)


CORE_TABLES = ("spread", "field", "lift_cols", "lift_rows", "drop_cols", "drop_rows", "turn", "back")
OPEN_TABLES = ("quad", "rows") + CORE_TABLES


def open_kernel(total, weights_hbm, mask_hbm, dual_hbm, kernels_hbm, target_hbm, *rest):
    count = len(OPEN_TABLES)
    tables_hbm, rest = rest[:count], rest[count:]
    outs, rest = rest[:8], rest[8:]
    base_ref, gates_ref, own_ref, corner1, corner2, middle2, lines_ref, edges_ref = outs
    sources = [*tables_hbm[:2], kernels_hbm, weights_hbm, *tables_hbm[2:], target_hbm]
    mask_ref, dual_ref = rest[:2]
    staged, (line_semaphores, semaphores) = rest[2:-2], rest[-2:]
    size = mask_ref.shape[0]
    pieces = size // INTERSECTION
    edge = size - INTERSECTION

    def cut(at):
        return slice(at * INTERSECTION, (at + 1) * INTERSECTION)

    copies = [
        pltpu.make_async_copy(source, target, semaphores.at[at])
        for at, (source, target) in enumerate(zip(sources, staged))
    ]
    parts = [
        [
            pltpu.make_async_copy(source.at[cut(at), :], target.at[cut(at), :], line_semaphores.at[which, at])
            for which, (source, target) in enumerate(((mask_hbm, mask_ref), (dual_hbm, dual_ref)))
        ]
        for at in range(pieces)
    ]
    for copy in (copies[2], copies[3], copies[0]):
        copy.start()
    for pair in parts:
        for copy in pair:
            copy.start()
    for copy in [copies[1]] + copies[4:]:
        copy.start()
    quad_ref, rows_ref, kernels_ref, weights_ref, *core_refs, target_ref = staged
    band = base_ref.shape[0]
    width = 4 * band
    row, col, rows = place(total)
    even_col = col % 2 == 0

    copies[2].wait()
    copies[3].wait()
    gates = gates_of(kernels_ref, weights_ref, band)
    gates_ref[...] = gates

    copies[0].wait()
    quad = quad_ref[...]
    scaled = quad * edge_scale((size, 1), 0, size, col > 0, col < GRID_COLS - 1).astype(BF16)
    pair = jnp.concatenate([quad, scaled], axis=1)
    mask_parts, dual_parts, lefts, rights = [], [], [], []
    for at in range(pieces):
        for copy in parts[at]:
            copy.wait()
        mask, dual = mask_ref[cut(at), :], dual_ref[cut(at), :]
        mask_parts.append(dot(mask.astype(BF16), pair))
        dual_parts.append(dot(dual.astype(BF16), pair))
        ends = [0.5 * (mask[:, lanes] + dual[:, lanes]) for lanes in (slice(0, INTERSECTION), slice(edge, size))]
        lefts.append(dot(ends[0].astype(BF16), quad[edge:]))
        rights.append(dot(ends[1].astype(BF16), quad[:INTERSECTION]))

    early = ("spread", "field", "lift_cols", "lift_rows")
    order = list(zip(CORE_TABLES + ("target",), copies[4:]))
    for copy in [copies[1]] + [copy for name, copy in order if name in early]:
        copy.wait()

    def rest_here():
        for name, copy in order:
            if name not in early:
                copy.wait()

    lines = rows_ref[...]

    def block(value, at):
        return quad_form(value[:, at * width : (at + 1) * width])

    spectrum = block(row_transform(lines, jnp.concatenate([part[:, :width] for part in mask_parts], axis=0)), 0)
    dual_spectrum = block(row_transform(lines, jnp.concatenate([part[:, :width] for part in dual_parts], axis=0)), 0)
    base_ref[...] = 0.5 * spectrum - 0.25 * dual_spectrum
    line_scale = edge_scale((1, size), 1, size, row > 0, row < rows - 1).astype(BF16)
    outer = jnp.concatenate(
        [
            jnp.concatenate([a[:, width:] + b[:, width:] for a, b in zip(mask_parts, dual_parts)], axis=0),
            jnp.concatenate(lefts, axis=0),
            jnp.concatenate(rights, axis=0),
        ],
        axis=1,
    ).astype(BF16)
    around = row_transform(lines * line_scale, outer)
    upper = 0.5 * row_transform(lines[:, edge:], outer[:INTERSECTION])
    lower = 0.5 * row_transform(lines[:, :INTERSECTION], outer[edge:])

    adjoint = adjoint_of(spectrum, gates, target_ref, dict(zip(CORE_TABLES, core_refs)), rest_here)
    strips = {}
    for at in range(pieces):
        mask, dual = mask_ref[cut(at), :], dual_ref[cut(at), :]
        first, second = mask + dual, mask + 0.25 * dual
        near = jnp.concatenate([first[:, :INTERSECTION], second[:, :INTERSECTION]], axis=1)
        far = jnp.concatenate([first[:, edge:], second[:, edge:]], axis=1)
        to1, to2 = jnp.where(even_col, far, near), jnp.where(even_col, near, far)
        if at == 0 or at == pieces - 1:
            out = cut(0 if at == 0 else 1)
            corner1[out, :], corner2[out, :] = to1, to2
            strips[at] = (first, second)
        else:
            begin = 2 * INTERSECTION + band + (at - 1) * INTERSECTION
            corner1[begin : begin + INTERSECTION, :] = to1
            middle2[cut(at - 1), :] = to2
    middle2[size - 2 * INTERSECTION :, :] = jnp.zeros((middle2.shape[0] - size + 2 * INTERSECTION, middle2.shape[1]), F32)
    for part, lines_at in enumerate((cut(0), cut(1))):
        above, below = strips[0][part], strips[pieces - 1][part]
        for at, strip in enumerate((above, below)):
            edges_ref[at, lines_at, :] = jnp.concatenate([strip[:, :INTERSECTION], strip[:, edge:]], axis=1)
            lines_ref[at, lines_at, :] = strip[:, INTERSECTION:edge]

    own_ref[...] = jnp.concatenate([block(around, 0), block(upper, 0), block(lower, 0), adjoint], axis=0)
    left = [block(around, 1), block(upper, 1), block(lower, 1)]
    right = [block(around, 2), block(upper, 2), block(lower, 2)]
    tail = slice(2 * INTERSECTION, 2 * INTERSECTION + band)
    for ref, first, second in ((corner1, right, left), (corner2, left, right)):
        ref[tail, :] = pack([jnp.where(even_col, a, b) for a, b in zip(first, second)] + [adjoint])


def pack(blocks):
    lanes = lax.broadcasted_iota(jnp.int32, blocks[0].shape, 1)
    half = blocks[0].shape[1] // 2
    pairs = [jnp.where(lanes < half, a, pltpu.roll(b, half, 1)) for a, b in (blocks[:2], blocks[2:])]
    return jnp.concatenate(pairs, axis=1)


def unpack(tail):
    width = tail.shape[1] // 2
    first, second = tail[:, :width], tail[:, width:]
    return first, pltpu.roll(first, width // 2, 1), second, pltpu.roll(second, width // 2, 1)


def whole_adjoint(value):
    half = value.shape[1] // 2
    lanes = lax.broadcasted_iota(jnp.int32, value.shape, 1)
    return jnp.where(lanes < half, value, pltpu.roll(value, half, 1))


def whole_spectrum(value):
    band = value.shape[1] // 4
    lanes = lax.broadcasted_iota(jnp.int32, value.shape, 1)
    right = jnp.where(lanes < 3 * band, -pltpu.roll(value, band, 1), pltpu.roll(value, 3 * band, 1))
    return jnp.where(lanes < 2 * band, value, right)


def middle_kernel(total, own_ref, got1_ref, got2_ref, edges_ref, lines_ref, keep_ref, *sends):
    band = keep_ref.shape[0]
    row, col, rows = place(total)
    even_col = col % 2 == 0
    cut = INTERSECTION
    beside = has_beside(col)
    tail = slice(2 * cut, 2 * cut + band)
    one, two = unpack(got1_ref[tail, :]), unpack(kept(beside, got2_ref[tail, :]))
    mine = [own_ref[at * band : (at + 1) * band, :] for at in range(4)]
    keep, upper, lower = [mine[at] + one[at] + two[at] for at in range(3)]
    keep_ref[...] = keep
    summed = []
    for at in range(2):
        lines = slice(at * cut, (at + 1) * cut)
        first, second = got1_ref[lines, :], kept(beside, got2_ref[lines, :])
        left, right = jnp.where(even_col, second, first), jnp.where(even_col, first, second)
        summed.append(
            edges_ref[at]
            + jnp.concatenate(
                [
                    jnp.concatenate([left[:, :cut], right[:, :cut]], axis=1),
                    jnp.concatenate([left[:, cut:], right[:, cut:]], axis=1),
                ],
                axis=0,
            )
        )
    tails = [pack([value, mine[3], one[3], two[3]]) for value in (upper, lower)]
    tails = [jnp.concatenate([value[:, :cut], value[:, cut:]], axis=0) for value in tails]
    for at in range(SETS):
        down = row % SETS == at
        message_ref, shared_ref = sends[at], sends[SETS + at]
        ends = jnp.where(down, summed[1], summed[0])
        left, right = ends[:, :cut], ends[:, cut:]
        inner = jnp.where(down, lines_ref[1], lines_ref[0])
        message_ref[: 2 * cut, :] = jnp.where(even_col, left, right)
        for block in range(inner.shape[1] // cut):
            message_ref[2 * (block + 1) * cut : 2 * (block + 2) * cut, :] = inner[:, block * cut : (block + 1) * cut]
        message_ref[message_ref.shape[0] - 2 * band :, :] = jnp.where(down, tails[1], tails[0])
        shared_ref[...] = jnp.where(even_col, right, left)


def from_rows(row, rows, got):
    even = row % SETS == 0
    above, below = jnp.where(even, got[1], got[0]), jnp.where(even, got[0], got[1])
    return kept(row > 0, above), kept(row < rows - 1, below)


def tails_of(blocks, table):
    size = table.shape[1] // 2
    width = blocks.shape[1]
    lanes = lax.broadcasted_iota(jnp.int32, (1, width), 1)
    high, low = split(blocks)
    pair = jnp.where(lanes < width // 2, high, low)
    return dot(jnp.concatenate([pair, high], axis=1), table)


def columns_of(table, begin, end):
    size = table.shape[1] // 2
    return jnp.concatenate([table[:, begin:end], table[:, size + begin : size + end]], axis=1)


def stack_of(value, at, band):
    wide = value.shape[1] // 2
    lines = value[at * band : (at + 1) * band]
    return jnp.concatenate([lines[:, :wide], lines[:, wide:]], axis=0)


def widen(value, left, right, edge):
    return jnp.concatenate(
        [value[:, :INTERSECTION] + left, value[:, INTERSECTION:edge], value[:, edge:] + right], axis=1
    )


def deep(value):
    high, low = split(value)
    return jnp.concatenate([high, low, high], axis=0)


def prepare_kernel(total, base_ref, keep_ref, own_ref, lanes_ref, flip_ref, gates_ref, mask_ref, dual_ref, corner1_ref, corner2_ref, shared1_ref, shared2_ref, tail_ref, final_ref, early_hbm, out_ref, gates_out, mask_out, dual_out, shared_out):
    band = base_ref.shape[0]
    size = mask_ref.shape[0]
    edge = size - INTERSECTION
    adjoint = own_ref[3 * band :, :]
    width = adjoint.shape[1]
    high, low = split(adjoint)
    lanes = lax.broadcasted_iota(jnp.int32, adjoint.shape, 1)
    mirrored = dot(jnp.where(lanes < width // 2, high, low), lanes_ref[...])
    high, low = split(mirrored[:, width:])
    flip = flip_ref[...]
    gradient_band = mirrored[:, :width] + dot(flip, high) + dot(flip, low)
    out_ref[...] = base_ref[...] + 0.5 * keep_ref[...] - 0.25 * gradient_band
    gates_out[...] = gates_ref[...]
    shared_out[...] = jnp.concatenate([shared1_ref[...], shared2_ref[...]], axis=0)

    row, col, rows = place(total)
    even_col = col % 2 == 0
    scale = 2.0 / (size * size)
    tail_table = tail_ref[...]
    beside = has_beside(col)
    tail = slice(2 * INTERSECTION, 2 * INTERSECTION + band)
    first, second = [whole_adjoint(unpack(value)[3]) for value in (corner1_ref[tail, :], kept(beside, corner2_ref[tail, :]))]
    left, right = jnp.where(even_col, second, first), jnp.where(even_col, first, second)
    own_tail = stack_of(tails_of(adjoint * scale, tail_table), 0, band)
    left_tail = stack_of(tails_of(left * scale, columns_of(tail_table, edge, size)), 0, band)
    right_tail = stack_of(tails_of(right * scale, columns_of(tail_table, 0, INTERSECTION)), 0, band)
    columns = edge_scale((1, size), 1, size, col > 0, col < GRID_COLS - 1)
    summed = columns * widen(own_tail, left_tail, right_tail, edge)
    for begin in range(0, size, INTERSECTION):
        end = begin + INTERSECTION
        share = jnp.asarray(1.0, F32)
        if begin == 0:
            share = share_of(row > 0)
        if end == size:
            share = share_of(row < rows - 1)
        if begin < 2 * INTERSECTION or end == size:
            rhs = deep(
                jnp.concatenate(
                    [(-0.125 * share) * summed - 0.125 * own_tail, (0.25 * share) * summed - 0.25 * own_tail], axis=1
                )
            )
        products = dot(final_ref[begin:end, :], rhs)
        mask, dual = mask_ref[begin:end, :], dual_ref[begin:end, :]
        agreed0, agreed1 = mask + dual, mask + 0.25 * dual
        if begin == 0 or end == size:
            out = slice(0, INTERSECTION) if begin == 0 else slice(INTERSECTION, 2 * INTERSECTION)
            ends1, ends2 = corner1_ref[out, :], kept(beside, corner2_ref[out, :])
            lefts, rights = jnp.where(even_col, ends2, ends1), jnp.where(even_col, ends1, ends2)
            agreed0 = widen(agreed0, lefts[:, :INTERSECTION], rights[:, :INTERSECTION], edge)
            agreed1 = widen(agreed1, lefts[:, INTERSECTION:], rights[:, INTERSECTION:], edge)
        weight = columns * share
        agreed0, agreed1 = agreed0 * weight, agreed1 * weight
        mask_out[begin:end, :] = 0.5 * (agreed0 + agreed1) - 0.375 * dual + products[:, :size]
        dual_out[begin:end, :] = 1.5 * mask + 0.75 * dual - 0.5 * agreed0 - agreed1 + products[:, size:]


def second_kernel(total, part_ref, got1_ref, got2_ref, gates_ref, target_ref, *rest):
    tables = dict(zip(CORE_TABLES, rest))
    out_ref = rest[len(CORE_TABLES)]
    band = part_ref.shape[0]
    got = [ref[ref.shape[0] - 2 * band : ref.shape[0] - band, :] for ref in (got1_ref, got2_ref)]
    row, col, rows = place(total)
    above, below = from_rows(row, rows, got)
    spectrum = whole_spectrum(part_ref[...] + 0.5 * (above + below))
    out_ref[...] = adjoint_of(spectrum, gates_ref[...], target_ref, tables)


def last_kernel(total, mask_ref, dual_ref, corner1_ref, middle2_ref, edge1_ref, edge2_ref, shared1_ref, shared2_ref, handed_ref, adjoint_ref, tail_ref, final_ref, final_edge_ref, mask_hbm, dual_hbm, mask_out, dual_out, semaphores):
    size = mask_ref.shape[0]
    band, width = adjoint_ref.shape
    edge = size - INTERSECTION
    row, col, rows = place(total)
    even_col = col % 2 == 0
    scale = 2.0 / (size * size)
    tail_table = tail_ref[...]
    columns = edge_scale((1, size), 1, size, col > 0, col < GRID_COLS - 1)
    copies = []

    def store(begin, mask, dual):
        lines = slice(begin, begin + INTERSECTION)
        for which, (value, source, target) in enumerate(((mask, mask_out, mask_hbm), (dual, dual_out, dual_hbm))):
            source[lines, :] = value
            copy = pltpu.make_async_copy(
                source.at[lines, :], target.at[lines, :], semaphores.at[which, begin // INTERSECTION]
            )
            copy.start()
            copies.append(copy)

    new_rhs = deep(stack_of(tails_of(adjoint_ref[...] * (-0.25 * scale), tail_table), 0, band))
    left_share, right_share = share_of(col > 0), share_of(col < GRID_COLS - 1)
    for begin in range(INTERSECTION, edge, INTERSECTION):
        lines = slice(begin, begin + INTERSECTION)
        out = slice(begin - INTERSECTION, begin)
        along = begin + INTERSECTION + band
        ends1, ends2 = corner1_ref[along : along + INTERSECTION, :], kept(has_beside(col), middle2_ref[out, :])
        left = left_share * jnp.where(even_col, ends2, ends1)
        right = right_share * jnp.where(even_col, ends1, ends2)
        left0, left1, right0, right1 = [
            value[:, cut] for value in (left, right) for cut in (slice(0, INTERSECTION), slice(INTERSECTION, None))
        ]
        mask = mask_ref[lines, :] + dot(final_ref[lines, :], new_rhs)
        store(
            begin,
            widen(mask, 0.5 * (left0 + left1), 0.5 * (right0 + right1), edge),
            widen(dual_ref[lines, :], -0.5 * left0 - left1, -0.5 * right0 - right1, edge),
        )

    refs = (edge1_ref, edge2_ref)
    begin = edge1_ref.shape[0] - 2 * band
    ends = [
        jnp.concatenate([ref[begin : begin + band, :], ref[begin + band :, :]], axis=1) for ref in refs
    ]
    blocks = [unpack(value)[1:] for value in from_rows(row, rows, ends)]
    columns_at = [whole_adjoint(jnp.concatenate([a, b], axis=0)) * scale for a, b in zip(*blocks)]
    left = jnp.where(even_col, columns_at[2], columns_at[1])
    right = jnp.where(even_col, columns_at[1], columns_at[2])
    tails = tails_of(columns_at[0], tail_table)
    left_tails = tails_of(left, columns_of(tail_table, edge, size))
    right_tails = tails_of(right, columns_of(tail_table, 0, INTERSECTION))
    inner = slice(INTERSECTION, edge)
    for at, begin in enumerate((0, edge)):
        lines = slice(begin, begin + INTERSECTION)
        share = share_of(row > 0) if at == 0 else share_of(row < rows - 1)
        summed = (columns * share) * widen(
            stack_of(tails, at, band), stack_of(left_tails, at, band), stack_of(right_tails, at, band), edge
        )
        rhs = deep(jnp.concatenate([-0.125 * summed, 0.25 * summed], axis=1))
        products = dot(final_edge_ref[at * INTERSECTION : (at + 1) * INTERSECTION, :], rhs)

        def across(part):
            def cut(block):
                begin = (2 * block + part) * INTERSECTION
                return slice(begin, begin + INTERSECTION)

            def got(block):
                return from_rows(row, rows, [ref[cut(block), :] for ref in refs])[at]

            outer = (col == 0) | (col == GRID_COLS - 1)
            shared = [
                jnp.where(outer, ref[cut(0), :], handed_ref[cut(which), :])
                for which, ref in enumerate((shared1_ref, shared2_ref))
            ]
            shared, other = from_rows(row, rows, shared)[at], got(0)
            inner = [got(1 + block) for block in range((size - 2 * INTERSECTION) // INTERSECTION)]
            left, right = jnp.where(even_col, other, shared), jnp.where(even_col, shared, other)
            return jnp.concatenate([left, *inner, right], axis=1)

        weight = columns * share
        first, second = across(0) * weight, across(1) * weight
        mask = mask_ref[lines, :] + dot(final_ref[lines, :], new_rhs) + products[:, :size]
        store(begin, mask + 0.5 * (first + second), dual_ref[lines, :] + products[:, size:] - 0.5 * first - second)
    for copy in copies:
        copy.wait()


VMEM_SPEC = pl.BlockSpec(memory_space=pltpu.VMEM)
HBM_SPEC = pl.BlockSpec(memory_space=pltpu.HBM)


def call(kernel, outs, operands, flops, name, in_specs=None, out_spec=VMEM_SPEC, scratch=(), limit=VMEM_LIMIT):
    return pl.pallas_call(
        kernel,
        out_shape=[jax.ShapeDtypeStruct(shape, dtype) for shape, dtype in outs],
        in_specs=in_specs or [VMEM_SPEC] * len(operands),
        out_specs=[out_spec] * len(outs),
        scratch_shapes=list(scratch),
        compiler_params=pltpu.CompilerParams(vmem_limit_bytes=limit),
        cost_estimate=pl.CostEstimate(flops=flops, bytes_accessed=1 << 20, transcendentals=0),
        name=name,
    )(*operands)


def swaps(total):
    cols = GRID_COLS
    along, across = [[], []], [[] for _ in range(SETS)]
    for index in range(total):
        row, col = index // cols, index % cols
        if col + 1 < cols:
            along[col % 2] += [(index, index + 1), (index + 1, index)]
        if index + cols < total:
            across[row % SETS] += [(index, index + cols), (index + cols, index)]
    return along, across


def per_device(mask_init, dual_init, target, kernels, weights):
    mask, dual, goal = mask_init[0], dual_init[0], target[0]
    size = mask.shape[0]
    count = kernels.shape[0]
    band = math.isqrt(kernels.shape[2])
    width = 4 * band
    total = lax.axis_size("ty")
    (row_pairs1, row_pairs2), col_pairs = swaps(total)
    tables = {name: jnp.asarray(table) for name, table in build_tables(size, band).items()}
    core = [tables[name] for name in CORE_TABLES]

    regions = lax.axis_size("region")

    def trade(value, pairs, twinned=False):
        if not twinned:
            return lax.ppermute(value, "ty", pairs)
        busy = {first for first, second in pairs}
        twins = [(first, first ^ 1) for first in range(regions) if first ^ 1 < regions]
        whole = [(at * total + first, at * total + second) for at in range(regions) for first, second in pairs]
        whole += [(a * total + tile, b * total + tile) for tile in range(total) if tile not in busy for a, b in twins]
        return lax.ppermute(value, ("region", "ty"), whole)

    both = 2 * INTERSECTION
    inner = size - both
    block, gate = ((band, width), F32), ((count * band, width), F32)
    stack, message = ((4 * band, width), F32), ((both + band, both), F32)
    side, lines = ((inner + INTERSECTION, both), F32), ((2, both, inner), F32)
    long_message = ((2 * both + band, both), F32)
    operands = [weights, mask, dual, kernels, goal] + [tables[name] for name in OPEN_TABLES]
    operands = [pltpu.with_memory_space_constraint(value, pltpu.HBM) for value in operands]
    before, after = [mask, dual, tables["quad"], tables["rows"], kernels], core + [goal]
    base, gates, own, corner1, corner2, middle2, line_ends, edges = call(
        functools.partial(open_kernel, total),
        [block, gate, stack, long_message, message, side, lines, ((2, both, both), F32)],
        operands,
        4 * 10**9,
        "open",
        in_specs=[HBM_SPEC] * len(operands),
        scratch=[pltpu.VMEM(value.shape, value.dtype) for value in before]
        + [pltpu.SMEM(weights.shape, weights.dtype)]
        + [pltpu.VMEM(value.shape, value.dtype) for value in after]
        + [
            pltpu.SemaphoreType.DMA((2, size // INTERSECTION)),
            pltpu.SemaphoreType.DMA((len(before) + len(after) - 1,)),
        ],
    )
    corners2, corners1 = trade(corner2, row_pairs2), trade(corner1, row_pairs1)
    keep, *sends = call(
        functools.partial(middle_kernel, total),
        [block] + [((both + 2 * inner + 2 * band, INTERSECTION), F32)] * SETS + [((both, INTERSECTION), F32)] * SETS,
        [own, corners1, corners2, edges, line_ends],
        10**7,
        "middle",
    )
    gots = [trade(value, pairs, True) for value, pairs in zip(sends, col_pairs)]
    outer_pairs = [[pair for pair in pairs if pair[0] % GRID_COLS in (0, GRID_COLS - 1)] for pairs in col_pairs]
    shared = [trade(value, pairs) for value, pairs in zip(sends[SETS:], outer_pairs)]
    middles2 = trade(middle2, row_pairs2)
    whole = ((size, size), F32)
    part, gates, mask, dual, shared_out = call(
        functools.partial(prepare_kernel, total),
        [block, gate, whole, whole, ((2 * both, INTERSECTION), F32)],
        [base, keep, own, tables["mirror_lanes"], tables["mirror_rows"], gates, mask, dual, corners1, corners2, *shared]
        + [tables["tail"], tables["final"], middles2],
        10**9,
        "prepare",
        in_specs=[VMEM_SPEC] * 14 + [HBM_SPEC],
    )
    handed = trade(shared_out, row_pairs1)
    (adjoint1,) = call(
        functools.partial(second_kernel, total),
        [block],
        [part, *gots, gates, goal] + core,
        3 * 10**9,
        "second",
    )
    mask, dual = call(
        functools.partial(last_kernel, total),
        [whole, whole],
        [mask, dual, corners1, middles2, *gots, *shared, handed, adjoint1]
        + [tables["tail"], tables["final"], tables["final_edge"]],
        2 * 10**9,
        "last",
        out_spec=HBM_SPEC,
        scratch=[
            pltpu.VMEM((size, size), F32),
            pltpu.VMEM((size, size), F32),
            pltpu.SemaphoreType.DMA((2, size // INTERSECTION)),
        ],
    )
    return (mask[None], dual[None])


def solution(mesh):
    tiles = P(("region", "ty"), None, None)
    return jax.shard_map(
        per_device,
        mesh=mesh,
        in_specs=(tiles, tiles, tiles, P(), P()),
        out_specs=(tiles, tiles),
        check_vma=False,
    )
```
